32 devices in a mesh: geom: 4 (over x, core), dom: 8 (over z, y).
Axes of the slice: x: 2, y: 2, z: 4, core: 2. Of those that a mesh axis runs over, the one named last changes fastest.
Arguments:
- h_in: bfloat16 [4, 4096, 512], P('geom', 'dom'), may hold values from -6 to 6
- edge_in: bfloat16 [4, 16384, 512], P('geom', 'dom'), may hold values from -6 to 6
- new_index: int32 [4, 4096], P('geom', 'dom'), may hold values from 0 to 4095, as said below
- source: int32 [4, 16384], P('geom', 'dom'), may hold values from 0 to 4095, as said below
- w_edge_in: bfloat16 [1536, 512], replicated, may hold values from -0.15625 to 0.15625
- w_edge_out: bfloat16 [512, 512], replicated, may hold values from -0.25 to 0.25
- w_node_in: bfloat16 [1024, 512], replicated, may hold values from -0.1875 to 0.1875
- w_node_out: bfloat16 [512, 512], replicated, may hold values from -0.25 to 0.25
- cot_nodes: bfloat16 [4, 4096, 512], P('geom', 'dom'), may hold values from -6 to 6
- cot_edges: bfloat16 [4, 16384, 512], P('geom', 'dom'), may hold values from -6 to 6
Outputs:
- node_new: bfloat16 [4, 4096, 512], P('geom', 'dom')
- edge_new: bfloat16 [4, 16384, 512], P('geom', 'dom')
- grad_in: bfloat16 [4, 4096, 512], P('geom', 'dom')
- grad_edge: bfloat16 [4, 16384, 512], P('geom', 'dom')
- weight_grads: float32 [3584, 512], P('dom')
The draws below stay inside these ranges and needn't reach their ends.
Inputs may be any that keep to these rules, and one draw needn't show every extreme that they name: `new_index`: per geometry a permutation of the 4096 cells. The cells in rows k * 512 to (k + 1) * 512 - 1 of the old layout reach the rows of any one device of the new layout at most 96 times, exactly 96 times for some pairs. `source`: an edge of a cell in rows k * 512 to (k + 1) * 512 - 1 comes from a cell of the same range, of the last 64 cells of the range before, or of the first 64 cells of the range after.
All inputs are finite; a program needn't handle non-finite values.
Results may differ from the reference program's by a relative error of at most 0.019.
Values may be sent and summed in bfloat16 or wider, within the bound.
No kernel may reach another device: no remote copies, remote signals or barrier semaphores. Data moves between devices by JAX's collectives and lax.ppermute only.
A program may use at most 128 MiB of HBM per device.

```python
import math
import jax
import jax.numpy as jnp
import numpy as np
from jax import lax

D = 512
K = 4
C = 512
HB = 64
GEOMS = 4
PARTITIONS = 8
CELLS = 4096


def draw_new_index(key, part):
    base_count = C // PARTITIONS
    extra_count = base_count // 2
    counts = np.array([base_count + extra_count if offset % 2 == 0 else base_count - extra_count for offset in range(PARTITIONS)])
    bounds = jnp.asarray(np.cumsum(counts)[:-1], jnp.int32)

    def one_order(order_key):
        return jax.random.permutation(order_key, C).astype(jnp.int32)

    def one_geometry(geo_key):
        sub_keys = jax.random.split(geo_key, 2 * PARTITIONS)
        places = jax.vmap(one_order)(sub_keys[:PARTITIONS])
        shifts = jnp.sum((places[:, :, None] >= bounds[None, None, :]).astype(jnp.int32), axis=2)
        owners = (jnp.arange(PARTITIONS, dtype=jnp.int32)[:, None] + shifts) % PARTITIONS
        arrivals = jax.vmap(one_order)(sub_keys[PARTITIONS:])
        arrival_rows = arrivals[owners, places]
        return (owners * C + arrival_rows).reshape(-1).astype(jnp.int32)
    return jax.vmap(one_geometry)(jax.random.split(key, GEOMS))


def draw_source(key, part):

    def one_geometry(geo_key):
        sub_keys = jax.random.split(geo_key, 3)
        edge_ids = jnp.arange(CELLS * K, dtype=jnp.int32)
        cell_ids = edge_ids // K
        slot_ids = edge_ids % K
        device_ids = cell_ids // C
        row_ids = cell_ids % C
        kinds = jax.random.randint(sub_keys[0], (CELLS * K,), 0, 4, dtype=jnp.int32)
        local_pick = jax.random.randint(sub_keys[1], (CELLS * K,), 0, C, dtype=jnp.int32)
        rim_pick = jax.random.randint(sub_keys[2], (CELLS * K,), 0, HB, dtype=jnp.int32)
        from_prev = (kinds == 0) & (device_ids > 0) & (slot_ids > 0)
        from_next = (kinds == 1) & (device_ids < PARTITIONS - 1) & (slot_ids > 0)
        local_row = jnp.where(slot_ids == 0, (row_ids + 1) % C, local_pick)
        chosen = jnp.where(from_prev, (device_ids - 1) * C + C - HB + rim_pick, jnp.where(from_next, (device_ids + 1) * C + rim_pick, device_ids * C + local_row))
        return chosen.astype(jnp.int32)
    return jax.vmap(one_geometry)(jax.random.split(key, GEOMS))


def shard_levels(rng, dims, cuts, smallest, top_value):
    def one(axis_at, blocks):
        draws = jax.random.uniform(jax.random.fold_in(jax.random.fold_in(rng, 6), axis_at), (blocks,), jnp.float32, smallest / len(cuts), top_value / len(cuts))
        return jnp.repeat(jnp.exp(draws), dims[axis_at] // blocks).reshape((-1,) + (1,) * (len(dims) - axis_at - 1))

    loudness = one(*cuts[0])
    for cut in cuts[1:]:
        loudness = loudness * one(*cut)
    return loudness


def normal_values(own_key, dims, deviation, limit, pieces=(), kind=jnp.bfloat16):
    entries = jax.random.normal(own_key, dims, jnp.float32) * deviation
    if len(pieces) > 0:
        entries = shard_levels(own_key, dims, pieces, -0.22, 0.18) * entries
    return jnp.clip(entries, min=-limit, max=limit).astype(kind)


def setup_inputs(seed: int = 0) -> dict:
    key_of = jax.random.split(jax.random.key(seed), 11)
    return {
        "h_in": normal_values(key_of[0], (GEOMS, CELLS, D), 1.0, 6.0, ((0, 4), (1, 8))),
        "edge_in": normal_values(key_of[1], (GEOMS, CELLS * K, D), 1.0, 6.0, ((0, 4), (1, 8))),
        "new_index": draw_new_index(jax.random.fold_in(key_of[10], 71), 0),
        "source": draw_source(jax.random.fold_in(key_of[10], 71), 0),
        "w_edge_in": normal_values(key_of[4], (3 * D, D), (3 * D) ** -0.5, 0.15625),
        "w_edge_out": normal_values(key_of[5], (D, D), D ** -0.5, 0.25),
        "w_node_in": normal_values(key_of[6], (2 * D, D), (2 * D) ** -0.5, 0.1875),
        "w_node_out": normal_values(key_of[7], (D, D), D ** -0.5, 0.25),
        "cot_nodes": normal_values(key_of[8], (GEOMS, CELLS, D), 1.0, 6.0, ((0, 4), (1, 8))),
        "cot_edges": normal_values(key_of[9], (GEOMS, CELLS * K, D), 1.0, 6.0, ((0, 4), (1, 8))),
    }


def normalize(values):
    center = values - lax.optimization_barrier(jnp.mean(values, axis=-1, keepdims=True))
    inverse = lax.rsqrt(lax.optimization_barrier(jnp.mean(center * center, axis=-1, keepdims=True)) + 1e-05)
    return (center * inverse, inverse)

def normalize_back(normed, inverse, upstream):
    return inverse * (upstream - lax.optimization_barrier(jnp.mean(upstream, axis=-1, keepdims=True)) - normed * lax.optimization_barrier(jnp.mean(upstream * normed, axis=-1, keepdims=True)))

def silu_slope(values):
    sigma = jax.nn.sigmoid(values)
    return sigma * (1.0 + values * (1.0 - sigma))

def matmul(left, right):
    return jnp.dot(left, right, preferred_element_type=jnp.float32)

def layer_math(nodes, edges, senders, w_edge_in, w_edge_out, w_node_in, w_node_out, cot_nodes, cot_edges, fan_in):
    width = nodes.shape[1]
    cell_count = nodes.shape[0]
    receivers = jnp.repeat(nodes, fan_in, axis=0)
    w_edge_self = w_edge_in[:width]
    w_edge_send = w_edge_in[width:2 * width]
    w_edge_recv = w_edge_in[2 * width:]
    w_node_self = w_node_in[:width]
    w_node_agg = w_node_in[width:]
    edge_pre = matmul(edges, w_edge_self) + matmul(senders, w_edge_send) + matmul(receivers, w_edge_recv)
    edge_hidden = jax.nn.silu(edge_pre).astype(jnp.bfloat16)
    edge_post = matmul(edge_hidden, w_edge_out)
    edge_normed, edge_inverse = normalize(edge_post)
    edge_new = (edges.astype(jnp.float32) + edge_normed).astype(jnp.bfloat16)
    summed = lax.optimization_barrier(jnp.sum(edge_new.astype(jnp.float32).reshape(cell_count, fan_in, width), axis=1)).astype(jnp.bfloat16)
    node_pre = matmul(nodes, w_node_self) + matmul(summed, w_node_agg)
    node_hidden = jax.nn.silu(node_pre).astype(jnp.bfloat16)
    node_post = matmul(node_hidden, w_node_out)
    node_normed, node_inverse = normalize(node_post)
    node_new = (nodes.astype(jnp.float32) + node_normed).astype(jnp.bfloat16)
    node_upstream = cot_nodes.astype(jnp.float32)
    node_post_grad = normalize_back(node_normed, node_inverse, node_upstream).astype(jnp.bfloat16)
    grad_node_out = matmul(node_hidden.T, node_post_grad)
    node_pre_grad = (matmul(node_post_grad, w_node_out.T) * silu_slope(node_pre)).astype(jnp.bfloat16)
    grad_node_self = matmul(nodes.T, node_pre_grad)
    grad_node_agg = matmul(summed.T, node_pre_grad)
    summed_grad = matmul(node_pre_grad, w_node_agg.T)
    edge_upstream = cot_edges.astype(jnp.float32) + jnp.repeat(summed_grad, fan_in, axis=0)
    edge_post_grad = normalize_back(edge_normed, edge_inverse, edge_upstream).astype(jnp.bfloat16)
    grad_edge_out = matmul(edge_hidden.T, edge_post_grad)
    edge_pre_grad = (matmul(edge_post_grad, w_edge_out.T) * silu_slope(edge_pre)).astype(jnp.bfloat16)
    grad_edge_self = matmul(edges.T, edge_pre_grad)
    grad_edge_send = matmul(senders.T, edge_pre_grad)
    grad_edge_recv = matmul(receivers.T, edge_pre_grad)
    grad_edge = (edge_upstream + matmul(edge_pre_grad, w_edge_self.T)).astype(jnp.bfloat16)
    sender_grad = matmul(edge_pre_grad, w_edge_send.T)
    receiver_grad = lax.optimization_barrier(jnp.sum(matmul(edge_pre_grad, w_edge_recv.T).reshape(cell_count, fan_in, width), axis=1))
    node_grad = node_upstream + matmul(node_pre_grad, w_node_self.T) + receiver_grad
    stacked = jnp.concatenate([grad_edge_self, grad_edge_send, grad_edge_recv, grad_edge_out, grad_node_self, grad_node_agg, grad_node_out], axis=0)
    return (node_new, edge_new, grad_edge, node_grad, sender_grad, stacked)

def reference(h_in, edge_in, new_index, source, w_edge_in, w_edge_out, w_node_in, w_node_out, cot_nodes, cot_edges):
    node_list = []
    edge_list = []
    grad_in_list = []
    grad_edge_list = []
    total = jnp.zeros((7 * D, D), jnp.float32)
    for geometry in range(GEOMS):
        places = new_index[geometry].astype(jnp.int32)
        senders_at = source[geometry].astype(jnp.int32)
        nodes = jnp.zeros((CELLS, D), jnp.bfloat16).at[places].set(h_in[geometry])
        senders = nodes[senders_at]
        node_new, edge_new, grad_edge, node_grad, sender_grad, stacked = layer_math(nodes, edge_in[geometry], senders, w_edge_in, w_edge_out, w_node_in, w_node_out, cot_nodes[geometry], cot_edges[geometry], K)
        node_grad = node_grad + jnp.zeros((CELLS, D), jnp.float32).at[senders_at].add(sender_grad)
        grad_in_list.append(node_grad.astype(jnp.bfloat16)[places])
        node_list.append(node_new)
        edge_list.append(edge_new)
        grad_edge_list.append(grad_edge)
        total = total + stacked
    weight_grads = total * (1.0 / math.sqrt(GEOMS * CELLS * K))
    return (jnp.stack(node_list), jnp.stack(edge_list), jnp.stack(grad_in_list), jnp.stack(grad_edge_list), weight_grads)
```

```python
import functools
import math

import jax
import jax.numpy as jnp
from jax import lax
from jax.experimental import pallas as pl
from jax.experimental.pallas import tpu as pltpu
from jax.sharding import PartitionSpec as P

HB = 64
LANES = 128
EDGE_BLOCK = 256
MIB = 1024 * 1024
F32 = jnp.float32
BF16 = jnp.bfloat16
VMEM = pltpu.VMEM
SMEM = pltpu.SMEM


def dot_nn(left, right):
    return lax.dot_general(left, right, (((1,), (0,)), ((), ())), preferred_element_type=F32)


def dot_nt(left, right):
    return lax.dot_general(left, right, (((1,), (1,)), ((), ())), preferred_element_type=F32)


def dot_tn(left, right):
    return lax.dot_general(left, right, (((0,), (0,)), ((), ())), preferred_element_type=F32)


def iota(shape, axis):
    return lax.broadcasted_iota(jnp.int32, shape, axis)


def hot(condition):
    return jnp.where(condition, 1.0, 0.0).astype(BF16)


def sigmoid(values):
    return 0.5 * jnp.tanh(0.5 * values) + 0.5


def normalize(values):
    center = values - jnp.mean(values, axis=-1, keepdims=True)
    inverse = lax.rsqrt(jnp.mean(center * center, axis=-1, keepdims=True) + 1e-05)
    return center * inverse, inverse


def normalize_back(normed, inverse, upstream):
    return inverse * (
        upstream
        - jnp.mean(upstream, axis=-1, keepdims=True)
        - normed * jnp.mean(upstream * normed, axis=-1, keepdims=True)
    )


def slots_of(index, me, part_count, cell_count):
    owner = jnp.zeros_like(index)
    for part in range(1, part_count):
        owner = owner + jnp.where(index >= part * cell_count, 1, 0)
    row = index - owner * cell_count
    ahead = owner - me
    ahead = jnp.where(ahead < 0, ahead + part_count, ahead)
    high = -(-part_count // 16) * 16
    member = hot(iota((high, cell_count), 0) == ahead)
    before = hot(iota((cell_count, cell_count), 0) < iota((cell_count, cell_count), 1))
    rank = jnp.sum(member.astype(F32) * dot_nn(member, before), axis=0, keepdims=True)
    return ahead * LANES + rank.astype(jnp.int32), row


def pack_kernel(part_count, capacity, scal, h_ref, index_ref, *outs):
    cell_count, width = h_ref.shape
    chunks = width // LANES
    slot, row = slots_of(index_ref[...], scal[0], part_count, cell_count)
    kind = iota((16, cell_count), 0)
    coded = jnp.where(
        kind == 0, row >> 8, jnp.where(kind == 1, row & 255, jnp.where(kind == 2, 1, 0))
    )
    coded = coded.astype(F32).astype(BF16)
    cells = h_ref[...]
    for step in range(part_count):
        pick = hot(iota((LANES, cell_count), 0) + step * LANES == slot)
        rows = dot_nn(pick, cells).astype(BF16)
        for chunk in range(chunks):
            outs[step][chunk * capacity : (chunk + 1) * capacity, :] = rows[
                :capacity, chunk * LANES : (chunk + 1) * LANES
            ]
        outs[step][chunks * capacity :, :] = dot_nt(coded, pick).astype(BF16)


def place(ids, cell_count):
    ids = ids.astype(F32)
    spot = ids[0:1] * 256.0 + ids[1:2] + (ids[2:3] - 1.0) * 65536.0
    return hot(iota((cell_count, LANES), 0) == spot.astype(jnp.int32))


def unpack_kernel(part_count, capacity, *refs):
    blocks = refs[:part_count]
    nodes_ref, head_ref, tail_ref, ids_ref, rows_ref, hot_ref = refs[part_count:]
    cell_count, width = nodes_ref.shape
    chunks = width // LANES
    for step in range(part_count):
        base = step * LANES
        ids = blocks[step][chunks * capacity :, :]
        ids_ref[step * 16 : (step + 1) * 16, :] = ids
        hot_ref[:, base : base + LANES] = place(ids, cell_count)
        for chunk in range(chunks):
            rows_ref[base : base + capacity, chunk * LANES : (chunk + 1) * LANES] = blocks[step][
                chunk * capacity : (chunk + 1) * capacity, :
            ]
        if capacity < LANES:
            rows_ref[base + capacity : base + LANES, :] = jnp.zeros(
                (LANES - capacity, width), BF16
            )
    nodes = dot_nn(hot_ref[...], rows_ref[...]).astype(BF16)
    nodes_ref[...] = nodes
    head_ref[...] = nodes[:HB]
    tail_ref[...] = nodes[cell_count - HB :]


def forward_kernel(
    fan_in,
    scal,
    source_ref,
    edges_ref,
    nodes_ref,
    prev_ref,
    next_ref,
    cot_ref,
    w_edge_in_ref,
    w_edge_out_ref,
    w_node_in_ref,
    w_node_out_ref,
    edge_new_ref,
    hidden_ref,
    slope_ref,
    normed_ref,
    inverse_ref,
    node_new_ref,
    summed_grad_ref,
    base_ref,
    keep_ref,
    send_ref,
    table_ref,
    recv_hi_ref,
    recv_lo_ref,
    summed_ref,
    scale,
):
    cell_count, width = nodes_ref.shape
    step = pl.program_id(0)
    padded = cell_count + 2 * HB
    cells = EDGE_BLOCK // fan_in

    @pl.when(step == 0)
    def _():
        w_send = w_edge_in_ref[width : 2 * width, :]
        table_ref[:HB, :] = dot_nn(prev_ref[...], w_send).astype(BF16)
        table_ref[HB : HB + cell_count, :] = dot_nn(nodes_ref[...], w_send).astype(BF16)
        table_ref[HB + cell_count : padded, :] = dot_nn(next_ref[...], w_send).astype(BF16)
        received = dot_nn(nodes_ref[...], w_edge_in_ref[2 * width :, :])
        high = received.astype(BF16)
        recv_hi_ref[...] = high
        recv_lo_ref[...] = (received - high.astype(F32)).astype(BF16)

    spot = pl.ds(pl.multiple_of(step * cells, cells), cells)
    table_ref[padded : padded + cells, :] = recv_hi_ref[spot, :]
    table_ref[padded + cells : padded + 2 * cells, :] = recv_lo_ref[spot, :]
    local = (source_ref[...] - scal[0] * cell_count + HB).astype(F32)
    local = jnp.transpose(jnp.broadcast_to(local, (LANES, EDGE_BLOCK))).astype(jnp.int32)
    lane = iota((EDGE_BLOCK, LANES), 1)
    pieces = [hot(local == lane + at) for at in range(0, padded, LANES)]
    owner = iota((EDGE_BLOCK, 2 * cells), 0) // fan_in
    member = iota((EDGE_BLOCK, 2 * cells), 1)
    pieces.append(hot((owner == member) | (owner + cells == member)))
    gather = jnp.concatenate(pieces, axis=1)
    edges = edges_ref[...]
    pre = dot_nn(edges, w_edge_in_ref[:width, :]) + dot_nn(gather, table_ref[...])
    gate = sigmoid(pre)
    hidden = (pre * gate).astype(BF16)
    hidden_ref[...] = hidden
    slope_ref[...] = (gate * (1.0 + pre * (1.0 - gate))).astype(BF16)
    normed, inverse = normalize(dot_nn(hidden, w_edge_out_ref[...]))
    normed_ref[...] = normed.astype(BF16)
    inverse_ref[...] = inverse
    edge_new = (edges.astype(F32) + normed).astype(BF16)
    edge_new_ref[...] = edge_new
    collect = hot(iota((cells, EDGE_BLOCK), 0) == iota((cells, EDGE_BLOCK), 1) // fan_in)
    summed_ref[spot, :] = dot_nn(collect, edge_new).astype(BF16)

    @pl.when(step == pl.num_programs(0) - 1)
    def _():
        nodes = nodes_ref[...]
        summed = summed_ref[...]
        node_pre = dot_nn(nodes, w_node_in_ref[:width, :]) + dot_nn(
            summed, w_node_in_ref[width:, :]
        )
        node_gate = sigmoid(node_pre)
        node_hidden = (node_pre * node_gate).astype(BF16)
        node_normed, node_inverse = normalize(dot_nn(node_hidden, w_node_out_ref[...]))
        node_new_ref[...] = (nodes.astype(F32) + node_normed).astype(BF16)
        upstream = cot_ref[...].astype(F32)
        post_grad = normalize_back(node_normed, node_inverse, upstream).astype(BF16)
        node_slope = node_gate * (1.0 + node_pre * (1.0 - node_gate))
        pre_grad = (dot_nt(post_grad, w_node_out_ref[...]) * node_slope).astype(BF16)
        summed_grad = dot_nt(pre_grad, w_node_in_ref[width:, :])
        high = summed_grad.astype(BF16)
        low = (summed_grad - high.astype(F32)).astype(BF16)
        for block in range(cell_count // cells):
            at = slice(block * cells, (block + 1) * cells)
            summed_grad_ref[block * 2 * cells : block * 2 * cells + cells, :] = high[at]
            summed_grad_ref[block * 2 * cells + cells : (block + 1) * 2 * cells, :] = low[at]
        base_ref[...] = upstream + dot_nt(pre_grad, w_node_in_ref[:width, :])
        half = width // 2
        for mine in (0, 1):

            @pl.when(scal[1] == mine)
            def _(mine=mine):
                for target, part in ((keep_ref, mine), (send_ref, 1 - mine)):
                    at = slice(part * half, (part + 1) * half)
                    for place_at, left, right in (
                        (0, nodes, pre_grad),
                        (1, summed, pre_grad),
                        (2, node_hidden, post_grad),
                    ):
                        target[place_at * width : (place_at + 1) * width, :] = (
                            dot_tn(left, right[:, at]) * scale
                        ).astype(BF16)


def backward_kernel(
    fan_in,
    scal,
    source_ref,
    cot_ref,
    summed_grad_ref,
    slope_ref,
    normed_ref,
    inverse_ref,
    base_ref,
    w_edge_in_ref,
    w_edge_out_ref,
    pre_grad_ref,
    post_grad_ref,
    sent_ref,
    received_ref,
    to_prev_ref,
    to_next_ref,
    node_grad_ref,
    all_grad_ref,
    scatter_ref,
):
    cell_count, width = node_grad_ref.shape
    step = pl.program_id(0)
    padded = cell_count + 2 * HB
    cells = EDGE_BLOCK // fan_in
    member = iota((EDGE_BLOCK, 2 * cells), 1)
    owner = iota((EDGE_BLOCK, 2 * cells), 0) // fan_in
    spread = hot((owner == member) | (owner + cells == member))
    upstream = cot_ref[...].astype(F32) + dot_nn(spread, summed_grad_ref[...])
    post_grad = normalize_back(normed_ref[...].astype(F32), inverse_ref[...], upstream).astype(BF16)
    post_grad_ref[...] = post_grad
    pre_grad = (dot_nt(post_grad, w_edge_out_ref[...]) * slope_ref[...].astype(F32)).astype(BF16)
    pre_grad_ref[...] = pre_grad
    rows = pl.ds(pl.multiple_of(step * EDGE_BLOCK, EDGE_BLOCK), EDGE_BLOCK)
    all_grad_ref[rows, :] = pre_grad
    local = source_ref[...] - scal[0] * cell_count + HB
    scatter_ref[:, rows] = hot(iota((padded, EDGE_BLOCK), 0) == local)
    collect = hot(iota((cells, EDGE_BLOCK), 0) == iota((cells, EDGE_BLOCK), 1) // fan_in)
    spot = pl.ds(pl.multiple_of(step * cells, cells), cells)
    received_ref[spot, :] = dot_nn(collect, pre_grad).astype(BF16)

    @pl.when(step == pl.num_programs(0) - 1)
    def _():
        sent = dot_nn(scatter_ref[...], all_grad_ref[...]).astype(BF16)
        sent_ref[...] = sent
        sender = dot_nt(sent, w_edge_in_ref[width : 2 * width, :])
        to_prev_ref[...] = sender[:HB].astype(BF16)
        to_next_ref[...] = sender[HB + cell_count :].astype(BF16)
        node_grad_ref[...] = (
            base_ref[...]
            + dot_nt(received_ref[...], w_edge_in_ref[2 * width :, :])
            + sender[HB : HB + cell_count]
        )


def weight_kernel(
    scal,
    edges_ref,
    pre_grad_ref,
    hidden_ref,
    post_grad_ref,
    nodes_ref,
    prev_ref,
    next_ref,
    sent_ref,
    received_ref,
    keep_ref,
    send_ref,
    scale,
):
    cell_count, width = nodes_ref.shape
    half = width // 2
    for mine in (0, 1):

        @pl.when(scal[1] == mine)
        def _(mine=mine):
            for target, part in ((send_ref, 1 - mine), (keep_ref, mine)):
                at = slice(part * half, (part + 1) * half)

                def put(place_at, value, target=target):
                    target[place_at * width : (place_at + 1) * width, :] = (value * scale).astype(
                        BF16
                    )

                put(0, dot_tn(edges_ref[...], pre_grad_ref[:, at]))
                put(
                    1,
                    dot_tn(prev_ref[...], sent_ref[:HB, at])
                    + dot_tn(nodes_ref[...], sent_ref[HB : HB + cell_count, at])
                    + dot_tn(next_ref[...], sent_ref[HB + cell_count :, at]),
                )
                put(2, dot_tn(nodes_ref[...], received_ref[:, at]))
                put(3, dot_tn(hidden_ref[...], post_grad_ref[:, at]))


def edge_kernel(fan_in, cot_ref, summed_grad_ref, pre_grad_ref, w_edge_in_ref, grad_edge_ref):
    width = cot_ref.shape[1]
    cells = EDGE_BLOCK // fan_in
    member = iota((EDGE_BLOCK, 2 * cells), 1)
    owner = iota((EDGE_BLOCK, 2 * cells), 0) // fan_in
    spread = hot((owner == member) | (owner + cells == member))
    upstream = cot_ref[...].astype(F32) + dot_nn(spread, summed_grad_ref[...])
    grad_edge_ref[...] = (upstream + dot_nt(pre_grad_ref[...], w_edge_in_ref[:width, :])).astype(
        BF16
    )


def return_kernel(part_count, capacity, node_grad_ref, from_prev_ref, from_next_ref, ids_ref, *outs):
    cell_count, width = node_grad_ref.shape
    chunks = width // LANES
    first = node_grad_ref[:HB, :] + from_prev_ref[...].astype(F32)
    last = node_grad_ref[cell_count - HB :, :] + from_next_ref[...].astype(F32)
    grad = jnp.concatenate(
        [first, node_grad_ref[HB : cell_count - HB, :], last], axis=0
    ).astype(BF16)
    for step in range(part_count):
        pick = place(ids_ref[step * 16 : (step + 1) * 16, :], cell_count)
        rows = dot_tn(pick, grad).astype(BF16)
        for chunk in range(chunks):
            outs[step][chunk * capacity : (chunk + 1) * capacity, :] = rows[
                :capacity, chunk * LANES : (chunk + 1) * LANES
            ]


def finish_kernel(part_count, capacity, scal, index_ref, *refs):
    blocks = refs[:part_count]
    out_ref, rows_ref, pick_ref = refs[part_count:]
    cell_count, width = out_ref.shape
    chunks = width // LANES
    slot, _ = slots_of(index_ref[...], scal[0], part_count, cell_count)
    for step in range(part_count):
        base = step * LANES
        pick_ref[base : base + LANES, :] = hot(iota((LANES, cell_count), 0) + base == slot)
        for chunk in range(chunks):
            rows_ref[base : base + capacity, chunk * LANES : (chunk + 1) * LANES] = blocks[step][
                chunk * capacity : (chunk + 1) * capacity, :
            ]
        if capacity < LANES:
            rows_ref[base + capacity : base + LANES, :] = jnp.zeros(
                (LANES - capacity, width), BF16
            )
    out_ref[...] = dot_tn(pick_ref[...], rows_ref[...]).astype(BF16)


def shape(dims, kind=BF16):
    return jax.ShapeDtypeStruct(dims, kind)


def whole(count):
    return [pl.BlockSpec(memory_space=VMEM)] * count


def scalars():
    return pl.BlockSpec(memory_space=SMEM)


def params(limit):
    return pltpu.CompilerParams(vmem_limit_bytes=limit * MIB)


def cost(flops, bytes_accessed):
    return pl.CostEstimate(flops=flops, bytes_accessed=bytes_accessed, transcendentals=0)


def full(dims):
    return pl.BlockSpec(dims, lambda step: (0,) * len(dims))


def rows_spec(rows, columns):
    return pl.BlockSpec((rows, columns), lambda step: (step, 0))


def swap(value, axis, bit):
    count = lax.axis_size(axis)
    return lax.ppermute(value, axis, [(at, at ^ bit) for at in range(count)])


def add(left, right):
    return (left.astype(F32) + right.astype(F32)).astype(BF16)


def halve(value, axis, bit, dim):
    mine = (lax.axis_index(axis) // bit) % 2
    half = value.shape[dim] // 2
    keep = lax.dynamic_slice_in_dim(value, mine * half, half, dim)
    send = lax.dynamic_slice_in_dim(value, (1 - mine) * half, half, dim)
    return add(keep, swap(send, axis, bit))


def halve_owner(value, axis):
    mine = lax.axis_index(axis) % 2
    pairs = value.reshape((value.shape[0] // 2, 2) + value.shape[1:])
    keep = lax.dynamic_index_in_dim(pairs, mine, 1, keepdims=False)
    send = lax.dynamic_index_in_dim(pairs, 1 - mine, 1, keepdims=False)
    return add(keep, swap(send, axis, 1))


def reduce_weights(value, geom_count, part_count):
    bits = []
    bit = 2
    while bit < geom_count:
        bits.append(bit)
        bit *= 2
    rows, columns = value.shape
    value = value.reshape(part_count, rows // part_count, columns)
    half = rows // part_count // 2
    left = value[:, :half]
    right = value[:, half:]
    for bit in bits:
        left = halve(left, "geom", bit, 2)
    left = halve_owner(left, "dom")
    right = halve_owner(right, "dom")
    for bit in bits:
        right = halve(right, "geom", bit, 2)
    both = jnp.concatenate([left, right], axis=1)
    owner = lax.axis_index("dom") // 2
    total = lax.dynamic_index_in_dim(both, owner, 0, keepdims=False).astype(F32)
    for other in range(part_count // 2 - 1, 0, -1):
        piece = lax.dynamic_index_in_dim(both, owner ^ other, 0, keepdims=False)
        total = total + swap(piece, "dom", 2 * other).astype(F32)
    total = total.astype(BF16)
    for bit in bits[::-1] + [1]:
        theirs = swap(total, "geom", bit)
        mine = (lax.axis_index("geom") // bit) % 2
        total = jnp.where(
            mine == 0,
            jnp.concatenate([total, theirs], axis=1),
            jnp.concatenate([theirs, total], axis=1),
        )
    return total.astype(F32)


def shift(value, steps):
    count = lax.axis_size("dom")
    return lax.ppermute(value, "dom", [(at, (at + steps) % count) for at in range(count)])


def neighbour(value, step):
    count = lax.axis_size("dom")
    return lax.ppermute(
        value, "dom", [(at, at + step) for at in range(count) if 0 <= at + step < count]
    )


def send_order(part_count):
    return sorted(range(1, part_count), key=lambda at: (-min(at, part_count - at), at))


def local(
    h_in,
    edge_in,
    new_index,
    source,
    w_edge_in,
    w_edge_out,
    w_node_in,
    w_node_out,
    cot_nodes,
    cot_edges,
):
    _, cell_count, width = h_in.shape
    edge_count = source.shape[1]
    fan_in = edge_count // cell_count
    part_count = lax.axis_size("dom")
    geom_count = lax.axis_size("geom")
    capacity = cell_count // part_count + cell_count // part_count // 2
    chunks = width // LANES
    block_rows = chunks * capacity
    scale = 1.0 / math.sqrt(geom_count * part_count * cell_count * fan_in)
    scal = jnp.stack([lax.axis_index("dom"), lax.axis_index("geom") % 2]).astype(jnp.int32)
    edges = edge_in[0]
    cot = cot_edges[0]

    sends = pl.pallas_call(
        functools.partial(pack_kernel, part_count, capacity),
        out_shape=[shape((block_rows + 16, LANES))] * part_count,
        in_specs=[scalars()] + whole(2),
        out_specs=whole(part_count),
        compiler_params=params(16),
        name="pack",
    )(scal, h_in[0], new_index)
    got = {0: sends[0]}
    for step in send_order(part_count):
        got[step] = shift(sends[step], step)
    nodes, head, tail, ids = pl.pallas_call(
        functools.partial(unpack_kernel, part_count, capacity),
        out_shape=[
            shape((cell_count, width)),
            shape((HB, width)),
            shape((HB, width)),
            shape((part_count * 16, LANES)),
        ],
        in_specs=whole(part_count),
        out_specs=whole(4),
        scratch_shapes=[
            VMEM((part_count * LANES, width), BF16),
            VMEM((cell_count, part_count * LANES), BF16),
        ],
        compiler_params=params(16),
        name="unpack",
    )(*[got[step] for step in range(part_count)])
    before = neighbour(tail, 1)
    after = neighbour(head, -1)

    steps = edge_count // EDGE_BLOCK
    cells = EDGE_BLOCK // fan_in
    padded = cell_count + 2 * HB
    half = width // 2
    edge_rows = rows_spec(EDGE_BLOCK, width)
    (
        edge_new,
        hidden,
        slope,
        normed,
        inverse,
        node_new,
        summed_grad,
        base,
        keep_node,
        send_node,
    ) = pl.pallas_call(
        lambda *refs: forward_kernel(fan_in, *refs, scale=scale),
        grid=(steps,),
        out_shape=[
            shape((edge_count, width)),
            shape((edge_count, width)),
            shape((edge_count, width)),
            shape((edge_count, width)),
            shape((edge_count, 1), F32),
            shape((cell_count, width)),
            shape((2 * cell_count, width)),
            shape((cell_count, width), F32),
            shape((3 * width, half)),
            shape((3 * width, half)),
        ],
        in_specs=[
            scalars(),
            pl.BlockSpec((1, EDGE_BLOCK), lambda step: (0, step)),
            edge_rows,
            full((cell_count, width)),
            full((HB, width)),
            full((HB, width)),
            full((cell_count, width)),
            full(w_edge_in.shape),
            full(w_edge_out.shape),
            full(w_node_in.shape),
            full(w_node_out.shape),
        ],
        out_specs=[
            edge_rows,
            edge_rows,
            edge_rows,
            edge_rows,
            rows_spec(EDGE_BLOCK, 1),
            full((cell_count, width)),
            full((2 * cell_count, width)),
            full((cell_count, width)),
            full((3 * width, half)),
            full((3 * width, half)),
        ],
        scratch_shapes=[
            VMEM((padded + 2 * cells, width), BF16),
            VMEM((cell_count, width), BF16),
            VMEM((cell_count, width), BF16),
            VMEM((cell_count, width), BF16),
        ],
        compiler_params=params(40),
        name="forward",
    )(
        scal,
        source,
        edges,
        nodes,
        before,
        after,
        cot_nodes[0],
        w_edge_in,
        w_edge_out,
        w_node_in,
        w_node_out,
    )

    pre_grad, post_grad, sent, received, to_prev, to_next, node_grad = pl.pallas_call(
        functools.partial(backward_kernel, fan_in),
        grid=(steps,),
        out_shape=[
            shape((edge_count, width)),
            shape((edge_count, width)),
            shape((padded, width)),
            shape((cell_count, width)),
            shape((HB, width)),
            shape((HB, width)),
            shape((cell_count, width), F32),
        ],
        in_specs=[
            scalars(),
            pl.BlockSpec((1, EDGE_BLOCK), lambda step: (0, step)),
            edge_rows,
            rows_spec(2 * cells, width),
            edge_rows,
            edge_rows,
            rows_spec(EDGE_BLOCK, 1),
            full((cell_count, width)),
            full(w_edge_in.shape),
            full(w_edge_out.shape),
        ],
        out_specs=[
            edge_rows,
            edge_rows,
            full((padded, width)),
            full((cell_count, width)),
            full((HB, width)),
            full((HB, width)),
            full((cell_count, width)),
        ],
        scratch_shapes=[
            VMEM((edge_count, width), BF16),
            VMEM((padded, edge_count), BF16),
        ],
        compiler_params=params(40),
        name="backward",
    )(scal, source, cot, summed_grad, slope, normed, inverse, base, w_edge_in, w_edge_out)
    from_next = neighbour(to_prev, -1)
    from_prev = neighbour(to_next, 1)

    keep_edge, send_edge = pl.pallas_call(
        lambda *refs: weight_kernel(*refs, scale=scale),
        out_shape=[shape((4 * width, half))] * 2,
        in_specs=[scalars()] + whole(9),
        out_specs=whole(2),
        compiler_params=params(40),
        name="weights",
    )(scal, edges, pre_grad, hidden, post_grad, nodes, before, after, sent, received)

    grad_edge = pl.pallas_call(
        functools.partial(edge_kernel, fan_in),
        grid=(steps,),
        out_shape=shape((edge_count, width)),
        in_specs=[edge_rows, rows_spec(2 * cells, width), edge_rows, full(w_edge_in.shape)],
        out_specs=edge_rows,
        compiler_params=params(24),
        name="edges",
    )(cot, summed_grad, pre_grad, w_edge_in)

    returning = pl.pallas_call(
        functools.partial(return_kernel, part_count, capacity),
        out_shape=[shape((block_rows, LANES))] * part_count,
        in_specs=whole(4),
        out_specs=whole(part_count),
        compiler_params=params(16),
        name="returning",
    )(node_grad, from_prev, from_next, ids)
    back = {0: returning[0]}
    for step in send_order(part_count):
        back[step] = shift(returning[step], -step)
    grad_in = pl.pallas_call(
        functools.partial(finish_kernel, part_count, capacity),
        out_shape=shape((cell_count, width)),
        in_specs=[scalars()] + whole(1 + part_count),
        out_specs=pl.BlockSpec(memory_space=VMEM),
        scratch_shapes=[
            VMEM((part_count * LANES, width), BF16),
            VMEM((part_count * LANES, cell_count), BF16),
        ],
        compiler_params=params(16),
        name="finish",
    )(scal, new_index, *[back[step] for step in range(part_count)])

    core_edge = add(keep_edge, swap(send_edge, "geom", 1))
    core_node = add(keep_node, swap(send_node, "geom", 1))
    weight_grads = reduce_weights(
        jnp.concatenate([core_edge, core_node], axis=0), geom_count, part_count
    )
    return (node_new[None], edge_new[None], grad_in[None], grad_edge[None], weight_grads)


def solution(mesh):
    return jax.shard_map(
        local,
        mesh=mesh,
        in_specs=(
            P("geom", "dom", None),
            P("geom", "dom", None),
            P("geom", "dom"),
            P("geom", "dom"),
            P(),
            P(),
            P(),
            P(),
            P("geom", "dom", None),
            P("geom", "dom", None),
        ),
        out_specs=(
            P("geom", "dom", None),
            P("geom", "dom", None),
            P("geom", "dom", None),
            P("geom", "dom", None),
            P("dom", None),
        ),
        check_vma=False,
    )
```

```python
import functools
import math

import jax
import jax.numpy as jnp
from jax import lax
from jax.experimental import pallas as pl
from jax.experimental.pallas import tpu as pltpu
from jax.sharding import PartitionSpec as P

HB = 64
LANES = 128
EDGE_BLOCK = 512
MIB = 1024 * 1024
MAIN_LIMIT = 25
PREP_LIMIT = 20
PART, CORE, DOM_BIT, OWNER, GEOM_BITS = range(5)
F32 = jnp.float32
BF16 = jnp.bfloat16
VMEM = pltpu.VMEM
SMEM = pltpu.SMEM


def dot_nn(left, right):
    return lax.dot_general(left, right, (((1,), (0,)), ((), ())), preferred_element_type=F32)


def dot_nt(left, right):
    return lax.dot_general(left, right, (((1,), (1,)), ((), ())), preferred_element_type=F32)


def dot_tn(left, right):
    return lax.dot_general(left, right, (((0,), (0,)), ((), ())), preferred_element_type=F32)


def iota(shape, axis):
    return lax.broadcasted_iota(jnp.int32, shape, axis)


def hot(condition):
    return jnp.where(condition, 1.0, 0.0).astype(BF16)


def sigmoid(values):
    return 0.5 * jnp.tanh(0.5 * values) + 0.5


def normalize(values):
    center = values - jnp.mean(values, axis=-1, keepdims=True)
    inverse = lax.rsqrt(jnp.mean(center * center, axis=-1, keepdims=True) + 1e-05)
    return center * inverse, inverse


def normalize_back(normed, inverse, upstream):
    return inverse * (
        upstream
        - jnp.mean(upstream, axis=-1, keepdims=True)
        - normed * jnp.mean(upstream * normed, axis=-1, keepdims=True)
    )


def slots_of(index, me, part_count, cell_count):
    owner = jnp.zeros_like(index)
    for part in range(1, part_count):
        owner = owner + jnp.where(index >= part * cell_count, 1, 0)
    row = index - owner * cell_count
    ahead = owner - me
    ahead = jnp.where(ahead < 0, ahead + part_count, ahead)
    high = -(-part_count // 16) * 16
    member = hot(iota((high, cell_count), 0) == ahead)
    before = hot(iota((cell_count, cell_count), 0) < iota((cell_count, cell_count), 1))
    rank = jnp.sum(member.astype(F32) * dot_nn(member, before), axis=0, keepdims=True)
    return ahead * LANES + rank.astype(jnp.int32), row


def pack_kernel(part_count, capacity, scal, h_ref, index_ref, *outs):
    cell_count, width = h_ref.shape
    chunks = width // LANES
    slot, row = slots_of(index_ref[...], scal[PART], part_count, cell_count)
    kind = iota((16, cell_count), 0)
    coded = jnp.where(
        kind == 0, row >> 8, jnp.where(kind == 1, row & 255, jnp.where(kind == 2, 1, 0))
    )
    coded = coded.astype(F32).astype(BF16)
    cells = h_ref[...]
    for step in range(part_count):
        pick = hot(iota((LANES, cell_count), 0) + step * LANES == slot)
        rows = dot_nn(pick, cells).astype(BF16)
        for chunk in range(chunks):
            outs[step][chunk * capacity : (chunk + 1) * capacity, :] = rows[
                :capacity, chunk * LANES : (chunk + 1) * LANES
            ]
        outs[step][chunks * capacity :, :] = dot_nt(coded, pick).astype(BF16)
    outs[part_count][...] = jnp.zeros(outs[part_count].shape, F32)


def place(ids, cell_count):
    ids = ids.astype(F32)
    spot = ids[0:1] * 256.0 + ids[1:2] + (ids[2:3] - 1.0) * 65536.0
    return hot(iota((cell_count, LANES), 0) == spot.astype(jnp.int32))


def unpack_kernel(part_count, capacity, *refs):
    blocks = refs[:part_count]
    _, nodes_ref, head_ref, tail_ref, ids_ref, rows_ref, hot_ref = refs[part_count:]
    cell_count, width = nodes_ref.shape
    chunks = width // LANES
    for step in range(part_count):
        base = step * LANES
        ids = blocks[step][chunks * capacity :, :]
        ids_ref[step * 16 : (step + 1) * 16, :] = ids
        hot_ref[:, base : base + LANES] = place(ids, cell_count)
        for chunk in range(chunks):
            rows_ref[base : base + capacity, chunk * LANES : (chunk + 1) * LANES] = blocks[step][
                chunk * capacity : (chunk + 1) * capacity, :
            ]
        if capacity < LANES:
            rows_ref[base + capacity : base + LANES, :] = jnp.zeros(
                (LANES - capacity, width), BF16
            )
    nodes = dot_nn(hot_ref[...], rows_ref[...]).astype(BF16)
    nodes_ref[...] = nodes
    head_ref[...] = nodes[:HB]
    tail_ref[...] = nodes[cell_count - HB :]


def prep_kernel(
    fan_in,
    cell_count,
    scal,
    source_hbm,
    edges_hbm,
    cot_nodes_hbm,
    cot_edges_hbm,
    w_edge_in_hbm,
    w_edge_out_hbm,
    w_node_in_hbm,
    w_node_out_hbm,
    _,
    edges_ref,
    cot_nodes_ref,
    cot_edges_ref,
    w_edge_in_ref,
    w_edge_out_ref,
    w_node_in_ref,
    w_node_out_ref,
    gather_ref,
    scatter_ref,
    pre_ref,
    token_ref,
    source_ref,
    sems,
):
    edge_count, width = edges_ref.shape
    padded = cell_count + 2 * HB
    cells = EDGE_BLOCK // fan_in
    loads = [
        pltpu.make_async_copy(far, near, sems.at[at])
        for at, (far, near) in enumerate(
            (
                (source_hbm, source_ref),
                (edges_hbm, edges_ref),
                (w_edge_in_hbm, w_edge_in_ref),
                (w_edge_out_hbm, w_edge_out_ref),
                (w_node_in_hbm, w_node_in_ref),
                (w_node_out_hbm, w_node_out_ref),
                (cot_nodes_hbm, cot_nodes_ref),
                (cot_edges_hbm, cot_edges_ref),
            )
        )
    ]
    for load in loads:
        load.start()
    token_ref[...] = jnp.zeros(token_ref.shape, F32)
    loads[0].wait()
    offset = scal[PART] * cell_count - HB

    def hots(step, carry):
        rows = pl.ds(pl.multiple_of(step * EDGE_BLOCK, EDGE_BLOCK), EDGE_BLOCK)
        local = source_ref[:, rows] - offset
        scatter_ref[:, rows] = hot(iota((padded, EDGE_BLOCK), 0) == local)
        local = jnp.transpose(jnp.broadcast_to(local.astype(F32), (LANES, EDGE_BLOCK)))
        local = local.astype(jnp.int32)
        lane = iota((EDGE_BLOCK, LANES), 1)
        for at in range(0, padded, LANES):
            gather_ref[rows, at : at + LANES] = hot(local == lane + at)
        gather_ref[rows, padded:] = hot(
            iota((EDGE_BLOCK, cells), 0) // fan_in == iota((EDGE_BLOCK, cells), 1)
        )
        return carry

    lax.fori_loop(0, edge_count // EDGE_BLOCK, hots, 0)
    loads[1].wait()
    loads[2].wait()

    def first(step, carry):
        rows = pl.ds(pl.multiple_of(step * EDGE_BLOCK, EDGE_BLOCK), EDGE_BLOCK)
        pre_ref[rows, :] = dot_nn(edges_ref[rows, :], w_edge_in_ref[:width, :])
        return carry

    lax.fori_loop(0, edge_count // EDGE_BLOCK, first, 0)
    for load in loads[3:]:
        load.wait()


def main_kernel(
    fan_in,
    scale,
    scal,
    nodes_ref,
    prev_ref,
    next_ref,
    edges_ref,
    cot_nodes_ref,
    cot_edges_ref,
    w_edge_in_ref,
    w_edge_out_ref,
    w_node_in_ref,
    w_node_out_ref,
    gather_ref,
    scatter_ref,
    pre_ref,
    edge_new_hbm,
    node_new_hbm,
    pre_grad_ref,
    summed_grad_ref,
    to_prev_ref,
    to_next_ref,
    node_grad_ref,
    keep_ref,
    send_ref,
    node_new_ref,
    cells_ref,
    table_ref,
    recv_ref,
    hidden_ref,
    slope_ref,
    normed_ref,
    inverse_ref,
    summed_ref,
    post_grad_ref,
    received_ref,
    out_sems,
):
    cell_count, width = nodes_ref.shape
    edge_count = edges_ref.shape[0]
    steps = edge_count // EDGE_BLOCK
    padded = cell_count + 2 * HB
    cells = EDGE_BLOCK // fan_in
    half = width // 2
    inner = slice(HB, HB + cell_count)

    cells_ref[:HB, :] = prev_ref[...]
    cells_ref[inner, :] = nodes_ref[...]
    cells_ref[HB + cell_count :, :] = next_ref[...]
    table_ref[:padded, :] = dot_nn(cells_ref[...], w_edge_in_ref[width : 2 * width, :]).astype(BF16)
    recv_ref[...] = dot_nn(nodes_ref[...], w_edge_in_ref[2 * width :, :]).astype(BF16)
    collect = hot(iota((cells, EDGE_BLOCK), 0) == iota((cells, EDGE_BLOCK), 1) // fan_in)

    def forward(step, carry):
        spot = pl.ds(pl.multiple_of(step * cells, cells), cells)
        rows = pl.ds(pl.multiple_of(step * EDGE_BLOCK, EDGE_BLOCK), EDGE_BLOCK)
        table_ref[padded : padded + cells, :] = recv_ref[spot, :]
        edges = edges_ref[rows, :]
        pre = pre_ref[rows, :] + dot_nn(gather_ref[rows, :], table_ref[...])
        gate = sigmoid(pre)
        hidden = (pre * gate).astype(BF16)
        hidden_ref[rows, :] = hidden
        slope_ref[rows, :] = (gate * (1.0 + pre * (1.0 - gate))).astype(BF16)
        normed, inverse = normalize(dot_nn(hidden, w_edge_out_ref[...]))
        normed_ref[rows, :] = normed.astype(BF16)
        inverse_ref[rows, :] = inverse
        edge_new = (edges.astype(F32) + normed).astype(BF16)
        post_grad_ref[rows, :] = edge_new
        summed_ref[spot, :] = dot_nn(collect, edge_new).astype(BF16)
        return carry

    lax.fori_loop(0, steps, forward, 0)
    edge_store = pltpu.make_async_copy(post_grad_ref, edge_new_hbm, out_sems.at[0])
    edge_store.start()
    nodes = nodes_ref[...]
    summed = summed_ref[...]
    node_pre = dot_nn(nodes, w_node_in_ref[:width, :]) + dot_nn(summed, w_node_in_ref[width:, :])
    node_gate = sigmoid(node_pre)
    node_hidden = (node_pre * node_gate).astype(BF16)
    node_normed, node_inverse = normalize(dot_nn(node_hidden, w_node_out_ref[...]))
    node_new_ref[...] = (nodes.astype(F32) + node_normed).astype(BF16)
    node_store = pltpu.make_async_copy(node_new_ref, node_new_hbm, out_sems.at[1])
    node_store.start()
    upstream = cot_nodes_ref[...].astype(F32)
    node_post_grad = normalize_back(node_normed, node_inverse, upstream).astype(BF16)
    node_slope = node_gate * (1.0 + node_pre * (1.0 - node_gate))
    node_pre_grad = (dot_nt(node_post_grad, w_node_out_ref[...]) * node_slope).astype(BF16)
    summed_grad = dot_nt(node_pre_grad, w_node_in_ref[width:, :])
    high = summed_grad.astype(BF16)
    low = (summed_grad - high.astype(F32)).astype(BF16)
    for block in range(steps):
        at = slice(block * cells, (block + 1) * cells)
        summed_grad_ref[2 * block * cells : (2 * block + 1) * cells, :] = high[at]
        summed_grad_ref[(2 * block + 1) * cells : 2 * (block + 1) * cells, :] = low[at]
    node_grad_ref[...] = upstream + dot_nt(node_pre_grad, w_node_in_ref[:width, :])
    member = iota((EDGE_BLOCK, 2 * cells), 1)
    owner = iota((EDGE_BLOCK, 2 * cells), 0) // fan_in
    spread = hot((owner == member) | (owner + cells == member))

    edge_store.wait()

    def backward(step, carry):
        spot = pl.ds(pl.multiple_of(step * cells, cells), cells)
        pair = pl.ds(pl.multiple_of(step * 2 * cells, 2 * cells), 2 * cells)
        rows = pl.ds(pl.multiple_of(step * EDGE_BLOCK, EDGE_BLOCK), EDGE_BLOCK)
        upstream = cot_edges_ref[rows, :].astype(F32) + dot_nn(spread, summed_grad_ref[pair, :])
        post_grad = normalize_back(
            normed_ref[rows, :].astype(F32), inverse_ref[rows, :], upstream
        )
        post_grad = post_grad.astype(BF16)
        post_grad_ref[rows, :] = post_grad
        pre_grad = (dot_nt(post_grad, w_edge_out_ref[...]) * slope_ref[rows, :].astype(F32)).astype(
            BF16
        )
        pre_grad_ref[rows, :] = pre_grad
        received_ref[spot, :] = dot_nn(collect, pre_grad).astype(BF16)
        return carry

    lax.fori_loop(0, steps, backward, 0)
    first = scal[CORE] == 0

    def put(place_at, value):
        value = (value * scale).astype(BF16)
        rows = slice(place_at * width, (place_at + 1) * width)
        left = value[:, :half]
        right = value[:, half:]
        keep_ref[rows, :] = jnp.where(first, left, right)
        send_ref[rows, :] = jnp.where(first, right, left)

    sent = dot_nn(scatter_ref[...], pre_grad_ref[...]).astype(BF16)
    sender = dot_nt(sent, w_edge_in_ref[width : 2 * width, :])
    to_prev_ref[...] = sender[:HB].astype(BF16)
    to_next_ref[...] = sender[HB + cell_count :].astype(BF16)
    node_grad_ref[...] = (
        node_grad_ref[...]
        + dot_nt(received_ref[...], w_edge_in_ref[2 * width :, :])
        + sender[inner]
    )
    put(0, dot_tn(edges_ref[...], pre_grad_ref[...]))
    put(1, dot_tn(cells_ref[...], sent))
    put(2, dot_tn(nodes, received_ref[...]))
    put(3, dot_tn(hidden_ref[...], post_grad_ref[...]))
    put(4, dot_tn(nodes, node_pre_grad))
    put(5, dot_tn(summed, node_pre_grad))
    put(6, dot_tn(node_hidden, node_post_grad))
    node_store.wait()


def edge_kernel(
    fan_in,
    cot_ref,
    summed_grad_ref,
    pre_grad_ref,
    w_edge_in_ref,
    _,
    grad_edge_hbm,
    token_ref,
    grad_edge_ref,
    sems,
):
    edge_count, width = cot_ref.shape
    steps = edge_count // EDGE_BLOCK
    cells = EDGE_BLOCK // fan_in
    member = iota((EDGE_BLOCK, 2 * cells), 1)
    owner = iota((EDGE_BLOCK, 2 * cells), 0) // fan_in
    spread = hot((owner == member) | (owner + cells == member))
    stores = []
    for step in range(steps):
        rows = slice(step * EDGE_BLOCK, (step + 1) * EDGE_BLOCK)
        pair = slice(step * 2 * cells, (step + 1) * 2 * cells)
        upstream = cot_ref[rows, :].astype(F32) + dot_nn(spread, summed_grad_ref[pair, :])
        grad_edge_ref[rows, :] = (
            upstream + dot_nt(pre_grad_ref[rows, :], w_edge_in_ref[:width, :])
        ).astype(BF16)
        stores.append(
            pltpu.make_async_copy(
                grad_edge_ref.at[rows, :], grad_edge_hbm.at[rows, :], sems.at[step]
            )
        )
        stores[-1].start()
    token_ref[...] = jnp.zeros(token_ref.shape, F32)
    for store in stores:
        store.wait()


def return_kernel(
    part_count, capacity, scal, node_grad_ref, from_prev_ref, from_next_ref, ids_ref, out_ref, token_ref
):
    cell_count, width = node_grad_ref.shape
    chunks = width // LANES
    block_rows = chunks * capacity
    token_ref[...] = jnp.zeros(token_ref.shape, F32)
    first = node_grad_ref[:HB, :] + from_prev_ref[...].astype(F32)
    last = node_grad_ref[cell_count - HB :, :] + from_next_ref[...].astype(F32)
    grad = jnp.concatenate(
        [first, node_grad_ref[HB : cell_count - HB, :], last], axis=0
    ).astype(BF16)
    for step in range(part_count):
        pick = place(ids_ref[step * 16 : (step + 1) * 16, :], cell_count)
        rows = dot_tn(pick, grad).astype(BF16)
        owner = scal[PART] - step
        owner = jnp.where(owner < 0, owner + part_count, owner)
        for chunk in range(chunks):
            start = pl.multiple_of(owner * block_rows + chunk * capacity, 16)
            out_ref[pl.ds(start, capacity), :] = rows[
                :capacity, chunk * LANES : (chunk + 1) * LANES
            ]


def finish_kernel(
    part_count, capacity, scal, index_ref, block_ref, out_ref, token_ref, rows_ref, pick_ref
):
    cell_count, width = out_ref.shape
    chunks = width // LANES
    block_rows = chunks * capacity
    token_ref[...] = jnp.zeros(token_ref.shape, F32)
    slot, _ = slots_of(index_ref[...], scal[PART], part_count, cell_count)
    for step in range(part_count):
        base = step * LANES
        pick_ref[base : base + LANES, :] = hot(iota((LANES, cell_count), 0) + base == slot)
        owner = scal[PART] + step
        owner = jnp.where(owner >= part_count, owner - part_count, owner)
        for chunk in range(chunks):
            start = pl.multiple_of(owner * block_rows + chunk * capacity, 16)
            rows_ref[base : base + capacity, chunk * LANES : (chunk + 1) * LANES] = block_ref[
                pl.ds(start, capacity), :
            ]
        if capacity < LANES:
            rows_ref[base + capacity : base + LANES, :] = jnp.zeros(
                (LANES - capacity, width), BF16
            )
    out_ref[...] = dot_tn(pick_ref[...], rows_ref[...]).astype(BF16)


def shape(dims, kind=BF16):
    return jax.ShapeDtypeStruct(dims, kind)


def whole(count):
    return [pl.BlockSpec(memory_space=VMEM)] * count


def scalars():
    return pl.BlockSpec(memory_space=SMEM)


def params(limit):
    return pltpu.CompilerParams(vmem_limit_bytes=limit * MIB)


def cost(flops, bytes_accessed):
    return pl.CostEstimate(flops=flops, bytes_accessed=bytes_accessed, transcendentals=0)


def full(dims):
    return pl.BlockSpec(dims, lambda step: (0,) * len(dims))


def rows_spec(rows, columns):
    return pl.BlockSpec((rows, columns), lambda step: (step, 0))


def swap(value, axis, bit):
    count = lax.axis_size(axis)
    return lax.ppermute(value, axis, [(at, at ^ bit) for at in range(count)])


def take(value, kind, bit):
    if kind == "columns":
        half = value.shape[2] // 2
        parts = value[:, :, :half], value[:, :, half:]
    else:
        pairs = value.reshape((value.shape[0] // 2, 2) + value.shape[1:])
        parts = pairs[:, 0], pairs[:, 1]
    return jnp.where(bit == 0, parts[0], parts[1])


def core_kernel(kinds, bits, scal, keep_ref, got_ref, *refs):
    total_ref, left_ref, right_ref = refs[-3:]
    total = (keep_ref[...].astype(F32) + got_ref[...].astype(F32)).astype(BF16)
    total = total.reshape(total_ref.shape)
    total_ref[...] = total
    half = total.shape[1] // 2
    left_ref[...] = take(total[:, :half], kinds[0], 1 - scal[bits[0]])
    right_ref[...] = take(total[:, half:], kinds[1], 1 - scal[bits[1]])


def stage_kernel(part, kinds, bits, scal, value_ref, got_ref, *refs):
    total_ref, send_ref = refs[-2:]
    value = value_ref[...]
    if part is not None:
        half = value.shape[1] // 2
        value = value[:, part * half : (part + 1) * half]
    mine = take(value, kinds[0], scal[bits[0]]).astype(F32)
    total = (mine + got_ref[...].astype(F32)).astype(BF16)
    total_ref[...] = total
    send_ref[...] = take(total, kinds[1], 1 - scal[bits[1]])


def split_kernel(kinds, bits, scal, *refs):
    left_ref, left_got_ref, right_ref, right_got_ref = refs[:4]
    outs = refs[-(left_got_ref.shape[0]) :]
    left = take(left_ref[...], kinds[0], scal[bits[0]]).astype(F32)
    left = (left + left_got_ref[...].astype(F32)).astype(BF16)
    right = take(right_ref[...], kinds[1], scal[bits[1]]).astype(F32)
    right = (right + right_got_ref[...].astype(F32)).astype(BF16)
    half = left.shape[1]
    owner = scal[OWNER]
    for other, out in enumerate(outs):
        for at in range(len(outs)):

            @pl.when((owner ^ other) == at)
            def _(out=out, at=at):
                out[:half, :] = left[at]
                out[half:, :] = right[at]


def sum_kernel(*refs):
    total = refs[0][...].astype(F32)
    for ref in refs[1:-2]:
        total = total + ref[...].astype(F32)
    refs[-1][...] = total.astype(BF16)


def join_kernel(at, scal, mine_ref, theirs_ref, out_ref):
    mine = mine_ref[...]
    theirs = theirs_ref[...]
    columns = mine.shape[1]
    first = scal[at] == 0
    out_ref[:, :columns] = jnp.where(first, mine, theirs).astype(out_ref.dtype)
    out_ref[:, columns:] = jnp.where(first, theirs, mine).astype(out_ref.dtype)


def local_call(kernel, outs, name, *operands):
    return pl.pallas_call(
        kernel,
        out_shape=[near_shape(*out) for out in outs],
        in_specs=[scalars()] + whole(len(operands) - 1),
        out_specs=whole(len(outs)),
        compiler_params=params(24),
        name=name,
    )(*operands)


def halved(dims, kind):
    if kind == "columns":
        return (dims[0], dims[1], dims[2] // 2)
    return (dims[0] // 2,) + dims[1:]


def reduce_weights(scal, keep, got, geom_count, part_count, early, late):
    bits = []
    bit = 2
    while bit < geom_count:
        bits.append(bit)
        bit *= 2
    columns = [("columns", "geom", bit, GEOM_BITS + at) for at, bit in enumerate(bits)]
    owner = ("owners", "dom", 1, DOM_BIT)
    left = columns + [owner]
    right = [owner] + columns
    rows, width = keep.shape
    dims = (part_count, rows // part_count, width)
    piece = (part_count, rows // part_count // 2, width)
    total, send_left, send_right = local_call(
        functools.partial(core_kernel, (left[0][0], right[0][0]), (left[0][3], right[0][3])),
        [(dims,), (halved(piece, left[0][0]),), (halved(piece, right[0][0]),)],
        "core",
        scal,
        keep,
        got,
    )
    ends = []
    for part, chain, send in ((0, left, send_left), (1, right, send_right)):
        value = total
        now = piece
        for at in range(len(chain) - 1):
            kind, axis, bit, place_at = chain[at]
            follow = chain[at + 1]
            now = halved(now, kind)
            value, send = local_call(
                functools.partial(
                    stage_kernel,
                    part if at == 0 else None,
                    (kind, follow[0]),
                    (place_at, follow[3]),
                ),
                [(now,), (halved(now, follow[0]),)],
                "stage",
                scal,
                value,
                swap(send, axis, bit),
                *early,
            )
        if len(chain) == 1:
            half = rows // part_count // 2
            value = value[:, part * half : (part + 1) * half]
        ends.append((value, swap(send, chain[-1][1], chain[-1][2])))
        end = halved(now, chain[-1][0])
    out = (2 * end[1], end[2])
    owners = part_count // 2
    pieces = local_call(
        functools.partial(split_kernel, (left[-1][0], right[-1][0]), (left[-1][3], right[-1][3])),
        [(out,)] * owners,
        "split",
        scal,
        *ends[0],
        *ends[1],
    )
    got = [swap(pieces[other], "dom", 2 * other) for other in range(owners - 1, 0, -1)]
    total = pl.pallas_call(
        sum_kernel,
        out_shape=near_shape(out),
        in_specs=whole(owners + 1),
        out_specs=pl.BlockSpec(memory_space=VMEM),
        compiler_params=params(24),
        name="sum",
    )(pieces[0], *got, late)
    for place_at, bit in [(GEOM_BITS + at, bit) for at, bit in enumerate(bits)][::-1] + [
        (CORE, 1)
    ]:
        out = (out[0], 2 * out[1])
        last = bit == 1
        total = pl.pallas_call(
            functools.partial(join_kernel, place_at),
            out_shape=shape(out, F32) if last else near_shape(out),
            in_specs=[scalars()] + whole(2),
            out_specs=pl.BlockSpec(memory_space=VMEM),
            compiler_params=params(24),
            name="join",
        )(scal, total, swap(total, "geom", bit))
    return total


def shift(value, steps):
    count = lax.axis_size("dom")
    return lax.ppermute(value, "dom", [(at, (at + steps) % count) for at in range(count)])


def neighbour(value, step):
    count = lax.axis_size("dom")
    return lax.ppermute(
        value, "dom", [(at, at + step) for at in range(count) if 0 <= at + step < count]
    )


def send_order(part_count):
    return sorted(range(1, part_count), key=lambda at: (-min(at, part_count - at), at))


def near_shape(dims, kind=BF16):
    return pltpu.VMEM(dims, kind)


def run_prep(
    fan_in,
    cell_count,
    scal,
    source,
    edges,
    cot_nodes,
    cot_edges,
    w_edge_in,
    w_edge_out,
    w_node_in,
    w_node_out,
    token,
):
    edge_count = edges.shape[0]
    padded = cell_count + 2 * HB
    cells = EDGE_BLOCK // fan_in
    near = pl.BlockSpec(memory_space=VMEM)
    return pl.pallas_call(
        functools.partial(prep_kernel, fan_in, cell_count),
        out_shape=[
            near_shape(like.shape)
            for like in (edges, cot_nodes, cot_edges, w_edge_in, w_edge_out, w_node_in, w_node_out)
        ]
        + [
            near_shape((edge_count, padded + cells)),
            near_shape((padded, edge_count)),
            near_shape(edges.shape, F32),
            near_shape((8, LANES), F32),
        ],
        in_specs=[scalars()] + [pl.BlockSpec(memory_space=pltpu.HBM)] * 8 + [near],
        out_specs=[near] * 11,
        scratch_shapes=[VMEM(source.shape, jnp.int32), pltpu.SemaphoreType.DMA((8,))],
        compiler_params=params(PREP_LIMIT),
        cost_estimate=cost(4 * edge_count * edges.shape[1] ** 2, 20 * MIB),
        name="prep",
    )(
        scal,
        *[
            pltpu.with_memory_space_constraint(value, pltpu.HBM)
            for value in (
                source,
                edges,
                cot_nodes,
                cot_edges,
                w_edge_in,
                w_edge_out,
                w_node_in,
                w_node_out,
            )
        ],
        token,
    )


def run_main(fan_in, scale, scal, nodes, before, after, prepared):
    edge_count, width = prepared[0].shape
    cell_count = nodes.shape[0]
    cells = EDGE_BLOCK // fan_in
    padded = cell_count + 2 * HB
    far = pl.BlockSpec(memory_space=pltpu.HBM)
    near = pl.BlockSpec(memory_space=VMEM)
    by_edge = (edge_count, width)
    by_cell = (cell_count, width)
    weights = (7 * width, width // 2)
    return pl.pallas_call(
        functools.partial(main_kernel, fan_in, scale),
        out_shape=[
            shape(by_edge),
            shape(by_cell),
            near_shape(by_edge),
            near_shape((2 * cell_count, width)),
            near_shape((HB, width)),
            near_shape((HB, width)),
            near_shape(by_cell, F32),
            near_shape(weights),
            near_shape(weights),
        ],
        in_specs=[scalars()] + [near] * 13,
        out_specs=[far, far] + [near] * 7,
        scratch_shapes=[
            VMEM(by_cell, BF16),
            VMEM((padded, width), BF16),
            VMEM((padded + cells, width), BF16),
            VMEM(by_cell, BF16),
            VMEM(by_edge, BF16),
            VMEM(by_edge, BF16),
            VMEM(by_edge, BF16),
            VMEM((edge_count, 1), F32),
            VMEM(by_cell, BF16),
            VMEM(by_edge, BF16),
            VMEM(by_cell, BF16),
            pltpu.SemaphoreType.DMA((2,)),
        ],
        compiler_params=params(MAIN_LIMIT),
        cost_estimate=cost(28 * edge_count * width * width, 16 * MIB),
        name="main",
    )(scal, nodes, before, after, *prepared)


def run_edges(fan_in, cot, summed_grad, pre_grad, w_edge_in, token):
    edge_count, width = cot.shape
    steps = edge_count // EDGE_BLOCK
    return pl.pallas_call(
        functools.partial(edge_kernel, fan_in),
        out_shape=[shape((edge_count, width)), near_shape((8, LANES), F32)],
        in_specs=whole(5),
        out_specs=[pl.BlockSpec(memory_space=pltpu.HBM), pl.BlockSpec(memory_space=VMEM)],
        scratch_shapes=[VMEM((edge_count, width), BF16), pltpu.SemaphoreType.DMA((steps,))],
        compiler_params=params(24),
        cost_estimate=cost(4 * edge_count * width * width, 7 * MIB),
        name="edges",
    )(cot, summed_grad, pre_grad, w_edge_in, token)


def local(
    h_in,
    edge_in,
    new_index,
    source,
    w_edge_in,
    w_edge_out,
    w_node_in,
    w_node_out,
    cot_nodes,
    cot_edges,
):
    _, cell_count, width = h_in.shape
    edge_count = source.shape[1]
    fan_in = edge_count // cell_count
    part_count = lax.axis_size("dom")
    geom_count = lax.axis_size("geom")
    capacity = cell_count // part_count + cell_count // part_count // 2
    chunks = width // LANES
    block_rows = chunks * capacity
    scale = 1.0 / math.sqrt(geom_count * part_count * cell_count * fan_in)
    part = lax.axis_index("dom")
    geom = lax.axis_index("geom")
    scal = [part, geom % 2, part % 2, part // 2]
    geom = geom // 2
    for _ in range(1, geom_count.bit_length() - 1):
        scal.append(geom % 2)
        geom = geom // 2
    scal = jnp.stack(scal).astype(jnp.int32)
    edges = edge_in[0]
    cot = cot_edges[0]

    sends = pl.pallas_call(
        functools.partial(pack_kernel, part_count, capacity),
        out_shape=[shape((block_rows + 16, LANES))] * part_count + [near_shape((8, LANES), F32)],
        in_specs=[scalars()] + whole(2),
        out_specs=whole(part_count + 1),
        compiler_params=params(24),
        name="pack",
    )(scal, h_in[0], new_index)
    prepared = run_prep(
        fan_in,
        cell_count,
        scal,
        source,
        edges,
        cot_nodes[0],
        cot,
        w_edge_in,
        w_edge_out,
        w_node_in,
        w_node_out,
        sends[part_count],
    )
    got = {0: sends[0]}
    for step in send_order(part_count):
        got[step] = shift(sends[step], step)
    nodes, head, tail, ids = pl.pallas_call(
        functools.partial(unpack_kernel, part_count, capacity),
        out_shape=[
            shape((cell_count, width)),
            shape((HB, width)),
            shape((HB, width)),
            shape((part_count * 16, LANES)),
        ],
        in_specs=whole(part_count + 1),
        out_specs=whole(4),
        scratch_shapes=[
            VMEM((part_count * LANES, width), BF16),
            VMEM((cell_count, part_count * LANES), BF16),
        ],
        compiler_params=params(24),
        name="unpack",
    )(*[got[step] for step in range(part_count)], prepared[-1])
    before = neighbour(tail, 1)
    after = neighbour(head, -1)

    (
        edge_new,
        node_new,
        pre_grad,
        summed_grad,
        to_prev,
        to_next,
        node_grad,
        keep,
        send,
    ) = run_main(fan_in, scale, scal, nodes, before, after, prepared[:-1])
    from_next = neighbour(to_prev, -1)
    from_prev = neighbour(to_next, 1)

    returning, token = pl.pallas_call(
        functools.partial(return_kernel, part_count, capacity),
        out_shape=[near_shape((part_count * block_rows, LANES)), near_shape((8, LANES), F32)],
        in_specs=[scalars()] + whole(4),
        out_specs=whole(2),
        compiler_params=params(24),
        name="returning",
    )(scal, node_grad, from_prev, from_next, ids)
    back = lax.all_to_all(
        returning.reshape(part_count, block_rows, LANES), "dom", 0, 0, tiled=True
    ).reshape(part_count * block_rows, LANES)
    grad_edge, edge_token = run_edges(
        fan_in, prepared[2], summed_grad, pre_grad, prepared[3], token
    )
    grad_in, late = pl.pallas_call(
        functools.partial(finish_kernel, part_count, capacity),
        out_shape=[shape((cell_count, width)), near_shape((8, LANES), F32)],
        in_specs=[scalars()] + whole(2),
        out_specs=whole(2),
        scratch_shapes=[
            VMEM((part_count * LANES, width), BF16),
            VMEM((part_count * LANES, cell_count), BF16),
        ],
        compiler_params=params(24),
        name="finish",
    )(scal, new_index, back)
    weight_grads = reduce_weights(
        scal, keep, swap(send, "geom", 1), geom_count, part_count, (token, edge_token), late
    )
    return (node_new[None], edge_new[None], grad_in[None], grad_edge[None], weight_grads)


def solution(mesh):
    return jax.shard_map(
        local,
        mesh=mesh,
        in_specs=(
            P("geom", "dom", None),
            P("geom", "dom", None),
            P("geom", "dom"),
            P("geom", "dom"),
            P(),
            P(),
            P(),
            P(),
            P("geom", "dom", None),
            P("geom", "dom", None),
        ),
        out_specs=(
            P("geom", "dom", None),
            P("geom", "dom", None),
            P("geom", "dom", None),
            P("geom", "dom", None),
            P("dom", None),
        ),
        check_vma=False,
    )
```

```python
import functools
import math

import jax
import jax.numpy as jnp
from jax import lax
from jax.experimental import pallas as pl
from jax.experimental.pallas import tpu as pltpu
from jax.sharding import PartitionSpec as P

HB = 64
LANES = 128
EDGE_BLOCK = 512
MIB = 1024 * 1024
MAIN_LIMIT = 25
FIRST, SECOND = 3, 7
PREP_LIMIT = 20
PART, CORE, DOM_BIT, OWNER, GEOM_BITS = range(5)
F32 = jnp.float32
BF16 = jnp.bfloat16
VMEM = pltpu.VMEM
SMEM = pltpu.SMEM


def dot_nn(left, right):
    return lax.dot_general(left, right, (((1,), (0,)), ((), ())), preferred_element_type=F32)


def dot_nt(left, right):
    return lax.dot_general(left, right, (((1,), (1,)), ((), ())), preferred_element_type=F32)


def dot_tn(left, right):
    return lax.dot_general(left, right, (((0,), (0,)), ((), ())), preferred_element_type=F32)


def iota(shape, axis):
    return lax.broadcasted_iota(jnp.int32, shape, axis)


def hot(condition):
    return jnp.where(condition, 1.0, 0.0).astype(BF16)


def sigmoid(values):
    return 0.5 * jnp.tanh(0.5 * values) + 0.5


def normalize(values):
    center = values - jnp.mean(values, axis=-1, keepdims=True)
    inverse = lax.rsqrt(jnp.mean(center * center, axis=-1, keepdims=True) + 1e-05)
    return center * inverse, inverse


def normalize_back(normed, inverse, upstream):
    return inverse * (
        upstream
        - jnp.mean(upstream, axis=-1, keepdims=True)
        - normed * jnp.mean(upstream * normed, axis=-1, keepdims=True)
    )


def slots_of(index, me, part_count, cell_count):
    owner = jnp.zeros_like(index)
    for part in range(1, part_count):
        owner = owner + jnp.where(index >= part * cell_count, 1, 0)
    row = index - owner * cell_count
    ahead = owner - me
    ahead = jnp.where(ahead < 0, ahead + part_count, ahead)
    high = -(-part_count // 16) * 16
    member = hot(iota((high, cell_count), 0) == ahead)
    before = hot(iota((cell_count, cell_count), 0) < iota((cell_count, cell_count), 1))
    rank = jnp.sum(member.astype(F32) * dot_nn(member, before), axis=0, keepdims=True)
    return ahead * LANES + rank.astype(jnp.int32), row


def pack_kernel(part_count, capacity, scal, h_ref, index_ref, *outs):
    cell_count, width = h_ref.shape
    chunks = width // LANES
    slot, row = slots_of(index_ref[...], scal[PART], part_count, cell_count)
    kind = iota((16, cell_count), 0)
    coded = jnp.where(
        kind == 0, row >> 8, jnp.where(kind == 1, row & 255, jnp.where(kind == 2, 1, 0))
    )
    coded = coded.astype(F32).astype(BF16)
    cells = h_ref[...]
    for step in range(part_count):
        pick = hot(iota((LANES, cell_count), 0) + step * LANES == slot)
        rows = dot_nn(pick, cells).astype(BF16)
        for chunk in range(chunks):
            outs[step][chunk * capacity : (chunk + 1) * capacity, :] = rows[
                :capacity, chunk * LANES : (chunk + 1) * LANES
            ]
        outs[step][chunks * capacity :, :] = dot_nt(coded, pick).astype(BF16)
    outs[part_count][...] = jnp.zeros(outs[part_count].shape, F32)


def place(ids, cell_count):
    ids = ids.astype(F32)
    spot = ids[0:1] * 256.0 + ids[1:2] + (ids[2:3] - 1.0) * 65536.0
    return hot(iota((cell_count, LANES), 0) == spot.astype(jnp.int32))


def unpack_kernel(part_count, capacity, *refs):
    blocks = refs[:part_count]
    scal, _, nodes_ref, low_ref, high_ref, ids_ref, rows_ref, hot_ref = refs[part_count:]
    cell_count, width = nodes_ref.shape
    chunks = width // LANES
    for step in range(part_count):
        base = step * LANES
        ids = blocks[step][chunks * capacity :, :]
        ids_ref[step * 16 : (step + 1) * 16, :] = ids
        hot_ref[:, base : base + LANES] = place(ids, cell_count)
        for chunk in range(chunks):
            rows_ref[base : base + capacity, chunk * LANES : (chunk + 1) * LANES] = blocks[step][
                chunk * capacity : (chunk + 1) * capacity, :
            ]
        if capacity < LANES:
            rows_ref[base + capacity : base + LANES, :] = jnp.zeros(
                (LANES - capacity, width), BF16
            )
    nodes = dot_nn(hot_ref[...], rows_ref[...]).astype(BF16)
    nodes_ref[...] = nodes
    odd = scal[DOM_BIT] == 1
    head = nodes[:HB]
    tail = nodes[cell_count - HB :]
    low_ref[...] = jnp.where(odd, head, tail)
    high_ref[...] = jnp.where(odd, tail, head)


def prep_kernel(
    fan_in,
    cell_count,
    scal,
    source_hbm,
    edges_hbm,
    cot_nodes_hbm,
    cot_edges_hbm,
    w_edge_in_hbm,
    w_edge_out_hbm,
    w_node_in_hbm,
    w_node_out_hbm,
    _,
    edges_ref,
    cot_nodes_ref,
    cot_edges_ref,
    w_edge_in_ref,
    w_edge_out_ref,
    w_node_in_ref,
    w_node_out_ref,
    gather_ref,
    scatter_ref,
    pre_ref,
    token_ref,
    source_ref,
    sems,
):
    edge_count, width = edges_ref.shape
    padded = cell_count + 2 * HB
    cells = EDGE_BLOCK // fan_in
    loads = [
        pltpu.make_async_copy(far, near, sems.at[at])
        for at, (far, near) in enumerate(
            (
                (source_hbm, source_ref),
                (edges_hbm, edges_ref),
                (w_edge_in_hbm, w_edge_in_ref),
                (w_edge_out_hbm, w_edge_out_ref),
                (w_node_in_hbm, w_node_in_ref),
                (w_node_out_hbm, w_node_out_ref),
                (cot_nodes_hbm, cot_nodes_ref),
                (cot_edges_hbm, cot_edges_ref),
            )
        )
    ]
    for load in loads:
        load.start()
    token_ref[...] = jnp.zeros(token_ref.shape, F32)
    loads[0].wait()
    offset = scal[PART] * cell_count - HB

    def hots(step, carry):
        rows = pl.ds(pl.multiple_of(step * EDGE_BLOCK, EDGE_BLOCK), EDGE_BLOCK)
        local = source_ref[:, rows] - offset
        scatter_ref[:, rows] = hot(iota((padded, EDGE_BLOCK), 0) == local)
        local = jnp.transpose(jnp.broadcast_to(local.astype(F32), (LANES, EDGE_BLOCK)))
        local = local.astype(jnp.int32)
        lane = iota((EDGE_BLOCK, LANES), 1)
        for at in range(0, padded, LANES):
            gather_ref[rows, at : at + LANES] = hot(local == lane + at)
        gather_ref[rows, padded:] = hot(
            iota((EDGE_BLOCK, cells), 0) // fan_in == iota((EDGE_BLOCK, cells), 1)
        )
        return carry

    lax.fori_loop(0, edge_count // EDGE_BLOCK, hots, 0)
    loads[1].wait()
    loads[2].wait()

    def first(step, carry):
        rows = pl.ds(pl.multiple_of(step * EDGE_BLOCK, EDGE_BLOCK), EDGE_BLOCK)
        pre_ref[rows, :] = dot_nn(edges_ref[rows, :], w_edge_in_ref[:width, :])
        return carry

    lax.fori_loop(0, edge_count // EDGE_BLOCK, first, 0)
    for load in loads[3:]:
        load.wait()


def main_kernel(
    fan_in,
    scale,
    scal,
    nodes_ref,
    low_ref,
    high_ref,
    edges_ref,
    cot_nodes_ref,
    cot_edges_ref,
    w_edge_in_ref,
    w_edge_out_ref,
    w_node_in_ref,
    w_node_out_ref,
    gather_ref,
    scatter_ref,
    pre_ref,
    edge_new_hbm,
    node_new_hbm,
    pre_grad_hbm,
    summed_grad_hbm,
    sent_ref,
    received_ref,
    base_ref,
    keep_ref,
    send_ref,
    pre_grad_ref,
    summed_grad_ref,
    node_new_ref,
    cells_ref,
    table_ref,
    recv_ref,
    hidden_ref,
    slope_ref,
    normed_ref,
    inverse_ref,
    summed_ref,
    post_grad_ref,
    out_sems,
):
    cell_count, width = nodes_ref.shape
    edge_count = edges_ref.shape[0]
    steps = edge_count // EDGE_BLOCK
    padded = cell_count + 2 * HB
    cells = EDGE_BLOCK // fan_in
    half = width // 2
    inner = slice(HB, HB + cell_count)

    odd = scal[DOM_BIT] == 1
    low = low_ref[...]
    high = high_ref[...]
    cells_ref[:HB, :] = jnp.where(odd, low, high)
    cells_ref[inner, :] = nodes_ref[...]
    cells_ref[HB + cell_count :, :] = jnp.where(odd, high, low)
    table_ref[:padded, :] = dot_nn(cells_ref[...], w_edge_in_ref[width : 2 * width, :]).astype(BF16)
    recv_ref[...] = dot_nn(nodes_ref[...], w_edge_in_ref[2 * width :, :]).astype(BF16)
    collect = hot(iota((cells, EDGE_BLOCK), 0) == iota((cells, EDGE_BLOCK), 1) // fan_in)

    def forward(step, carry):
        spot = pl.ds(pl.multiple_of(step * cells, cells), cells)
        rows = pl.ds(pl.multiple_of(step * EDGE_BLOCK, EDGE_BLOCK), EDGE_BLOCK)
        table_ref[padded : padded + cells, :] = recv_ref[spot, :]
        edges = edges_ref[rows, :]
        pre = pre_ref[rows, :] + dot_nn(gather_ref[rows, :], table_ref[...])
        gate = sigmoid(pre)
        hidden = (pre * gate).astype(BF16)
        hidden_ref[rows, :] = hidden
        slope_ref[rows, :] = (gate * (1.0 + pre * (1.0 - gate))).astype(BF16)
        normed, inverse = normalize(dot_nn(hidden, w_edge_out_ref[...]))
        normed_ref[rows, :] = normed.astype(BF16)
        inverse_ref[rows, :] = inverse
        edge_new = (edges.astype(F32) + normed).astype(BF16)
        post_grad_ref[rows, :] = edge_new
        summed_ref[spot, :] = dot_nn(collect, edge_new).astype(BF16)
        return carry

    lax.fori_loop(0, steps, forward, 0, unroll=True)
    edge_store = pltpu.make_async_copy(post_grad_ref, edge_new_hbm, out_sems.at[0])
    edge_store.start()
    nodes = nodes_ref[...]
    summed = summed_ref[...]
    node_pre = dot_nn(nodes, w_node_in_ref[:width, :]) + dot_nn(summed, w_node_in_ref[width:, :])
    node_gate = sigmoid(node_pre)
    node_hidden = (node_pre * node_gate).astype(BF16)
    node_normed, node_inverse = normalize(dot_nn(node_hidden, w_node_out_ref[...]))
    node_new_ref[...] = (nodes.astype(F32) + node_normed).astype(BF16)
    node_store = pltpu.make_async_copy(node_new_ref, node_new_hbm, out_sems.at[1])
    node_store.start()
    upstream = cot_nodes_ref[...].astype(F32)
    node_post_grad = normalize_back(node_normed, node_inverse, upstream).astype(BF16)
    node_slope = node_gate * (1.0 + node_pre * (1.0 - node_gate))
    node_pre_grad = (dot_nt(node_post_grad, w_node_out_ref[...]) * node_slope).astype(BF16)
    summed_grad = dot_nt(node_pre_grad, w_node_in_ref[width:, :])
    high = summed_grad.astype(BF16)
    low = (summed_grad - high.astype(F32)).astype(BF16)
    for block in range(steps):
        at = slice(block * cells, (block + 1) * cells)
        summed_grad_ref[2 * block * cells : (2 * block + 1) * cells, :] = high[at]
        summed_grad_ref[(2 * block + 1) * cells : 2 * (block + 1) * cells, :] = low[at]
    summed_store = pltpu.make_async_copy(summed_grad_ref, summed_grad_hbm, out_sems.at[2])
    summed_store.start()
    base_ref[...] = upstream + dot_nt(node_pre_grad, w_node_in_ref[:width, :])
    member = iota((EDGE_BLOCK, 2 * cells), 1)
    owner = iota((EDGE_BLOCK, 2 * cells), 0) // fan_in
    spread = hot((owner == member) | (owner + cells == member))

    edge_store.wait()

    def backward(step, carry):
        spot = pl.ds(pl.multiple_of(step * cells, cells), cells)
        pair = pl.ds(pl.multiple_of(step * 2 * cells, 2 * cells), 2 * cells)
        rows = pl.ds(pl.multiple_of(step * EDGE_BLOCK, EDGE_BLOCK), EDGE_BLOCK)
        upstream = cot_edges_ref[rows, :].astype(F32) + dot_nn(spread, summed_grad_ref[pair, :])
        post_grad = normalize_back(
            normed_ref[rows, :].astype(F32), inverse_ref[rows, :], upstream
        )
        post_grad = post_grad.astype(BF16)
        post_grad_ref[rows, :] = post_grad
        pre_grad = (dot_nt(post_grad, w_edge_out_ref[...]) * slope_ref[rows, :].astype(F32)).astype(
            BF16
        )
        pre_grad_ref[rows, :] = pre_grad
        received_ref[spot, :] = dot_nn(collect, pre_grad).astype(BF16)
        return carry

    lax.fori_loop(0, steps, backward, 0, unroll=True)
    pre_store = pltpu.make_async_copy(pre_grad_ref, pre_grad_hbm, out_sems.at[3])
    pre_store.start()
    first = scal[CORE] == 0

    def put(place_at, value):
        value = (value * scale).astype(BF16)
        rows = slice(place_at * width, (place_at + 1) * width)
        left = value[:, :half]
        right = value[:, half:]
        keep_ref[rows, :] = jnp.where(first, left, right)
        send_ref[rows, :] = jnp.where(first, right, left)

    sent = dot_nn(scatter_ref[...], pre_grad_ref[...]).astype(BF16)
    sent_ref[...] = sent
    put(0, dot_tn(edges_ref[...], pre_grad_ref[...]))
    put(1, dot_tn(cells_ref[...], sent))
    put(2, dot_tn(nodes, received_ref[...]))
    put(3, dot_tn(hidden_ref[...], post_grad_ref[...]))
    put(4, dot_tn(nodes, node_pre_grad))
    put(5, dot_tn(summed, node_pre_grad))
    put(6, dot_tn(node_hidden, node_post_grad))
    node_store.wait()
    summed_store.wait()
    pre_store.wait()


def cell_kernel(
    scal,
    sent_ref,
    received_ref,
    base_ref,
    w_edge_in_ref,
    low_ref,
    high_ref,
    node_grad_ref,
    rim_ref,
):
    cell_count, width = received_ref.shape
    sender = dot_nt(sent_ref[...], w_edge_in_ref[width : 2 * width, :])
    odd = scal[DOM_BIT] == 1
    to_prev = sender[:HB].astype(BF16)
    to_next = sender[HB + cell_count :].astype(BF16)
    low_ref[...] = jnp.where(odd, to_prev, to_next)
    high_ref[...] = jnp.where(odd, to_next, to_prev)
    node_grad = (
        base_ref[...]
        + dot_nt(received_ref[...], w_edge_in_ref[2 * width :, :])
        + sender[HB : HB + cell_count]
    )
    node_grad_ref[...] = node_grad.astype(BF16)
    rim_ref[:HB, :] = node_grad[:HB]
    rim_ref[HB:, :] = node_grad[cell_count - HB :]


def edge_kernel(
    fan_in,
    cot_hbm,
    summed_grad_hbm,
    pre_grad_hbm,
    w_edge_in_hbm,
    _,
    grad_edge_hbm,
    token_ref,
    cot_ref,
    summed_grad_ref,
    pre_grad_ref,
    w_edge_ref,
    grad_edge_ref,
    in_sems,
    out_sems,
):
    edge_count, width = cot_ref.shape
    steps = edge_count // EDGE_BLOCK
    cells = EDGE_BLOCK // fan_in
    loads = [
        pltpu.make_async_copy(w_edge_in_hbm.at[:width, :], w_edge_ref, in_sems.at[0]),
        pltpu.make_async_copy(summed_grad_hbm, summed_grad_ref, in_sems.at[1]),
    ]
    for step in range(steps):
        rows = slice(step * EDGE_BLOCK, (step + 1) * EDGE_BLOCK)
        for at, (far, near) in enumerate(((cot_hbm, cot_ref), (pre_grad_hbm, pre_grad_ref))):
            loads.append(
                pltpu.make_async_copy(
                    far.at[rows, :], near.at[rows, :], in_sems.at[2 + 2 * step + at]
                )
            )
    for load in loads:
        load.start()
    token_ref[...] = jnp.zeros(token_ref.shape, F32)
    member = iota((EDGE_BLOCK, 2 * cells), 1)
    owner = iota((EDGE_BLOCK, 2 * cells), 0) // fan_in
    spread = hot((owner == member) | (owner + cells == member))
    loads[0].wait()
    loads[1].wait()
    stores = []
    for step in range(steps):
        rows = slice(step * EDGE_BLOCK, (step + 1) * EDGE_BLOCK)
        pair = slice(step * 2 * cells, (step + 1) * 2 * cells)
        loads[2 + 2 * step].wait()
        loads[3 + 2 * step].wait()
        upstream = cot_ref[rows, :].astype(F32) + dot_nn(spread, summed_grad_ref[pair, :])
        grad_edge_ref[rows, :] = (
            upstream + dot_nt(pre_grad_ref[rows, :], w_edge_ref[...])
        ).astype(BF16)
        stores.append(
            pltpu.make_async_copy(
                grad_edge_ref.at[rows, :], grad_edge_hbm.at[rows, :], out_sems.at[step]
            )
        )
        stores[-1].start()
    for store in stores:
        store.wait()


def return_kernel(
    part_count,
    capacity,
    scal,
    node_grad_ref,
    rim_ref,
    low_ref,
    high_ref,
    ids_ref,
    *outs,
):
    cell_count, width = node_grad_ref.shape
    chunks = width // LANES
    outs[part_count][...] = jnp.zeros(outs[part_count].shape, F32)
    odd = scal[DOM_BIT] == 1
    low = low_ref[...].astype(F32)
    high = high_ref[...].astype(F32)
    first = rim_ref[:HB, :] + jnp.where(odd, low, high)
    last = rim_ref[HB:, :] + jnp.where(odd, high, low)
    grad = jnp.concatenate(
        [first.astype(BF16), node_grad_ref[HB : cell_count - HB, :], last.astype(BF16)], axis=0
    )
    for step in range(part_count):
        pick = place(ids_ref[step * 16 : (step + 1) * 16, :], cell_count)
        rows = dot_tn(pick, grad).astype(BF16)
        for chunk in range(chunks):
            outs[step][chunk * capacity : (chunk + 1) * capacity, :] = rows[
                :capacity, chunk * LANES : (chunk + 1) * LANES
            ]


def finish_kernel(part_count, capacity, scal, index_ref, *refs):
    blocks = refs[:part_count]
    out_ref, token_ref, rows_ref, pick_ref = refs[part_count:]
    cell_count, width = out_ref.shape
    chunks = width // LANES
    token_ref[...] = jnp.zeros(token_ref.shape, F32)
    slot, _ = slots_of(index_ref[...], scal[PART], part_count, cell_count)
    for step in range(part_count):
        base = step * LANES
        pick_ref[base : base + LANES, :] = hot(iota((LANES, cell_count), 0) + base == slot)
        for chunk in range(chunks):
            rows_ref[base : base + capacity, chunk * LANES : (chunk + 1) * LANES] = blocks[step][
                chunk * capacity : (chunk + 1) * capacity, :
            ]
        if capacity < LANES:
            rows_ref[base + capacity : base + LANES, :] = jnp.zeros(
                (LANES - capacity, width), BF16
            )
    out_ref[...] = dot_tn(pick_ref[...], rows_ref[...]).astype(BF16)


def shape(dims, kind=BF16):
    return jax.ShapeDtypeStruct(dims, kind)


def whole(count):
    return [pl.BlockSpec(memory_space=VMEM)] * count


def scalars():
    return pl.BlockSpec(memory_space=SMEM)


def params(limit):
    return pltpu.CompilerParams(vmem_limit_bytes=limit * MIB)


def cost(flops, bytes_accessed):
    return pl.CostEstimate(flops=flops, bytes_accessed=bytes_accessed, transcendentals=0)


def full(dims):
    return pl.BlockSpec(dims, lambda step: (0,) * len(dims))


def rows_spec(rows, columns):
    return pl.BlockSpec((rows, columns), lambda step: (step, 0))


def swap(value, axis, bit):
    count = lax.axis_size(axis)
    return lax.ppermute(value, axis, [(at, at ^ bit) for at in range(count)])


def take(value, kind, bit):
    if kind == "columns":
        half = value.shape[2] // 2
        parts = value[:, :, :half], value[:, :, half:]
    else:
        pairs = value.reshape((value.shape[0] // 2, 2) + value.shape[1:])
        parts = pairs[:, 0], pairs[:, 1]
    return jnp.where(bit == 0, parts[0], parts[1])


def core_kernel(kinds, bits, scal, keep_ref, got_ref, _, *refs):
    total_ref, left_ref, right_ref, token_ref = refs
    token_ref[...] = jnp.zeros(token_ref.shape, F32)
    total = (keep_ref[...].astype(F32) + got_ref[...].astype(F32)).astype(BF16)
    total = total.reshape(total_ref.shape)
    total_ref[...] = total
    half = total.shape[1] // 2
    left_ref[...] = take(total[:, :half], kinds[0], 1 - scal[bits[0]])
    right_ref[...] = take(total[:, half:], kinds[1], 1 - scal[bits[1]])


def stage_kernel(part, kinds, bits, scal, value_ref, got_ref, *refs):
    total_ref, send_ref = refs[-2:]
    value = value_ref[...]
    if part is not None:
        half = value.shape[1] // 2
        value = value[:, part * half : (part + 1) * half]
    mine = take(value, kinds[0], scal[bits[0]]).astype(F32)
    total = (mine + got_ref[...].astype(F32)).astype(BF16)
    total_ref[...] = total
    send_ref[...] = take(total, kinds[1], 1 - scal[bits[1]])


def split_kernel(kinds, bits, scal, *refs):
    left_ref, left_got_ref, right_ref, right_got_ref = refs[:4]
    outs = refs[-(left_got_ref.shape[0]) :]
    left = take(left_ref[...], kinds[0], scal[bits[0]]).astype(F32)
    left = (left + left_got_ref[...].astype(F32)).astype(BF16)
    right = take(right_ref[...], kinds[1], scal[bits[1]]).astype(F32)
    right = (right + right_got_ref[...].astype(F32)).astype(BF16)
    half = left.shape[1]
    owner = scal[OWNER]
    for other, out in enumerate(outs):
        for at in range(len(outs)):

            @pl.when((owner ^ other) == at)
            def _(out=out, at=at):
                out[:half, :] = left[at]
                out[half:, :] = right[at]


def sum_kernel(*refs):
    total = refs[0][...].astype(F32)
    for ref in refs[1:-2]:
        total = total + ref[...].astype(F32)
    refs[-1][...] = total.astype(BF16)


def join_kernel(at, scal, mine_ref, theirs_ref, out_ref):
    mine = mine_ref[...]
    theirs = theirs_ref[...]
    columns = mine.shape[1]
    first = scal[at] == 0
    out_ref[:, :columns] = jnp.where(first, mine, theirs).astype(out_ref.dtype)
    out_ref[:, columns:] = jnp.where(first, theirs, mine).astype(out_ref.dtype)


def local_call(kernel, outs, name, *operands):
    return pl.pallas_call(
        kernel,
        out_shape=[near_shape(*out) for out in outs],
        in_specs=[scalars()] + whole(len(operands) - 1),
        out_specs=whole(len(outs)),
        compiler_params=params(24),
        name=name,
    )(*operands)


def halved(dims, kind):
    if kind == "columns":
        return (dims[0], dims[1], dims[2] // 2)
    return (dims[0] // 2,) + dims[1:]


def chains(geom_count):
    columns = []
    bit = 2
    while bit < geom_count:
        columns.append(("columns", "geom", bit, GEOM_BITS + len(columns)))
        bit *= 2
    owner = ("owners", "dom", 1, DOM_BIT)
    return columns + [owner], [owner] + columns


def begin_weights(scal, keep, got, geom_count, part_count, *tokens):
    left, right = chains(geom_count)
    rows, width = keep.shape
    dims = (part_count, rows // part_count, width)
    piece = (part_count, rows // part_count // 2, width)
    return local_call(
        functools.partial(core_kernel, (left[0][0], right[0][0]), (left[0][3], right[0][3])),
        [
            (dims,),
            (halved(piece, left[0][0]),),
            (halved(piece, right[0][0]),),
            ((8, LANES), F32),
        ],
        "core",
        scal,
        keep,
        got,
        *tokens,
    )


def pair_weights(scal, total, send_left, send_right, geom_count, part_count, early):
    rows = total.shape[1]
    ends = []
    for part, chain, send in zip((0, 1), chains(geom_count), (send_left, send_right)):
        value = total
        now = (part_count, rows // 2, total.shape[2])
        for at in range(len(chain) - 1):
            kind, axis, bit, place_at = chain[at]
            follow = chain[at + 1]
            now = halved(now, kind)
            value, send = local_call(
                functools.partial(
                    stage_kernel,
                    part if at == 0 else None,
                    (kind, follow[0]),
                    (place_at, follow[3]),
                ),
                [(now,), (halved(now, follow[0]),)],
                "stage",
                scal,
                value,
                swap(send, axis, bit),
                *early[part],
            )
        if len(chain) == 1:
            half = rows // 2
            value = value[:, part * half : (part + 1) * half]
        ends.append((value, swap(send, chain[-1][1], chain[-1][2])))
        end = halved(now, chain[-1][0])
    return ends, end


def reduce_weights(scal, ends, end, geom_count, part_count, early, late):
    left, right = chains(geom_count)
    out = (2 * end[1], end[2])
    owners = part_count // 2
    pieces = local_call(
        functools.partial(split_kernel, (left[-1][0], right[-1][0]), (left[-1][3], right[-1][3])),
        [(out,)] * owners,
        "split",
        scal,
        *ends[0],
        *ends[1],
        early,
    )
    got = [swap(pieces[other], "dom", 2 * other) for other in range(owners - 1, 0, -1)]
    total = pl.pallas_call(
        sum_kernel,
        out_shape=near_shape(out),
        in_specs=whole(owners + 1),
        out_specs=pl.BlockSpec(memory_space=VMEM),
        compiler_params=params(24),
        name="sum",
    )(pieces[0], *got, late)
    for place_at, bit in [(link[3], link[2]) for link in left[-2::-1]] + [(CORE, 1)]:
        out = (out[0], 2 * out[1])
        last = bit == 1
        total = pl.pallas_call(
            functools.partial(join_kernel, place_at),
            out_shape=shape(out, F32) if last else near_shape(out),
            in_specs=[scalars()] + whole(2),
            out_specs=pl.BlockSpec(memory_space=VMEM),
            compiler_params=params(24),
            name="join",
        )(scal, total, swap(total, "geom", bit))
    return total


def shift(value, steps):
    count = lax.axis_size("dom")
    return lax.ppermute(value, "dom", [(at, (at + steps) % count) for at in range(count)])


def neighbour(value, first):
    count = lax.axis_size("dom")
    pairs = [(at, at + 1) for at in range(first, count - 1, 2)]
    return lax.ppermute(value, "dom", pairs + [(right, left) for left, right in pairs])


def send_order(part_count):
    return sorted(range(1, part_count), key=lambda at: (-min(at, part_count - at), at))


def pinned(value):
    return pltpu.with_memory_space_constraint(value, pltpu.HBM)


def near_shape(dims, kind=BF16):
    return pltpu.VMEM(dims, kind)


def run_prep(
    fan_in,
    cell_count,
    scal,
    source,
    edges,
    cot_nodes,
    cot_edges,
    w_edge_in,
    w_edge_out,
    w_node_in,
    w_node_out,
    token,
):
    edge_count = edges.shape[0]
    padded = cell_count + 2 * HB
    cells = EDGE_BLOCK // fan_in
    near = pl.BlockSpec(memory_space=VMEM)
    return pl.pallas_call(
        functools.partial(prep_kernel, fan_in, cell_count),
        out_shape=[
            near_shape(like.shape)
            for like in (edges, cot_nodes, cot_edges, w_edge_in, w_edge_out, w_node_in, w_node_out)
        ]
        + [
            near_shape((edge_count, padded + cells)),
            near_shape((padded, edge_count)),
            near_shape(edges.shape, F32),
            near_shape((8, LANES), F32),
        ],
        in_specs=[scalars()] + [pl.BlockSpec(memory_space=pltpu.HBM)] * 8 + [near],
        out_specs=[near] * 11,
        scratch_shapes=[VMEM(source.shape, jnp.int32), pltpu.SemaphoreType.DMA((8,))],
        compiler_params=params(PREP_LIMIT),
        cost_estimate=cost(4 * edge_count * edges.shape[1] ** 2, 20 * MIB),
        name="prep",
    )(
        scal,
        *[
            pinned(value)
            for value in (
                source,
                edges,
                cot_nodes,
                cot_edges,
                w_edge_in,
                w_edge_out,
                w_node_in,
                w_node_out,
            )
        ],
        token,
    )


def run_main(fan_in, scale, scal, nodes, low, high, prepared):
    edge_count, width = prepared[0].shape
    cell_count = nodes.shape[0]
    cells = EDGE_BLOCK // fan_in
    padded = cell_count + 2 * HB
    far = pl.BlockSpec(memory_space=pltpu.HBM)
    near = pl.BlockSpec(memory_space=VMEM)
    by_edge = (edge_count, width)
    by_cell = (cell_count, width)
    weights = (7 * width, width // 2)
    return pl.pallas_call(
        functools.partial(main_kernel, fan_in, scale),
        out_shape=[
            shape(by_edge),
            shape(by_cell),
            shape(by_edge),
            shape((2 * cell_count, width)),
            near_shape((padded, width)),
            near_shape(by_cell),
            near_shape(by_cell, F32),
            near_shape(weights),
            near_shape(weights),
        ],
        in_specs=[scalars()] + [near] * 13,
        out_specs=[far] * 4 + [near] * 5,
        scratch_shapes=[
            VMEM(by_edge, BF16),
            VMEM((2 * cell_count, width), BF16),
            VMEM(by_cell, BF16),
            VMEM((padded, width), BF16),
            VMEM((padded + cells, width), BF16),
            VMEM(by_cell, BF16),
            VMEM(by_edge, BF16),
            VMEM(by_edge, BF16),
            VMEM(by_edge, BF16),
            VMEM((edge_count, 1), F32),
            VMEM(by_cell, BF16),
            VMEM(by_edge, BF16),
            pltpu.SemaphoreType.DMA((4,)),
        ],
        compiler_params=params(MAIN_LIMIT),
        cost_estimate=cost(28 * edge_count * width * width, 16 * MIB),
        name="main",
    )(scal, nodes, low, high, *prepared)


def run_edges(fan_in, cot, summed_grad, pre_grad, w_edge_in, *tokens):
    edge_count, width = cot.shape
    steps = edge_count // EDGE_BLOCK
    far = pl.BlockSpec(memory_space=pltpu.HBM)
    return pl.pallas_call(
        functools.partial(edge_kernel, fan_in),
        out_shape=[shape((edge_count, width)), near_shape((8, LANES), F32)],
        in_specs=[far] * 4 + whole(len(tokens)),
        out_specs=[far, pl.BlockSpec(memory_space=VMEM)],
        scratch_shapes=[
            VMEM((edge_count, width), BF16),
            VMEM(summed_grad.shape, BF16),
            VMEM((edge_count, width), BF16),
            VMEM((width, width), BF16),
            VMEM((edge_count, width), BF16),
            pltpu.SemaphoreType.DMA((2 + 2 * steps,)),
            pltpu.SemaphoreType.DMA((steps,)),
        ],
        compiler_params=params(24),
        cost_estimate=cost(1, 1),
        name="edges",
    )(*[pinned(value) for value in (cot, summed_grad, pre_grad, w_edge_in)], *tokens)


def local(
    h_in,
    edge_in,
    new_index,
    source,
    w_edge_in,
    w_edge_out,
    w_node_in,
    w_node_out,
    cot_nodes,
    cot_edges,
):
    _, cell_count, width = h_in.shape
    edge_count = source.shape[1]
    fan_in = edge_count // cell_count
    part_count = lax.axis_size("dom")
    geom_count = lax.axis_size("geom")
    capacity = cell_count // part_count + cell_count // part_count // 2
    chunks = width // LANES
    block_rows = chunks * capacity
    scale = 1.0 / math.sqrt(geom_count * part_count * cell_count * fan_in)
    part = lax.axis_index("dom")
    geom = lax.axis_index("geom")
    scal = [part, geom % 2, part % 2, part // 2]
    geom = geom // 2
    for _ in range(1, geom_count.bit_length() - 1):
        scal.append(geom % 2)
        geom = geom // 2
    scal = jnp.stack(scal).astype(jnp.int32)
    edges = edge_in[0]
    cot = cot_edges[0]

    sends = pl.pallas_call(
        functools.partial(pack_kernel, part_count, capacity),
        out_shape=[shape((block_rows + 16, LANES))] * part_count + [near_shape((8, LANES), F32)],
        in_specs=[scalars()] + whole(2),
        out_specs=whole(part_count + 1),
        compiler_params=params(24),
        name="pack",
    )(scal, h_in[0], new_index)
    prepared = run_prep(
        fan_in,
        cell_count,
        scal,
        source,
        edges,
        cot_nodes[0],
        cot,
        w_edge_in,
        w_edge_out,
        w_node_in,
        w_node_out,
        sends[part_count],
    )
    got = {0: sends[0]}
    for step in send_order(part_count):
        got[step] = shift(sends[step], step)
    nodes, low, high, ids = pl.pallas_call(
        functools.partial(unpack_kernel, part_count, capacity),
        out_shape=[
            shape((cell_count, width)),
            shape((HB, width)),
            shape((HB, width)),
            shape((part_count * 16, LANES)),
        ],
        in_specs=whole(part_count) + [scalars()] + whole(1),
        out_specs=whole(4),
        scratch_shapes=[
            VMEM((part_count * LANES, width), BF16),
            VMEM((cell_count, part_count * LANES), BF16),
        ],
        compiler_params=params(24),
        name="unpack",
    )(*[got[step] for step in range(part_count)], scal, prepared[-1])
    low = neighbour(low, 0)
    high = neighbour(high, 1)

    (
        edge_new,
        node_new,
        pre_grad,
        summed_grad,
        sent,
        received,
        base,
        keep,
        send,
    ) = run_main(fan_in, scale, scal, nodes, low, high, prepared[:-1])
    low, high, node_grad, rim = pl.pallas_call(
        cell_kernel,
        out_shape=[
            near_shape((HB, width)),
            near_shape((HB, width)),
            near_shape((cell_count, width)),
            near_shape((2 * HB, width), F32),
        ],
        in_specs=[scalars()] + whole(4),
        out_specs=whole(4),
        compiler_params=params(24),
        cost_estimate=cost(3 * cell_count * width * width, 3 * MIB),
        name="cells",
    )(scal, sent, received, base, prepared[3])
    low = neighbour(low, 0)
    high = neighbour(high, 1)
    *returning, token = pl.pallas_call(
        functools.partial(return_kernel, part_count, capacity),
        out_shape=[near_shape((block_rows, LANES))] * part_count + [near_shape((8, LANES), F32)],
        in_specs=[scalars()] + whole(5),
        out_specs=whole(part_count + 1),
        compiler_params=params(24),
        cost_estimate=cost(1, 1),
        name="returning",
    )(scal, node_grad, rim, low, high, ids)
    *begun, token = begin_weights(
        scal, keep, swap(send, "geom", 1), geom_count, part_count, token
    )

    grad_edge, edge_token = run_edges(
        fan_in, cot, summed_grad, pre_grad, w_edge_in, token
    )
    back = {0: returning[0]}
    for step in send_order(part_count):
        back[step] = shift(returning[step], -step)
    early = [back[step] for step in send_order(part_count)]
    ends, end = pair_weights(
        scal, *begun, geom_count, part_count, (early[:FIRST], early[:SECOND])
    )
    grad_in, late = pl.pallas_call(
        functools.partial(finish_kernel, part_count, capacity),
        out_shape=[shape((cell_count, width)), near_shape((8, LANES), F32)],
        in_specs=[scalars()] + whole(1 + part_count),
        out_specs=whole(2),
        scratch_shapes=[
            VMEM((part_count * LANES, width), BF16),
            VMEM((part_count * LANES, cell_count), BF16),
        ],
        compiler_params=params(24),
        name="finish",
    )(scal, new_index, *[back[step] for step in range(part_count)])
    weight_grads = reduce_weights(scal, ends, end, geom_count, part_count, edge_token, late)
    return (node_new[None], edge_new[None], grad_in[None], grad_edge[None], weight_grads)


def solution(mesh):
    return jax.shard_map(
        local,
        mesh=mesh,
        in_specs=(
            P("geom", "dom", None),
            P("geom", "dom", None),
            P("geom", "dom"),
            P("geom", "dom"),
            P(),
            P(),
            P(),
            P(),
            P("geom", "dom", None),
            P("geom", "dom", None),
        ),
        out_specs=(
            P("geom", "dom", None),
            P("geom", "dom", None),
            P("geom", "dom", None),
            P("geom", "dom", None),
            P("dom", None),
        ),
        check_vma=False,
    )
```

```python
import functools
import math

import jax
import jax.numpy as jnp
from jax import lax
from jax.experimental import pallas as pl
from jax.experimental.pallas import tpu as pltpu
from jax.sharding import PartitionSpec as P

HB = 64
LANES = 128
EDGE_BLOCK = 512
MIB = 1024 * 1024
MAIN_LIMIT = 25
FIRST, SECOND = 3, 7
PREP_LIMIT = 20
PART, CORE, DOM_BIT, OWNER, GEOM_BITS = range(5)
F32 = jnp.float32
BF16 = jnp.bfloat16
VMEM = pltpu.VMEM
SMEM = pltpu.SMEM


def dot_nn(left, right):
    return lax.dot_general(left, right, (((1,), (0,)), ((), ())), preferred_element_type=F32)


def dot_nt(left, right):
    return lax.dot_general(left, right, (((1,), (1,)), ((), ())), preferred_element_type=F32)


def dot_tn(left, right):
    return lax.dot_general(left, right, (((0,), (0,)), ((), ())), preferred_element_type=F32)


def iota(shape, axis):
    return lax.broadcasted_iota(jnp.int32, shape, axis)


def hot(condition):
    return jnp.where(condition, 1.0, 0.0).astype(BF16)


def sigmoid(values):
    return 0.5 * jnp.tanh(0.5 * values) + 0.5


def normalize(values):
    center = values - jnp.mean(values, axis=-1, keepdims=True)
    inverse = lax.rsqrt(jnp.mean(center * center, axis=-1, keepdims=True) + 1e-05)
    return center * inverse, inverse


def normalize_back(normed, inverse, upstream):
    return inverse * (
        upstream
        - jnp.mean(upstream, axis=-1, keepdims=True)
        - normed * jnp.mean(upstream * normed, axis=-1, keepdims=True)
    )


def slots_of(index, me, part_count, cell_count):
    owner = jnp.zeros_like(index)
    for part in range(1, part_count):
        owner = owner + jnp.where(index >= part * cell_count, 1, 0)
    row = index - owner * cell_count
    ahead = owner - me
    ahead = jnp.where(ahead < 0, ahead + part_count, ahead)
    high = -(-part_count // 16) * 16
    member = hot(iota((high, cell_count), 0) == ahead)
    before = hot(iota((cell_count, cell_count), 0) < iota((cell_count, cell_count), 1))
    rank = jnp.sum(member.astype(F32) * dot_nn(member, before), axis=0, keepdims=True)
    return ahead * LANES + rank.astype(jnp.int32), row


def pack_kernel(part_count, capacity, scal, h_hbm, index_hbm, *refs):
    outs = refs[:-3]
    h_ref, index_ref, sems = refs[-3:]
    cell_count, width = h_ref.shape
    loads = [
        pltpu.make_async_copy(index_hbm, index_ref, sems.at[0]),
        pltpu.make_async_copy(h_hbm, h_ref, sems.at[1]),
    ]
    for load in loads:
        load.start()
    loads[0].wait()
    chunks = width // LANES
    slot, row = slots_of(index_ref[...], scal[PART], part_count, cell_count)
    kind = iota((16, cell_count), 0)
    coded = jnp.where(
        kind == 0, row >> 8, jnp.where(kind == 1, row & 255, jnp.where(kind == 2, 1, 0))
    )
    coded = coded.astype(F32).astype(BF16)
    loads[1].wait()
    cells = h_ref[...]
    for step in range(part_count):
        pick = hot(iota((LANES, cell_count), 0) + step * LANES == slot)
        rows = dot_nn(pick, cells).astype(BF16)
        for chunk in range(chunks):
            outs[step][chunk * capacity : (chunk + 1) * capacity, :] = rows[
                :capacity, chunk * LANES : (chunk + 1) * LANES
            ]
        outs[step][chunks * capacity :, :] = dot_nt(coded, pick).astype(BF16)
    outs[part_count][...] = jnp.zeros(outs[part_count].shape, F32)


def place(ids, cell_count):
    ids = ids.astype(F32)
    spot = ids[0:1] * 256.0 + ids[1:2] + (ids[2:3] - 1.0) * 65536.0
    return hot(iota((cell_count, LANES), 0) == spot.astype(jnp.int32))


def unpack_kernel(part_count, capacity, *refs):
    blocks = refs[:part_count]
    scal, _, nodes_ref, low_ref, high_ref, ids_ref, rows_ref, hot_ref = refs[part_count:]
    cell_count, width = nodes_ref.shape
    chunks = width // LANES
    for step in range(part_count):
        base = step * LANES
        ids = blocks[step][chunks * capacity :, :]
        ids_ref[step * 16 : (step + 1) * 16, :] = ids
        hot_ref[:, base : base + LANES] = place(ids, cell_count)
        for chunk in range(chunks):
            rows_ref[base : base + capacity, chunk * LANES : (chunk + 1) * LANES] = blocks[step][
                chunk * capacity : (chunk + 1) * capacity, :
            ]
        if capacity < LANES:
            rows_ref[base + capacity : base + LANES, :] = jnp.zeros(
                (LANES - capacity, width), BF16
            )
    nodes = dot_nn(hot_ref[...], rows_ref[...]).astype(BF16)
    nodes_ref[...] = nodes
    odd = scal[DOM_BIT] == 1
    head = nodes[:HB]
    tail = nodes[cell_count - HB :]
    low_ref[...] = jnp.where(odd, head, tail)
    high_ref[...] = jnp.where(odd, tail, head)


def spread_rows(wide, base, rows, fan_in):
    count, width = rows.shape
    chunks = width // LANES
    for chunk in range(chunks):
        for at in range(fan_in):
            wide[base + chunk, pl.ds(at, count, stride=fan_in), :] = rows[
                :, chunk * LANES : (chunk + 1) * LANES
            ]
    return jnp.concatenate([wide[base + chunk] for chunk in range(chunks)], axis=1)


def collect_rows(wide, base, values, fan_in):
    count = values.shape[0] // fan_in
    sums = []
    for chunk in range(values.shape[1] // LANES):
        wide[base + chunk] = values[:, chunk * LANES : (chunk + 1) * LANES]
        total = wide[base + chunk, pl.ds(0, count, stride=fan_in), :]
        for at in range(1, fan_in):
            total = total + wide[base + chunk, pl.ds(at, count, stride=fan_in), :]
        sums.append(total)
    return jnp.concatenate(sums, axis=1)


def prep_kernel(
    fan_in,
    cell_count,
    scal,
    source_hbm,
    edges_hbm,
    cot_nodes_hbm,
    cot_edges_hbm,
    w_edge_in_hbm,
    w_edge_out_hbm,
    w_node_in_hbm,
    w_node_out_hbm,
    _,
    edges_ref,
    cot_nodes_ref,
    cot_edges_ref,
    w_edge_in_ref,
    w_edge_out_ref,
    w_node_in_ref,
    w_node_out_ref,
    gather_ref,
    scatter_ref,
    pre_ref,
    token_ref,
    source_ref,
    sems,
):
    edge_count, width = edges_ref.shape
    padded = cell_count + 2 * HB
    cells = EDGE_BLOCK // fan_in
    loads = [
        pltpu.make_async_copy(far, near, sems.at[at])
        for at, (far, near) in enumerate(
            (
                (source_hbm, source_ref),
                (edges_hbm, edges_ref),
                (w_edge_in_hbm, w_edge_in_ref),
                (w_edge_out_hbm, w_edge_out_ref),
                (w_node_in_hbm, w_node_in_ref),
                (w_node_out_hbm, w_node_out_ref),
                (cot_nodes_hbm, cot_nodes_ref),
                (cot_edges_hbm, cot_edges_ref),
            )
        )
    ]
    for load in loads:
        load.start()
    token_ref[...] = jnp.zeros(token_ref.shape, F32)
    loads[0].wait()
    offset = scal[PART] * cell_count - HB

    def hots(step, carry):
        rows = pl.ds(pl.multiple_of(step * EDGE_BLOCK, EDGE_BLOCK), EDGE_BLOCK)
        local = source_ref[:, rows] - offset
        scatter_ref[:, rows] = hot(iota((padded, EDGE_BLOCK), 0) == local)
        local = jnp.transpose(jnp.broadcast_to(local.astype(F32), (LANES, EDGE_BLOCK)))
        local = local.astype(jnp.int32)
        lane = iota((EDGE_BLOCK, LANES), 1)
        for at in range(0, padded, LANES):
            gather_ref[rows, at : at + LANES] = hot(local == lane + at)
        gather_ref[rows, padded:] = hot(
            iota((EDGE_BLOCK, cells), 0) // fan_in == iota((EDGE_BLOCK, cells), 1)
        )
        return carry

    lax.fori_loop(0, edge_count // EDGE_BLOCK, hots, 0)
    loads[1].wait()
    loads[2].wait()

    def first(step, carry):
        rows = pl.ds(pl.multiple_of(step * EDGE_BLOCK, EDGE_BLOCK), EDGE_BLOCK)
        pre_ref[rows, :] = dot_nn(edges_ref[rows, :], w_edge_in_ref[:width, :])
        return carry

    lax.fori_loop(0, edge_count // EDGE_BLOCK, first, 0)
    for load in loads[3:]:
        load.wait()


def main_kernel(
    fan_in,
    scale,
    scal,
    nodes_ref,
    low_ref,
    high_ref,
    edges_ref,
    cot_nodes_ref,
    cot_edges_ref,
    w_edge_in_ref,
    w_edge_out_ref,
    w_node_in_ref,
    w_node_out_ref,
    gather_ref,
    scatter_ref,
    pre_ref,
    edge_new_hbm,
    node_new_hbm,
    pre_grad_hbm,
    summed_grad_hbm,
    sent_ref,
    received_ref,
    base_ref,
    keep_ref,
    send_ref,
    pre_grad_ref,
    summed_grad_ref,
    node_new_ref,
    cells_ref,
    table_ref,
    recv_ref,
    hidden_ref,
    slope_ref,
    normed_ref,
    inverse_ref,
    summed_ref,
    post_grad_ref,
    wide_ref,
    out_sems,
):
    cell_count, width = nodes_ref.shape
    edge_count = edges_ref.shape[0]
    steps = edge_count // EDGE_BLOCK
    padded = cell_count + 2 * HB
    cells = EDGE_BLOCK // fan_in
    half = width // 2
    inner = slice(HB, HB + cell_count)

    odd = scal[DOM_BIT] == 1
    low = low_ref[...]
    high = high_ref[...]
    cells_ref[:HB, :] = jnp.where(odd, low, high)
    cells_ref[inner, :] = nodes_ref[...]
    cells_ref[HB + cell_count :, :] = jnp.where(odd, high, low)
    table_ref[:padded, :] = dot_nn(cells_ref[...], w_edge_in_ref[width : 2 * width, :]).astype(BF16)
    recv_ref[...] = dot_nn(nodes_ref[...], w_edge_in_ref[2 * width :, :]).astype(BF16)

    for step in range(steps):
        spot = slice(step * cells, (step + 1) * cells)
        rows = slice(step * EDGE_BLOCK, (step + 1) * EDGE_BLOCK)
        table_ref[padded : padded + cells, :] = recv_ref[spot, :]
        edges = edges_ref[rows, :]
        pre = pre_ref[rows, :] + dot_nn(gather_ref[rows, :], table_ref[...])
        gate = sigmoid(pre)
        hidden = (pre * gate).astype(BF16)
        hidden_ref[rows, :] = hidden
        slope_ref[rows, :] = (gate * (1.0 + pre * (1.0 - gate))).astype(BF16)
        normed, inverse = normalize(dot_nn(hidden, w_edge_out_ref[...]))
        normed_ref[rows, :] = normed.astype(BF16)
        inverse_ref[rows, :] = inverse
        edge_new = (edges.astype(F32) + normed).astype(BF16)
        post_grad_ref[rows, :] = edge_new
        summed_ref[spot, :] = collect_rows(wide_ref, 0, edge_new.astype(F32), fan_in).astype(BF16)

    edge_store = pltpu.make_async_copy(post_grad_ref, edge_new_hbm, out_sems.at[0])
    edge_store.start()
    nodes = nodes_ref[...]
    summed = summed_ref[...]
    node_pre = dot_nn(nodes, w_node_in_ref[:width, :]) + dot_nn(summed, w_node_in_ref[width:, :])
    node_gate = sigmoid(node_pre)
    node_hidden = (node_pre * node_gate).astype(BF16)
    node_normed, node_inverse = normalize(dot_nn(node_hidden, w_node_out_ref[...]))
    node_new_ref[...] = (nodes.astype(F32) + node_normed).astype(BF16)
    node_store = pltpu.make_async_copy(node_new_ref, node_new_hbm, out_sems.at[1])
    node_store.start()
    upstream = cot_nodes_ref[...].astype(F32)
    node_post_grad = normalize_back(node_normed, node_inverse, upstream).astype(BF16)
    node_slope = node_gate * (1.0 + node_pre * (1.0 - node_gate))
    node_pre_grad = (dot_nt(node_post_grad, w_node_out_ref[...]) * node_slope).astype(BF16)
    summed_grad = dot_nt(node_pre_grad, w_node_in_ref[width:, :])
    summed_grad_ref[...] = summed_grad
    summed_store = pltpu.make_async_copy(summed_grad_ref, summed_grad_hbm, out_sems.at[2])
    summed_store.start()
    base_ref[...] = upstream + dot_nt(node_pre_grad, w_node_in_ref[:width, :])
    edge_store.wait()
    for step in range(steps):
        spot = slice(step * cells, (step + 1) * cells)
        rows = slice(step * EDGE_BLOCK, (step + 1) * EDGE_BLOCK)
        base = (step % 2) * (width // LANES)
        upstream = cot_edges_ref[rows, :].astype(F32) + spread_rows(
            wide_ref, base, summed_grad_ref[spot, :], fan_in
        )
        post_grad = normalize_back(
            normed_ref[rows, :].astype(F32), inverse_ref[rows, :], upstream
        )
        post_grad = post_grad.astype(BF16)
        post_grad_ref[rows, :] = post_grad
        pre_grad = dot_nt(post_grad, w_edge_out_ref[...]) * slope_ref[rows, :].astype(F32)
        pre_grad = pre_grad.astype(BF16)
        pre_grad_ref[rows, :] = pre_grad
        received_ref[spot, :] = collect_rows(
            wide_ref, base, pre_grad.astype(F32), fan_in
        ).astype(BF16)

    pre_store = pltpu.make_async_copy(pre_grad_ref, pre_grad_hbm, out_sems.at[3])
    pre_store.start()
    first = scal[CORE] == 0

    def put(place_at, value):
        value = (value * scale).astype(BF16)
        rows = slice(place_at * width, (place_at + 1) * width)
        left = value[:, :half]
        right = value[:, half:]
        keep_ref[rows, :] = jnp.where(first, left, right)
        send_ref[rows, :] = jnp.where(first, right, left)

    sent = dot_nn(scatter_ref[...], pre_grad_ref[...]).astype(BF16)
    sent_ref[...] = sent
    put(0, dot_tn(edges_ref[...], pre_grad_ref[...]))
    put(1, dot_tn(cells_ref[...], sent))
    put(2, dot_tn(nodes, received_ref[...]))
    put(3, dot_tn(hidden_ref[...], post_grad_ref[...]))
    put(4, dot_tn(nodes, node_pre_grad))
    put(5, dot_tn(summed, node_pre_grad))
    put(6, dot_tn(node_hidden, node_post_grad))
    node_store.wait()
    summed_store.wait()
    pre_store.wait()


def cell_kernel(
    scal,
    sent_ref,
    received_ref,
    base_ref,
    w_edge_in_ref,
    low_ref,
    high_ref,
    node_grad_ref,
    rim_ref,
):
    cell_count, width = received_ref.shape
    sender = dot_nt(sent_ref[...], w_edge_in_ref[width : 2 * width, :])
    odd = scal[DOM_BIT] == 1
    to_prev = sender[:HB].astype(BF16)
    to_next = sender[HB + cell_count :].astype(BF16)
    low_ref[...] = jnp.where(odd, to_prev, to_next)
    high_ref[...] = jnp.where(odd, to_next, to_prev)
    node_grad = (
        base_ref[...]
        + dot_nt(received_ref[...], w_edge_in_ref[2 * width :, :])
        + sender[HB : HB + cell_count]
    )
    node_grad_ref[...] = node_grad.astype(BF16)
    rim_ref[:HB, :] = node_grad[:HB]
    rim_ref[HB:, :] = node_grad[cell_count - HB :]


def edge_kernel(
    fan_in,
    cot_hbm,
    summed_grad_hbm,
    pre_grad_hbm,
    w_edge_in_hbm,
    _,
    grad_edge_hbm,
    token_ref,
    cot_ref,
    summed_grad_ref,
    pre_grad_ref,
    w_edge_ref,
    grad_edge_ref,
    wide_ref,
    in_sems,
    out_sems,
):
    edge_count, width = cot_ref.shape
    steps = edge_count // EDGE_BLOCK
    cells = EDGE_BLOCK // fan_in
    loads = [
        pltpu.make_async_copy(w_edge_in_hbm.at[:width, :], w_edge_ref, in_sems.at[0]),
        pltpu.make_async_copy(summed_grad_hbm, summed_grad_ref, in_sems.at[1]),
    ]
    for step in range(steps):
        rows = slice(step * EDGE_BLOCK, (step + 1) * EDGE_BLOCK)
        for at, (far, near) in enumerate(((cot_hbm, cot_ref), (pre_grad_hbm, pre_grad_ref))):
            loads.append(
                pltpu.make_async_copy(
                    far.at[rows, :], near.at[rows, :], in_sems.at[2 + 2 * step + at]
                )
            )
    for load in loads:
        load.start()
    token_ref[...] = jnp.zeros(token_ref.shape, F32)
    loads[0].wait()
    loads[1].wait()
    stores = []
    for step in range(steps):
        rows = slice(step * EDGE_BLOCK, (step + 1) * EDGE_BLOCK)
        loads[2 + 2 * step].wait()
        loads[3 + 2 * step].wait()
        upstream = cot_ref[rows, :].astype(F32) + spread_rows(
            wide_ref, 0, summed_grad_ref[step * cells : (step + 1) * cells, :], fan_in
        )
        grad_edge_ref[rows, :] = (
            upstream + dot_nt(pre_grad_ref[rows, :], w_edge_ref[...])
        ).astype(BF16)
        stores.append(
            pltpu.make_async_copy(
                grad_edge_ref.at[rows, :], grad_edge_hbm.at[rows, :], out_sems.at[step]
            )
        )
        stores[-1].start()
    for store in stores:
        store.wait()


def return_kernel(
    part_count,
    capacity,
    scal,
    node_grad_ref,
    rim_ref,
    low_ref,
    high_ref,
    ids_ref,
    *outs,
):
    cell_count, width = node_grad_ref.shape
    chunks = width // LANES
    outs[part_count][...] = jnp.zeros(outs[part_count].shape, F32)
    odd = scal[DOM_BIT] == 1
    low = low_ref[...].astype(F32)
    high = high_ref[...].astype(F32)
    first = rim_ref[:HB, :] + jnp.where(odd, low, high)
    last = rim_ref[HB:, :] + jnp.where(odd, high, low)
    grad = jnp.concatenate(
        [first.astype(BF16), node_grad_ref[HB : cell_count - HB, :], last.astype(BF16)], axis=0
    )
    for step in range(part_count):
        pick = place(ids_ref[step * 16 : (step + 1) * 16, :], cell_count)
        rows = dot_tn(pick, grad).astype(BF16)
        for chunk in range(chunks):
            outs[step][chunk * capacity : (chunk + 1) * capacity, :] = rows[
                :capacity, chunk * LANES : (chunk + 1) * LANES
            ]


def finish_kernel(part_count, capacity, scal, index_ref, *refs):
    blocks = refs[:part_count]
    out_ref, token_ref, rows_ref, pick_ref = refs[part_count:]
    cell_count, width = out_ref.shape
    chunks = width // LANES
    token_ref[...] = jnp.zeros(token_ref.shape, F32)
    slot, _ = slots_of(index_ref[...], scal[PART], part_count, cell_count)
    for step in range(part_count):
        base = step * LANES
        pick_ref[base : base + LANES, :] = hot(iota((LANES, cell_count), 0) + base == slot)
        for chunk in range(chunks):
            rows_ref[base : base + capacity, chunk * LANES : (chunk + 1) * LANES] = blocks[step][
                chunk * capacity : (chunk + 1) * capacity, :
            ]
        if capacity < LANES:
            rows_ref[base + capacity : base + LANES, :] = jnp.zeros(
                (LANES - capacity, width), BF16
            )
    out_ref[...] = dot_tn(pick_ref[...], rows_ref[...]).astype(BF16)


def shape(dims, kind=BF16):
    return jax.ShapeDtypeStruct(dims, kind)


def whole(count):
    return [pl.BlockSpec(memory_space=VMEM)] * count


def scalars():
    return pl.BlockSpec(memory_space=SMEM)


def params(limit):
    return pltpu.CompilerParams(vmem_limit_bytes=limit * MIB)


def cost(flops, bytes_accessed):
    return pl.CostEstimate(flops=flops, bytes_accessed=bytes_accessed, transcendentals=0)


def full(dims):
    return pl.BlockSpec(dims, lambda step: (0,) * len(dims))


def rows_spec(rows, columns):
    return pl.BlockSpec((rows, columns), lambda step: (step, 0))


def swap(value, axis, bit):
    count = lax.axis_size(axis)
    return lax.ppermute(value, axis, [(at, at ^ bit) for at in range(count)])


def take(value, kind, bit):
    if kind == "columns":
        half = value.shape[2] // 2
        parts = value[:, :, :half], value[:, :, half:]
    else:
        pairs = value.reshape((value.shape[0] // 2, 2) + value.shape[1:])
        parts = pairs[:, 0], pairs[:, 1]
    return jnp.where(bit == 0, parts[0], parts[1])


def core_kernel(kinds, bits, scal, keep_ref, got_ref, _, *refs):
    total_ref, left_ref, right_ref, token_ref = refs
    token_ref[...] = jnp.zeros(token_ref.shape, F32)
    total = (keep_ref[...].astype(F32) + got_ref[...].astype(F32)).astype(BF16)
    total = total.reshape(total_ref.shape)
    total_ref[...] = total
    half = total.shape[1] // 2
    left_ref[...] = take(total[:, :half], kinds[0], 1 - scal[bits[0]])
    right_ref[...] = take(total[:, half:], kinds[1], 1 - scal[bits[1]])


def stage_kernel(part, kinds, bits, scal, value_ref, got_ref, *refs):
    total_ref, send_ref = refs[-2:]
    value = value_ref[...]
    if part is not None:
        half = value.shape[1] // 2
        value = value[:, part * half : (part + 1) * half]
    mine = take(value, kinds[0], scal[bits[0]]).astype(F32)
    total = (mine + got_ref[...].astype(F32)).astype(BF16)
    total_ref[...] = total
    send_ref[...] = take(total, kinds[1], 1 - scal[bits[1]])


def split_kernel(kinds, bits, scal, *refs):
    left_ref, left_got_ref, right_ref, right_got_ref = refs[:4]
    outs = refs[-(left_got_ref.shape[0]) :]
    left = take(left_ref[...], kinds[0], scal[bits[0]]).astype(F32)
    left = (left + left_got_ref[...].astype(F32)).astype(BF16)
    right = take(right_ref[...], kinds[1], scal[bits[1]]).astype(F32)
    right = (right + right_got_ref[...].astype(F32)).astype(BF16)
    half = left.shape[1]
    owner = scal[OWNER]
    for other, out in enumerate(outs):
        for at in range(len(outs)):

            @pl.when((owner ^ other) == at)
            def _(out=out, at=at):
                out[:half, :] = left[at]
                out[half:, :] = right[at]


def sum_kernel(*refs):
    total = refs[0][...].astype(F32)
    for ref in refs[1:-2]:
        total = total + ref[...].astype(F32)
    refs[-1][...] = total.astype(BF16)


def join_kernel(at, scal, mine_ref, theirs_ref, out_ref):
    mine = mine_ref[...]
    theirs = theirs_ref[...]
    columns = mine.shape[1]
    first = scal[at] == 0
    out_ref[:, :columns] = jnp.where(first, mine, theirs).astype(out_ref.dtype)
    out_ref[:, columns:] = jnp.where(first, theirs, mine).astype(out_ref.dtype)


def local_call(kernel, outs, name, *operands):
    return pl.pallas_call(
        kernel,
        out_shape=[near_shape(*out) for out in outs],
        in_specs=[scalars()] + whole(len(operands) - 1),
        out_specs=whole(len(outs)),
        compiler_params=params(24),
        name=name,
    )(*operands)


def halved(dims, kind):
    if kind == "columns":
        return (dims[0], dims[1], dims[2] // 2)
    return (dims[0] // 2,) + dims[1:]


def chains(geom_count):
    columns = []
    bit = 2
    while bit < geom_count:
        columns.append(("columns", "geom", bit, GEOM_BITS + len(columns)))
        bit *= 2
    owner = ("owners", "dom", 1, DOM_BIT)
    return columns + [owner], [owner] + columns


def begin_weights(scal, keep, got, geom_count, part_count, *tokens):
    left, right = chains(geom_count)
    rows, width = keep.shape
    dims = (part_count, rows // part_count, width)
    piece = (part_count, rows // part_count // 2, width)
    return local_call(
        functools.partial(core_kernel, (left[0][0], right[0][0]), (left[0][3], right[0][3])),
        [
            (dims,),
            (halved(piece, left[0][0]),),
            (halved(piece, right[0][0]),),
            ((8, LANES), F32),
        ],
        "core",
        scal,
        keep,
        got,
        *tokens,
    )


def pair_weights(scal, total, send_left, send_right, geom_count, part_count, early):
    rows = total.shape[1]
    ends = []
    for part, chain, send in zip((0, 1), chains(geom_count), (send_left, send_right)):
        value = total
        now = (part_count, rows // 2, total.shape[2])
        for at in range(len(chain) - 1):
            kind, axis, bit, place_at = chain[at]
            follow = chain[at + 1]
            now = halved(now, kind)
            value, send = local_call(
                functools.partial(
                    stage_kernel,
                    part if at == 0 else None,
                    (kind, follow[0]),
                    (place_at, follow[3]),
                ),
                [(now,), (halved(now, follow[0]),)],
                "stage",
                scal,
                value,
                swap(send, axis, bit),
                *early[part],
            )
        if len(chain) == 1:
            half = rows // 2
            value = value[:, part * half : (part + 1) * half]
        ends.append((value, swap(send, chain[-1][1], chain[-1][2])))
        end = halved(now, chain[-1][0])
    return ends, end


def reduce_weights(scal, ends, end, geom_count, part_count, early, late):
    left, right = chains(geom_count)
    out = (2 * end[1], end[2])
    owners = part_count // 2
    pieces = local_call(
        functools.partial(split_kernel, (left[-1][0], right[-1][0]), (left[-1][3], right[-1][3])),
        [(out,)] * owners,
        "split",
        scal,
        *ends[0],
        *ends[1],
        early,
    )
    got = [swap(pieces[other], "dom", 2 * other) for other in range(owners - 1, 0, -1)]
    total = pl.pallas_call(
        sum_kernel,
        out_shape=near_shape(out),
        in_specs=whole(owners + 1),
        out_specs=pl.BlockSpec(memory_space=VMEM),
        compiler_params=params(24),
        name="sum",
    )(pieces[0], *got, late)
    for place_at, bit in [(link[3], link[2]) for link in left[-2::-1]] + [(CORE, 1)]:
        out = (out[0], 2 * out[1])
        last = bit == 1
        total = pl.pallas_call(
            functools.partial(join_kernel, place_at),
            out_shape=shape(out, F32) if last else near_shape(out),
            in_specs=[scalars()] + whole(2),
            out_specs=pl.BlockSpec(memory_space=VMEM),
            compiler_params=params(24),
            name="join",
        )(scal, total, swap(total, "geom", bit))
    return total


def shift(value, steps):
    count = lax.axis_size("dom")
    return lax.ppermute(value, "dom", [(at, (at + steps) % count) for at in range(count)])


def neighbour(value, first):
    count = lax.axis_size("dom")
    pairs = [(at, at + 1) for at in range(first, count - 1, 2)]
    return lax.ppermute(value, "dom", pairs + [(right, left) for left, right in pairs])


def send_order(part_count):
    return sorted(range(1, part_count), key=lambda at: (-min(at, part_count - at), at))


def pinned(value):
    return pltpu.with_memory_space_constraint(value, pltpu.HBM)


def near_shape(dims, kind=BF16):
    return pltpu.VMEM(dims, kind)


def run_prep(
    fan_in,
    cell_count,
    scal,
    source,
    edges,
    cot_nodes,
    cot_edges,
    w_edge_in,
    w_edge_out,
    w_node_in,
    w_node_out,
    token,
):
    edge_count = edges.shape[0]
    padded = cell_count + 2 * HB
    cells = EDGE_BLOCK // fan_in
    near = pl.BlockSpec(memory_space=VMEM)
    return pl.pallas_call(
        functools.partial(prep_kernel, fan_in, cell_count),
        out_shape=[
            near_shape(like.shape)
            for like in (edges, cot_nodes, cot_edges, w_edge_in, w_edge_out, w_node_in, w_node_out)
        ]
        + [
            near_shape((edge_count, padded + cells)),
            near_shape((padded, edge_count)),
            near_shape(edges.shape, F32),
            near_shape((8, LANES), F32),
        ],
        in_specs=[scalars()] + [pl.BlockSpec(memory_space=pltpu.HBM)] * 8 + [near],
        out_specs=[near] * 11,
        scratch_shapes=[VMEM(source.shape, jnp.int32), pltpu.SemaphoreType.DMA((8,))],
        compiler_params=params(PREP_LIMIT),
        cost_estimate=cost(4 * edge_count * edges.shape[1] ** 2, 20 * MIB),
        name="prep",
    )(
        scal,
        *[
            pinned(value)
            for value in (
                source,
                edges,
                cot_nodes,
                cot_edges,
                w_edge_in,
                w_edge_out,
                w_node_in,
                w_node_out,
            )
        ],
        token,
    )


def run_main(fan_in, scale, scal, nodes, low, high, prepared):
    edge_count, width = prepared[0].shape
    cell_count = nodes.shape[0]
    cells = EDGE_BLOCK // fan_in
    padded = cell_count + 2 * HB
    far = pl.BlockSpec(memory_space=pltpu.HBM)
    near = pl.BlockSpec(memory_space=VMEM)
    by_edge = (edge_count, width)
    by_cell = (cell_count, width)
    weights = (7 * width, width // 2)
    return pl.pallas_call(
        functools.partial(main_kernel, fan_in, scale),
        out_shape=[
            shape(by_edge),
            shape(by_cell),
            pltpu.HBM(by_edge, BF16),
            pltpu.HBM(by_cell, F32),
            near_shape((padded, width)),
            near_shape(by_cell),
            near_shape(by_cell, F32),
            near_shape(weights),
            near_shape(weights),
        ],
        in_specs=[scalars()] + [near] * 13,
        out_specs=[far] * 4 + [near] * 5,
        scratch_shapes=[
            VMEM(by_edge, BF16),
            VMEM(by_cell, F32),
            VMEM(by_cell, BF16),
            VMEM((padded, width), BF16),
            VMEM((padded + cells, width), BF16),
            VMEM(by_cell, BF16),
            VMEM(by_edge, BF16),
            VMEM(by_edge, BF16),
            VMEM(by_edge, BF16),
            VMEM((edge_count, 1), F32),
            VMEM(by_cell, BF16),
            VMEM(by_edge, BF16),
            VMEM((2 * width // LANES, EDGE_BLOCK, LANES), F32),
            pltpu.SemaphoreType.DMA((4,)),
        ],
        compiler_params=params(MAIN_LIMIT),
        cost_estimate=cost(28 * edge_count * width * width, 16 * MIB),
        name="main",
    )(scal, nodes, low, high, *prepared)


def run_edges(fan_in, cot, summed_grad, pre_grad, w_edge_in, *tokens):
    edge_count, width = cot.shape
    steps = edge_count // EDGE_BLOCK
    far = pl.BlockSpec(memory_space=pltpu.HBM)
    return pl.pallas_call(
        functools.partial(edge_kernel, fan_in),
        out_shape=[shape((edge_count, width)), near_shape((8, LANES), F32)],
        in_specs=[far] * 4 + whole(len(tokens)),
        out_specs=[far, pl.BlockSpec(memory_space=VMEM)],
        scratch_shapes=[
            VMEM((edge_count, width), BF16),
            VMEM(summed_grad.shape, F32),
            VMEM((edge_count, width), BF16),
            VMEM((width, width), BF16),
            VMEM((edge_count, width), BF16),
            VMEM((width // LANES, EDGE_BLOCK, LANES), F32),
            pltpu.SemaphoreType.DMA((2 + 2 * steps,)),
            pltpu.SemaphoreType.DMA((steps,)),
        ],
        compiler_params=params(24),
        cost_estimate=cost(1, 1),
        name="edges",
    )(*[pinned(value) for value in (cot, summed_grad, pre_grad, w_edge_in)], *tokens)


def local(
    h_in,
    edge_in,
    new_index,
    source,
    w_edge_in,
    w_edge_out,
    w_node_in,
    w_node_out,
    cot_nodes,
    cot_edges,
):
    _, cell_count, width = h_in.shape
    edge_count = source.shape[1]
    fan_in = edge_count // cell_count
    part_count = lax.axis_size("dom")
    geom_count = lax.axis_size("geom")
    capacity = cell_count // part_count + cell_count // part_count // 2
    chunks = width // LANES
    block_rows = chunks * capacity
    scale = 1.0 / math.sqrt(geom_count * part_count * cell_count * fan_in)
    part = lax.axis_index("dom")
    geom = lax.axis_index("geom")
    scal = [part, geom % 2, part % 2, part // 2]
    geom = geom // 2
    for _ in range(1, geom_count.bit_length() - 1):
        scal.append(geom % 2)
        geom = geom // 2
    scal = jnp.stack(scal).astype(jnp.int32)
    edges = edge_in[0]
    cot = cot_edges[0]

    sends = pl.pallas_call(
        functools.partial(pack_kernel, part_count, capacity),
        out_shape=[shape((block_rows + 16, LANES))] * part_count + [near_shape((8, LANES), F32)],
        in_specs=[scalars()] + [pl.BlockSpec(memory_space=pltpu.HBM)] * 2,
        out_specs=whole(part_count + 1),
        scratch_shapes=[
            VMEM((cell_count, width), BF16),
            VMEM((1, cell_count), jnp.int32),
            pltpu.SemaphoreType.DMA((2,)),
        ],
        compiler_params=params(24),
        name="pack",
    )(scal, pinned(h_in[0]), pinned(new_index))
    prepared = run_prep(
        fan_in,
        cell_count,
        scal,
        source,
        edges,
        cot_nodes[0],
        cot,
        w_edge_in,
        w_edge_out,
        w_node_in,
        w_node_out,
        sends[part_count],
    )
    got = {0: sends[0]}
    for step in send_order(part_count):
        got[step] = shift(sends[step], step)
    nodes, low, high, ids = pl.pallas_call(
        functools.partial(unpack_kernel, part_count, capacity),
        out_shape=[
            shape((cell_count, width)),
            shape((HB, width)),
            shape((HB, width)),
            shape((part_count * 16, LANES)),
        ],
        in_specs=whole(part_count) + [scalars()] + whole(1),
        out_specs=whole(4),
        scratch_shapes=[
            VMEM((part_count * LANES, width), BF16),
            VMEM((cell_count, part_count * LANES), BF16),
        ],
        compiler_params=params(24),
        name="unpack",
    )(*[got[step] for step in range(part_count)], scal, prepared[-1])
    low = neighbour(low, 0)
    high = neighbour(high, 1)

    (
        edge_new,
        node_new,
        pre_grad,
        summed_grad,
        sent,
        received,
        base,
        keep,
        send,
    ) = run_main(fan_in, scale, scal, nodes, low, high, prepared[:-1])
    low, high, node_grad, rim = pl.pallas_call(
        cell_kernel,
        out_shape=[
            near_shape((HB, width)),
            near_shape((HB, width)),
            near_shape((cell_count, width)),
            near_shape((2 * HB, width), F32),
        ],
        in_specs=[scalars()] + whole(4),
        out_specs=whole(4),
        compiler_params=params(24),
        cost_estimate=cost(3 * cell_count * width * width, 3 * MIB),
        name="cells",
    )(scal, sent, received, base, prepared[3])
    low = neighbour(low, 0)
    high = neighbour(high, 1)
    *returning, token = pl.pallas_call(
        functools.partial(return_kernel, part_count, capacity),
        out_shape=[near_shape((block_rows, LANES))] * part_count + [near_shape((8, LANES), F32)],
        in_specs=[scalars()] + whole(5),
        out_specs=whole(part_count + 1),
        compiler_params=params(24),
        cost_estimate=cost(1, 1),
        name="returning",
    )(scal, node_grad, rim, low, high, ids)
    *begun, token = begin_weights(
        scal, keep, swap(send, "geom", 1), geom_count, part_count, token
    )

    grad_edge, edge_token = run_edges(
        fan_in, cot, summed_grad, pre_grad, w_edge_in, token
    )
    back = {0: returning[0]}
    for step in send_order(part_count):
        back[step] = shift(returning[step], -step)
    early = [back[step] for step in send_order(part_count)]
    ends, end = pair_weights(
        scal, *begun, geom_count, part_count, (early[:FIRST], early[:SECOND])
    )
    grad_in, late = pl.pallas_call(
        functools.partial(finish_kernel, part_count, capacity),
        out_shape=[shape((cell_count, width)), near_shape((8, LANES), F32)],
        in_specs=[scalars()] + whole(1 + part_count),
        out_specs=whole(2),
        scratch_shapes=[
            VMEM((part_count * LANES, width), BF16),
            VMEM((part_count * LANES, cell_count), BF16),
        ],
        compiler_params=params(24),
        name="finish",
    )(scal, new_index, *[back[step] for step in range(part_count)])
    weight_grads = reduce_weights(scal, ends, end, geom_count, part_count, edge_token, late)
    return (node_new[None], edge_new[None], grad_in[None], grad_edge[None], weight_grads)


def solution(mesh):
    return jax.shard_map(
        local,
        mesh=mesh,
        in_specs=(
            P("geom", "dom", None),
            P("geom", "dom", None),
            P("geom", "dom"),
            P("geom", "dom"),
            P(),
            P(),
            P(),
            P(),
            P("geom", "dom", None),
            P("geom", "dom", None),
        ),
        out_specs=(
            P("geom", "dom", None),
            P("geom", "dom", None),
            P("geom", "dom", None),
            P("geom", "dom", None),
            P("dom", None),
        ),
        check_vma=False,
    )
```

```python
import functools
import math

import jax
import jax.numpy as jnp
from jax import lax
from jax.experimental import pallas as pl
from jax.experimental.pallas import tpu as pltpu
from jax.sharding import PartitionSpec as P

HB = 64
LANES = 128
EDGE_BLOCK = 512
MIB = 1024 * 1024
MAIN_LIMIT = 25
FIRST, SECOND = 3, 7
PREP_LIMIT = 20
PART, CORE, DOM_BIT, OWNER, GEOM_BITS = range(5)
F32 = jnp.float32
BF16 = jnp.bfloat16
VMEM = pltpu.VMEM


class Places:
    def __getitem__(self, at):
        part = lax.axis_index("dom")
        geom = lax.axis_index("geom")
        if at == PART:
            return part
        if at == CORE:
            return geom & 1
        if at == DOM_BIT:
            return part & 1
        if at == OWNER:
            return part >> 1
        return (geom >> (at - GEOM_BITS + 1)) & 1


def placed(kernel, *fixed):
    return lambda *refs: kernel(*fixed, Places(), *refs)


def dot_nn(left, right):
    return lax.dot_general(left, right, (((1,), (0,)), ((), ())), preferred_element_type=F32)


def dot_nt(left, right):
    return lax.dot_general(left, right, (((1,), (1,)), ((), ())), preferred_element_type=F32)


def dot_tn(left, right):
    return lax.dot_general(left, right, (((0,), (0,)), ((), ())), preferred_element_type=F32)


def iota(shape, axis):
    return lax.broadcasted_iota(jnp.int32, shape, axis)


def hot(condition):
    return jnp.where(condition, 1.0, 0.0).astype(BF16)


def sigmoid(values):
    return 0.5 * jnp.tanh(0.5 * values) + 0.5


def normalize(values):
    center = values - jnp.mean(values, axis=-1, keepdims=True)
    inverse = lax.rsqrt(jnp.mean(center * center, axis=-1, keepdims=True) + 1e-05)
    return center * inverse, inverse


def normalize_back(normed, inverse, upstream):
    return inverse * (
        upstream
        - jnp.mean(upstream, axis=-1, keepdims=True)
        - normed * jnp.mean(upstream * normed, axis=-1, keepdims=True)
    )


def slots_of(index, me, part_count, cell_count):
    owner = jnp.zeros_like(index)
    for part in range(1, part_count):
        owner = owner + jnp.where(index >= part * cell_count, 1, 0)
    row = index - owner * cell_count
    ahead = owner - me
    ahead = jnp.where(ahead < 0, ahead + part_count, ahead)
    high = -(-part_count // 16) * 16
    member = hot(iota((high, cell_count), 0) == ahead)
    before = hot(iota((cell_count, cell_count), 0) < iota((cell_count, cell_count), 1))
    rank = jnp.sum(member.astype(F32) * dot_nn(member, before), axis=0, keepdims=True)
    return ahead * LANES + rank.astype(jnp.int32), row


def pack_kernel(part_count, capacity, scal, h_hbm, index_hbm, *refs):
    outs = refs[:-3]
    h_ref, index_ref, sems = refs[-3:]
    cell_count, width = h_ref.shape
    loads = [
        pltpu.make_async_copy(index_hbm, index_ref, sems.at[0]),
        pltpu.make_async_copy(h_hbm, h_ref, sems.at[1]),
    ]
    for load in loads:
        load.start()
    loads[0].wait()
    chunks = width // LANES
    slot, row = slots_of(index_ref[...], scal[PART], part_count, cell_count)
    kind = iota((16, cell_count), 0)
    coded = jnp.where(
        kind == 0, row >> 8, jnp.where(kind == 1, row & 255, jnp.where(kind == 2, 1, 0))
    )
    coded = coded.astype(F32).astype(BF16)
    loads[1].wait()
    cells = h_ref[...]
    for step in range(part_count):
        pick = hot(iota((LANES, cell_count), 0) + step * LANES == slot)
        rows = dot_nn(pick, cells).astype(BF16)
        for chunk in range(chunks):
            outs[step][chunk * capacity : (chunk + 1) * capacity, :] = rows[
                :capacity, chunk * LANES : (chunk + 1) * LANES
            ]
        outs[step][chunks * capacity :, :] = dot_nt(coded, pick).astype(BF16)
    outs[part_count][...] = jnp.zeros(outs[part_count].shape, F32)


def place(ids, cell_count):
    ids = ids.astype(F32)
    spot = ids[0:1] * 256.0 + ids[1:2] + (ids[2:3] - 1.0) * 65536.0
    return hot(iota((cell_count, LANES), 0) == spot.astype(jnp.int32))


def unpack_kernel(part_count, capacity, scal, *refs):
    blocks = refs[:part_count]
    _, nodes_ref, low_ref, high_ref, ids_ref, rows_ref, hot_ref = refs[part_count:]
    cell_count, width = nodes_ref.shape
    chunks = width // LANES
    for step in range(part_count):
        base = step * LANES
        ids = blocks[step][chunks * capacity :, :]
        ids_ref[step * 16 : (step + 1) * 16, :] = ids
        hot_ref[:, base : base + LANES] = place(ids, cell_count)
        for chunk in range(chunks):
            rows_ref[base : base + capacity, chunk * LANES : (chunk + 1) * LANES] = blocks[step][
                chunk * capacity : (chunk + 1) * capacity, :
            ]
        if capacity < LANES:
            rows_ref[base + capacity : base + LANES, :] = jnp.zeros(
                (LANES - capacity, width), BF16
            )
    nodes = dot_nn(hot_ref[...], rows_ref[...]).astype(BF16)
    nodes_ref[...] = nodes
    odd = scal[DOM_BIT] == 1
    head = nodes[:HB]
    tail = nodes[cell_count - HB :]
    low_ref[...] = jnp.where(odd, head, tail)
    high_ref[...] = jnp.where(odd, tail, head)


def spread_rows(wide, base, rows, fan_in):
    count, width = rows.shape
    chunks = width // LANES
    for chunk in range(chunks):
        for at in range(fan_in):
            wide[base + chunk, pl.ds(at, count, stride=fan_in), :] = rows[
                :, chunk * LANES : (chunk + 1) * LANES
            ]
    return jnp.concatenate([wide[base + chunk] for chunk in range(chunks)], axis=1)


def collect_rows(wide, base, values, fan_in):
    count = values.shape[0] // fan_in
    sums = []
    for chunk in range(values.shape[1] // LANES):
        wide[base + chunk] = values[:, chunk * LANES : (chunk + 1) * LANES]
        total = wide[base + chunk, pl.ds(0, count, stride=fan_in), :]
        for at in range(1, fan_in):
            total = total + wide[base + chunk, pl.ds(at, count, stride=fan_in), :]
        sums.append(total)
    return jnp.concatenate(sums, axis=1)


def prep_kernel(
    fan_in,
    cell_count,
    scal,
    source_hbm,
    edges_hbm,
    cot_nodes_hbm,
    cot_edges_hbm,
    w_edge_in_hbm,
    w_edge_out_hbm,
    w_node_in_hbm,
    w_node_out_hbm,
    _,
    edges_ref,
    cot_nodes_ref,
    cot_edges_ref,
    w_edge_in_ref,
    w_edge_out_ref,
    w_node_in_ref,
    w_node_out_ref,
    gather_ref,
    scatter_ref,
    pre_ref,
    token_ref,
    source_ref,
    sems,
):
    edge_count, width = edges_ref.shape
    padded = cell_count + 2 * HB
    cells = EDGE_BLOCK // fan_in
    loads = [
        pltpu.make_async_copy(far, near, sems.at[at])
        for at, (far, near) in enumerate(
            (
                (source_hbm, source_ref),
                (edges_hbm, edges_ref),
                (w_edge_in_hbm, w_edge_in_ref),
                (w_edge_out_hbm, w_edge_out_ref),
                (w_node_in_hbm, w_node_in_ref),
                (w_node_out_hbm, w_node_out_ref),
                (cot_nodes_hbm, cot_nodes_ref),
                (cot_edges_hbm, cot_edges_ref),
            )
        )
    ]
    for load in loads:
        load.start()
    token_ref[...] = jnp.zeros(token_ref.shape, F32)
    loads[0].wait()
    offset = scal[PART] * cell_count - HB

    def hots(step, carry):
        rows = pl.ds(pl.multiple_of(step * EDGE_BLOCK, EDGE_BLOCK), EDGE_BLOCK)
        local = source_ref[:, rows] - offset
        scatter_ref[:, rows] = hot(iota((padded, EDGE_BLOCK), 0) == local)
        local = jnp.transpose(jnp.broadcast_to(local.astype(F32), (LANES, EDGE_BLOCK)))
        local = local.astype(jnp.int32)
        lane = iota((EDGE_BLOCK, LANES), 1)
        for at in range(0, padded, LANES):
            gather_ref[rows, at : at + LANES] = hot(local == lane + at)
        gather_ref[rows, padded:] = hot(
            iota((EDGE_BLOCK, cells), 0) // fan_in == iota((EDGE_BLOCK, cells), 1)
        )
        return carry

    lax.fori_loop(0, edge_count // EDGE_BLOCK, hots, 0)
    loads[1].wait()
    loads[2].wait()

    def first(step, carry):
        rows = pl.ds(pl.multiple_of(step * EDGE_BLOCK, EDGE_BLOCK), EDGE_BLOCK)
        pre_ref[rows, :] = dot_nn(edges_ref[rows, :], w_edge_in_ref[:width, :])
        return carry

    lax.fori_loop(0, edge_count // EDGE_BLOCK, first, 0)
    for load in loads[3:]:
        load.wait()


def main_kernel(
    fan_in,
    scale,
    scal,
    nodes_ref,
    low_ref,
    high_ref,
    edges_ref,
    cot_nodes_ref,
    cot_edges_ref,
    w_edge_in_ref,
    w_edge_out_ref,
    w_node_in_ref,
    w_node_out_ref,
    gather_ref,
    scatter_ref,
    pre_ref,
    edge_new_hbm,
    node_new_hbm,
    pre_grad_hbm,
    summed_grad_hbm,
    sent_ref,
    received_ref,
    base_ref,
    keep_ref,
    send_ref,
    pre_grad_ref,
    summed_grad_ref,
    node_new_ref,
    cells_ref,
    table_ref,
    recv_ref,
    hidden_ref,
    slope_ref,
    normed_ref,
    inverse_ref,
    summed_ref,
    post_grad_ref,
    wide_ref,
    out_sems,
):
    cell_count, width = nodes_ref.shape
    edge_count = edges_ref.shape[0]
    steps = edge_count // EDGE_BLOCK
    padded = cell_count + 2 * HB
    cells = EDGE_BLOCK // fan_in
    half = width // 2
    inner = slice(HB, HB + cell_count)

    odd = scal[DOM_BIT] == 1
    low = low_ref[...]
    high = high_ref[...]
    cells_ref[:HB, :] = jnp.where(odd, low, high)
    cells_ref[inner, :] = nodes_ref[...]
    cells_ref[HB + cell_count :, :] = jnp.where(odd, high, low)
    table_ref[:padded, :] = dot_nn(cells_ref[...], w_edge_in_ref[width : 2 * width, :]).astype(BF16)
    recv_ref[...] = dot_nn(nodes_ref[...], w_edge_in_ref[2 * width :, :]).astype(BF16)

    for step in range(steps):
        spot = slice(step * cells, (step + 1) * cells)
        rows = slice(step * EDGE_BLOCK, (step + 1) * EDGE_BLOCK)
        table_ref[padded : padded + cells, :] = recv_ref[spot, :]
        edges = edges_ref[rows, :]
        pre = pre_ref[rows, :] + dot_nn(gather_ref[rows, :], table_ref[...])
        gate = sigmoid(pre)
        hidden = (pre * gate).astype(BF16)
        hidden_ref[rows, :] = hidden
        slope_ref[rows, :] = (gate * (1.0 + pre * (1.0 - gate))).astype(BF16)
        normed, inverse = normalize(dot_nn(hidden, w_edge_out_ref[...]))
        normed_ref[rows, :] = normed.astype(BF16)
        inverse_ref[rows, :] = inverse
        edge_new = (edges.astype(F32) + normed).astype(BF16)
        post_grad_ref[rows, :] = edge_new
        summed_ref[spot, :] = collect_rows(wide_ref, 0, edge_new.astype(F32), fan_in).astype(BF16)

    edge_store = pltpu.make_async_copy(post_grad_ref, edge_new_hbm, out_sems.at[0])
    edge_store.start()
    nodes = nodes_ref[...]
    summed = summed_ref[...]
    node_pre = dot_nn(nodes, w_node_in_ref[:width, :]) + dot_nn(summed, w_node_in_ref[width:, :])
    node_gate = sigmoid(node_pre)
    node_hidden = (node_pre * node_gate).astype(BF16)
    node_normed, node_inverse = normalize(dot_nn(node_hidden, w_node_out_ref[...]))
    node_new_ref[...] = (nodes.astype(F32) + node_normed).astype(BF16)
    node_store = pltpu.make_async_copy(node_new_ref, node_new_hbm, out_sems.at[1])
    node_store.start()
    upstream = cot_nodes_ref[...].astype(F32)
    node_post_grad = normalize_back(node_normed, node_inverse, upstream).astype(BF16)
    node_slope = node_gate * (1.0 + node_pre * (1.0 - node_gate))
    node_pre_grad = (dot_nt(node_post_grad, w_node_out_ref[...]) * node_slope).astype(BF16)
    summed_grad = dot_nt(node_pre_grad, w_node_in_ref[width:, :])
    summed_grad_ref[...] = summed_grad
    summed_store = pltpu.make_async_copy(summed_grad_ref, summed_grad_hbm, out_sems.at[2])
    summed_store.start()
    base_ref[...] = upstream + dot_nt(node_pre_grad, w_node_in_ref[:width, :])
    edge_store.wait()
    for step in range(steps):
        spot = slice(step * cells, (step + 1) * cells)
        rows = slice(step * EDGE_BLOCK, (step + 1) * EDGE_BLOCK)
        base = (step % 2) * (width // LANES)
        upstream = cot_edges_ref[rows, :].astype(F32) + spread_rows(
            wide_ref, base, summed_grad_ref[spot, :], fan_in
        )
        post_grad = normalize_back(
            normed_ref[rows, :].astype(F32), inverse_ref[rows, :], upstream
        )
        post_grad = post_grad.astype(BF16)
        post_grad_ref[rows, :] = post_grad
        pre_grad = dot_nt(post_grad, w_edge_out_ref[...]) * slope_ref[rows, :].astype(F32)
        pre_grad = pre_grad.astype(BF16)
        pre_grad_ref[rows, :] = pre_grad
        received_ref[spot, :] = collect_rows(
            wide_ref, base, pre_grad.astype(F32), fan_in
        ).astype(BF16)

    pre_store = pltpu.make_async_copy(pre_grad_ref, pre_grad_hbm, out_sems.at[3])
    pre_store.start()
    first = scal[CORE] == 0

    def put(place_at, value):
        value = (value * scale).astype(BF16)
        rows = slice(place_at * width, (place_at + 1) * width)
        left = value[:, :half]
        right = value[:, half:]
        keep_ref[rows, :] = jnp.where(first, left, right)
        send_ref[rows, :] = jnp.where(first, right, left)

    sent = dot_nn(scatter_ref[...], pre_grad_ref[...]).astype(BF16)
    sent_ref[...] = sent
    put(0, dot_tn(edges_ref[...], pre_grad_ref[...]))
    put(1, dot_tn(cells_ref[...], sent))
    put(2, dot_tn(nodes, received_ref[...]))
    put(3, dot_tn(hidden_ref[...], post_grad_ref[...]))
    put(4, dot_tn(nodes, node_pre_grad))
    put(5, dot_tn(summed, node_pre_grad))
    put(6, dot_tn(node_hidden, node_post_grad))
    node_store.wait()
    summed_store.wait()
    pre_store.wait()


def cell_kernel(
    scal,
    sent_ref,
    received_ref,
    base_ref,
    w_edge_in_ref,
    low_ref,
    high_ref,
    node_grad_ref,
    rim_ref,
):
    cell_count, width = received_ref.shape
    sender = dot_nt(sent_ref[...], w_edge_in_ref[width : 2 * width, :])
    odd = scal[DOM_BIT] == 1
    to_prev = sender[:HB].astype(BF16)
    to_next = sender[HB + cell_count :].astype(BF16)
    low_ref[...] = jnp.where(odd, to_prev, to_next)
    high_ref[...] = jnp.where(odd, to_next, to_prev)
    node_grad = (
        base_ref[...]
        + dot_nt(received_ref[...], w_edge_in_ref[2 * width :, :])
        + sender[HB : HB + cell_count]
    )
    node_grad_ref[...] = node_grad.astype(BF16)
    rim_ref[:HB, :] = node_grad[:HB]
    rim_ref[HB:, :] = node_grad[cell_count - HB :]


def edge_kernel(
    fan_in,
    cot_hbm,
    summed_grad_hbm,
    pre_grad_hbm,
    w_edge_in_hbm,
    _,
    grad_edge_hbm,
    token_ref,
    cot_ref,
    summed_grad_ref,
    pre_grad_ref,
    w_edge_ref,
    grad_edge_ref,
    wide_ref,
    in_sems,
    out_sems,
):
    edge_count, width = cot_ref.shape
    steps = edge_count // EDGE_BLOCK
    cells = EDGE_BLOCK // fan_in
    loads = [
        pltpu.make_async_copy(w_edge_in_hbm.at[:width, :], w_edge_ref, in_sems.at[0]),
        pltpu.make_async_copy(summed_grad_hbm, summed_grad_ref, in_sems.at[1]),
    ]
    for step in range(steps):
        rows = slice(step * EDGE_BLOCK, (step + 1) * EDGE_BLOCK)
        for at, (far, near) in enumerate(((cot_hbm, cot_ref), (pre_grad_hbm, pre_grad_ref))):
            loads.append(
                pltpu.make_async_copy(
                    far.at[rows, :], near.at[rows, :], in_sems.at[2 + 2 * step + at]
                )
            )
    for load in loads:
        load.start()
    token_ref[...] = jnp.zeros(token_ref.shape, F32)
    loads[0].wait()
    loads[1].wait()
    stores = []
    for step in range(steps):
        rows = slice(step * EDGE_BLOCK, (step + 1) * EDGE_BLOCK)
        loads[2 + 2 * step].wait()
        loads[3 + 2 * step].wait()
        upstream = cot_ref[rows, :].astype(F32) + spread_rows(
            wide_ref, 0, summed_grad_ref[step * cells : (step + 1) * cells, :], fan_in
        )
        grad_edge_ref[rows, :] = (
            upstream + dot_nt(pre_grad_ref[rows, :], w_edge_ref[...])
        ).astype(BF16)
        stores.append(
            pltpu.make_async_copy(
                grad_edge_ref.at[rows, :], grad_edge_hbm.at[rows, :], out_sems.at[step]
            )
        )
        stores[-1].start()
    for store in stores:
        store.wait()


def return_kernel(
    part_count,
    capacity,
    scal,
    node_grad_ref,
    rim_ref,
    low_ref,
    high_ref,
    ids_ref,
    *outs,
):
    cell_count, width = node_grad_ref.shape
    chunks = width // LANES
    outs[part_count][...] = jnp.zeros(outs[part_count].shape, F32)
    odd = scal[DOM_BIT] == 1
    low = low_ref[...].astype(F32)
    high = high_ref[...].astype(F32)
    first = rim_ref[:HB, :] + jnp.where(odd, low, high)
    last = rim_ref[HB:, :] + jnp.where(odd, high, low)
    grad = jnp.concatenate(
        [first.astype(BF16), node_grad_ref[HB : cell_count - HB, :], last.astype(BF16)], axis=0
    )
    for step in range(part_count):
        pick = place(ids_ref[step * 16 : (step + 1) * 16, :], cell_count)
        rows = dot_tn(pick, grad).astype(BF16)
        for chunk in range(chunks):
            outs[step][chunk * capacity : (chunk + 1) * capacity, :] = rows[
                :capacity, chunk * LANES : (chunk + 1) * LANES
            ]


def finish_kernel(part_count, capacity, scal, index_ref, *refs):
    blocks = refs[:part_count]
    out_ref, token_ref, rows_ref, pick_ref = refs[part_count:]
    cell_count, width = out_ref.shape
    chunks = width // LANES
    token_ref[...] = jnp.zeros(token_ref.shape, F32)
    slot, _ = slots_of(index_ref[...], scal[PART], part_count, cell_count)
    for step in range(part_count):
        base = step * LANES
        pick_ref[base : base + LANES, :] = hot(iota((LANES, cell_count), 0) + base == slot)
        for chunk in range(chunks):
            rows_ref[base : base + capacity, chunk * LANES : (chunk + 1) * LANES] = blocks[step][
                chunk * capacity : (chunk + 1) * capacity, :
            ]
        if capacity < LANES:
            rows_ref[base + capacity : base + LANES, :] = jnp.zeros(
                (LANES - capacity, width), BF16
            )
    out_ref[...] = dot_tn(pick_ref[...], rows_ref[...]).astype(BF16)


def shape(dims, kind=BF16):
    return jax.ShapeDtypeStruct(dims, kind)


def whole(count):
    return [pl.BlockSpec(memory_space=VMEM)] * count


def params(limit):
    return pltpu.CompilerParams(vmem_limit_bytes=limit * MIB)


def cost(flops, bytes_accessed):
    return pl.CostEstimate(flops=flops, bytes_accessed=bytes_accessed, transcendentals=0)


def full(dims):
    return pl.BlockSpec(dims, lambda step: (0,) * len(dims))


def rows_spec(rows, columns):
    return pl.BlockSpec((rows, columns), lambda step: (step, 0))


def swap(value, axis, bit):
    count = lax.axis_size(axis)
    return lax.ppermute(value, axis, [(at, at ^ bit) for at in range(count)])


def take(value, kind, bit):
    if kind == "columns":
        half = value.shape[2] // 2
        parts = value[:, :, :half], value[:, :, half:]
    else:
        pairs = value.reshape((value.shape[0] // 2, 2) + value.shape[1:])
        parts = pairs[:, 0], pairs[:, 1]
    return jnp.where(bit == 0, parts[0], parts[1])


def core_kernel(kinds, bits, scal, keep_ref, got_ref, _, *refs):
    total_ref, left_ref, right_ref, token_ref = refs
    token_ref[...] = jnp.zeros(token_ref.shape, F32)
    total = (keep_ref[...].astype(F32) + got_ref[...].astype(F32)).astype(BF16)
    total = total.reshape(total_ref.shape)
    total_ref[...] = total
    half = total.shape[1] // 2
    left_ref[...] = take(total[:, :half], kinds[0], 1 - scal[bits[0]])
    right_ref[...] = take(total[:, half:], kinds[1], 1 - scal[bits[1]])


def stage_kernel(part, kinds, bits, scal, value_ref, got_ref, *refs):
    total_ref, send_ref = refs[-2:]
    value = value_ref[...]
    if part is not None:
        half = value.shape[1] // 2
        value = value[:, part * half : (part + 1) * half]
    mine = take(value, kinds[0], scal[bits[0]]).astype(F32)
    total = (mine + got_ref[...].astype(F32)).astype(BF16)
    total_ref[...] = total
    send_ref[...] = take(total, kinds[1], 1 - scal[bits[1]])


def split_kernel(kinds, bits, scal, *refs):
    left_ref, left_got_ref, right_ref, right_got_ref = refs[:4]
    outs = refs[-(left_got_ref.shape[0]) :]
    left = take(left_ref[...], kinds[0], scal[bits[0]]).astype(F32)
    left = (left + left_got_ref[...].astype(F32)).astype(BF16)
    right = take(right_ref[...], kinds[1], scal[bits[1]]).astype(F32)
    right = (right + right_got_ref[...].astype(F32)).astype(BF16)
    half = left.shape[1]
    owner = scal[OWNER]
    for other, out in enumerate(outs):
        for at in range(len(outs)):

            @pl.when((owner ^ other) == at)
            def _(out=out, at=at):
                out[:half, :] = left[at]
                out[half:, :] = right[at]


def sum_kernel(*refs):
    total = refs[0][...].astype(F32)
    for ref in refs[1:-2]:
        total = total + ref[...].astype(F32)
    refs[-1][...] = total.astype(BF16)


def join_kernel(at, scal, mine_ref, theirs_ref, out_ref):
    mine = mine_ref[...]
    theirs = theirs_ref[...]
    columns = mine.shape[1]
    first = scal[at] == 0
    out_ref[:, :columns] = jnp.where(first, mine, theirs).astype(out_ref.dtype)
    out_ref[:, columns:] = jnp.where(first, theirs, mine).astype(out_ref.dtype)


def local_call(kernel, outs, name, *operands):
    return pl.pallas_call(
        kernel,
        out_shape=[near_shape(*out) for out in outs],
        in_specs=whole(len(operands)),
        out_specs=whole(len(outs)),
        compiler_params=params(24),
        name=name,
    )(*operands)


def halved(dims, kind):
    if kind == "columns":
        return (dims[0], dims[1], dims[2] // 2)
    return (dims[0] // 2,) + dims[1:]


def chains(geom_count):
    columns = []
    bit = 2
    while bit < geom_count:
        columns.append(("columns", "geom", bit, GEOM_BITS + len(columns)))
        bit *= 2
    owner = ("owners", "dom", 1, DOM_BIT)
    return columns + [owner], [owner] + columns


def begin_weights(keep, got, geom_count, part_count, *tokens):
    left, right = chains(geom_count)
    rows, width = keep.shape
    dims = (part_count, rows // part_count, width)
    piece = (part_count, rows // part_count // 2, width)
    return local_call(
        placed(core_kernel, (left[0][0], right[0][0]), (left[0][3], right[0][3])),
        [
            (dims,),
            (halved(piece, left[0][0]),),
            (halved(piece, right[0][0]),),
            ((8, LANES), F32),
        ],
        "core",
        keep,
        got,
        *tokens,
    )


def pair_weights(total, send_left, send_right, geom_count, part_count, early):
    rows = total.shape[1]
    ends = []
    for part, chain, send in zip((0, 1), chains(geom_count), (send_left, send_right)):
        value = total
        now = (part_count, rows // 2, total.shape[2])
        for at in range(len(chain) - 1):
            kind, axis, bit, place_at = chain[at]
            follow = chain[at + 1]
            now = halved(now, kind)
            value, send = local_call(
                placed(
                    stage_kernel,
                    part if at == 0 else None,
                    (kind, follow[0]),
                    (place_at, follow[3]),
                ),
                [(now,), (halved(now, follow[0]),)],
                "stage",
                value,
                swap(send, axis, bit),
                *early[part],
            )
        if len(chain) == 1:
            half = rows // 2
            value = value[:, part * half : (part + 1) * half]
        ends.append((value, swap(send, chain[-1][1], chain[-1][2])))
        end = halved(now, chain[-1][0])
    return ends, end


def reduce_weights(ends, end, geom_count, part_count, early, late):
    left, right = chains(geom_count)
    out = (2 * end[1], end[2])
    owners = part_count // 2
    pieces = local_call(
        placed(split_kernel, (left[-1][0], right[-1][0]), (left[-1][3], right[-1][3])),
        [(out,)] * owners,
        "split",
        *ends[0],
        *ends[1],
        early,
    )
    got = [swap(pieces[other], "dom", 2 * other) for other in range(owners - 1, 0, -1)]
    total = pl.pallas_call(
        sum_kernel,
        out_shape=near_shape(out),
        in_specs=whole(owners + 1),
        out_specs=pl.BlockSpec(memory_space=VMEM),
        compiler_params=params(24),
        name="sum",
    )(pieces[0], *got, late)
    for place_at, bit in [(link[3], link[2]) for link in left[-2::-1]] + [(CORE, 1)]:
        out = (out[0], 2 * out[1])
        last = bit == 1
        total = pl.pallas_call(
            placed(join_kernel, place_at),
            out_shape=shape(out, F32) if last else near_shape(out),
            in_specs=whole(2),
            out_specs=pl.BlockSpec(memory_space=VMEM),
            compiler_params=params(24),
            name="join",
        )(total, swap(total, "geom", bit))
    return total


def shift(value, steps):
    count = lax.axis_size("dom")
    return lax.ppermute(value, "dom", [(at, (at + steps) % count) for at in range(count)])


def neighbour(value, first):
    count = lax.axis_size("dom")
    pairs = [(at, at + 1) for at in range(first, count - 1, 2)]
    return lax.ppermute(value, "dom", pairs + [(right, left) for left, right in pairs])


def send_order(part_count):
    return sorted(range(1, part_count), key=lambda at: (-min(at, part_count - at), at))


def pinned(value):
    return pltpu.with_memory_space_constraint(value, pltpu.HBM)


def near_shape(dims, kind=BF16):
    return pltpu.VMEM(dims, kind)


def run_prep(
    fan_in,
    cell_count,
    source,
    edges,
    cot_nodes,
    cot_edges,
    w_edge_in,
    w_edge_out,
    w_node_in,
    w_node_out,
    token,
):
    edge_count = edges.shape[0]
    padded = cell_count + 2 * HB
    cells = EDGE_BLOCK // fan_in
    near = pl.BlockSpec(memory_space=VMEM)
    return pl.pallas_call(
        placed(prep_kernel, fan_in, cell_count),
        out_shape=[
            near_shape(like.shape)
            for like in (edges, cot_nodes, cot_edges, w_edge_in, w_edge_out, w_node_in, w_node_out)
        ]
        + [
            near_shape((edge_count, padded + cells)),
            near_shape((padded, edge_count)),
            near_shape(edges.shape, F32),
            near_shape((8, LANES), F32),
        ],
        in_specs=[pl.BlockSpec(memory_space=pltpu.HBM)] * 8 + [near],
        out_specs=[near] * 11,
        scratch_shapes=[VMEM(source.shape, jnp.int32), pltpu.SemaphoreType.DMA((8,))],
        compiler_params=params(PREP_LIMIT),
        cost_estimate=cost(4 * edge_count * edges.shape[1] ** 2, 20 * MIB),
        name="prep",
    )(
        *[
            pinned(value)
            for value in (
                source,
                edges,
                cot_nodes,
                cot_edges,
                w_edge_in,
                w_edge_out,
                w_node_in,
                w_node_out,
            )
        ],
        token,
    )


def run_main(fan_in, scale, nodes, low, high, prepared):
    edge_count, width = prepared[0].shape
    cell_count = nodes.shape[0]
    cells = EDGE_BLOCK // fan_in
    padded = cell_count + 2 * HB
    far = pl.BlockSpec(memory_space=pltpu.HBM)
    near = pl.BlockSpec(memory_space=VMEM)
    by_edge = (edge_count, width)
    by_cell = (cell_count, width)
    weights = (7 * width, width // 2)
    return pl.pallas_call(
        placed(main_kernel, fan_in, scale),
        out_shape=[
            shape(by_edge),
            shape(by_cell),
            pltpu.HBM(by_edge, BF16),
            pltpu.HBM(by_cell, F32),
            near_shape((padded, width)),
            near_shape(by_cell),
            near_shape(by_cell, F32),
            near_shape(weights),
            near_shape(weights),
        ],
        in_specs=[near] * 13,
        out_specs=[far] * 4 + [near] * 5,
        scratch_shapes=[
            VMEM(by_edge, BF16),
            VMEM(by_cell, F32),
            VMEM(by_cell, BF16),
            VMEM((padded, width), BF16),
            VMEM((padded + cells, width), BF16),
            VMEM(by_cell, BF16),
            VMEM(by_edge, BF16),
            VMEM(by_edge, BF16),
            VMEM(by_edge, BF16),
            VMEM((edge_count, 1), F32),
            VMEM(by_cell, BF16),
            VMEM(by_edge, BF16),
            VMEM((2 * width // LANES, EDGE_BLOCK, LANES), F32),
            pltpu.SemaphoreType.DMA((4,)),
        ],
        compiler_params=params(MAIN_LIMIT),
        cost_estimate=cost(28 * edge_count * width * width, 16 * MIB),
        name="main",
    )(nodes, low, high, *prepared)


def run_edges(fan_in, cot, summed_grad, pre_grad, w_edge_in, *tokens):
    edge_count, width = cot.shape
    steps = edge_count // EDGE_BLOCK
    far = pl.BlockSpec(memory_space=pltpu.HBM)
    return pl.pallas_call(
        functools.partial(edge_kernel, fan_in),
        out_shape=[shape((edge_count, width)), near_shape((8, LANES), F32)],
        in_specs=[far] * 4 + whole(len(tokens)),
        out_specs=[far, pl.BlockSpec(memory_space=VMEM)],
        scratch_shapes=[
            VMEM((edge_count, width), BF16),
            VMEM(summed_grad.shape, F32),
            VMEM((edge_count, width), BF16),
            VMEM((width, width), BF16),
            VMEM((edge_count, width), BF16),
            VMEM((width // LANES, EDGE_BLOCK, LANES), F32),
            pltpu.SemaphoreType.DMA((2 + 2 * steps,)),
            pltpu.SemaphoreType.DMA((steps,)),
        ],
        compiler_params=params(24),
        cost_estimate=cost(1, 1),
        name="edges",
    )(*[pinned(value) for value in (cot, summed_grad, pre_grad, w_edge_in)], *tokens)


def local(
    h_in,
    edge_in,
    new_index,
    source,
    w_edge_in,
    w_edge_out,
    w_node_in,
    w_node_out,
    cot_nodes,
    cot_edges,
):
    _, cell_count, width = h_in.shape
    edge_count = source.shape[1]
    fan_in = edge_count // cell_count
    part_count = lax.axis_size("dom")
    geom_count = lax.axis_size("geom")
    capacity = cell_count // part_count + cell_count // part_count // 2
    chunks = width // LANES
    block_rows = chunks * capacity
    scale = 1.0 / math.sqrt(geom_count * part_count * cell_count * fan_in)
    edges = edge_in[0]
    cot = cot_edges[0]

    sends = pl.pallas_call(
        placed(pack_kernel, part_count, capacity),
        out_shape=[shape((block_rows + 16, LANES))] * part_count + [near_shape((8, LANES), F32)],
        in_specs=[pl.BlockSpec(memory_space=pltpu.HBM)] * 2,
        out_specs=whole(part_count + 1),
        scratch_shapes=[
            VMEM((cell_count, width), BF16),
            VMEM((1, cell_count), jnp.int32),
            pltpu.SemaphoreType.DMA((2,)),
        ],
        compiler_params=params(24),
        name="pack",
    )(pinned(h_in[0]), pinned(new_index))
    prepared = run_prep(
        fan_in,
        cell_count,
        source,
        edges,
        cot_nodes[0],
        cot,
        w_edge_in,
        w_edge_out,
        w_node_in,
        w_node_out,
        sends[part_count],
    )
    got = {0: sends[0]}
    for step in send_order(part_count):
        got[step] = shift(sends[step], step)
    nodes, low, high, ids = pl.pallas_call(
        placed(unpack_kernel, part_count, capacity),
        out_shape=[
            shape((cell_count, width)),
            shape((HB, width)),
            shape((HB, width)),
            shape((part_count * 16, LANES)),
        ],
        in_specs=whole(part_count + 1),
        out_specs=whole(4),
        scratch_shapes=[
            VMEM((part_count * LANES, width), BF16),
            VMEM((cell_count, part_count * LANES), BF16),
        ],
        compiler_params=params(24),
        name="unpack",
    )(*[got[step] for step in range(part_count)], prepared[-1])
    low = neighbour(low, 0)
    high = neighbour(high, 1)

    (
        edge_new,
        node_new,
        pre_grad,
        summed_grad,
        sent,
        received,
        base,
        keep,
        send,
    ) = run_main(fan_in, scale, nodes, low, high, prepared[:-1])
    low, high, node_grad, rim = pl.pallas_call(
        placed(cell_kernel),
        out_shape=[
            near_shape((HB, width)),
            near_shape((HB, width)),
            near_shape((cell_count, width)),
            near_shape((2 * HB, width), F32),
        ],
        in_specs=whole(4),
        out_specs=whole(4),
        compiler_params=params(24),
        cost_estimate=cost(3 * cell_count * width * width, 3 * MIB),
        name="cells",
    )(sent, received, base, prepared[3])
    low = neighbour(low, 0)
    high = neighbour(high, 1)
    *returning, token = pl.pallas_call(
        placed(return_kernel, part_count, capacity),
        out_shape=[near_shape((block_rows, LANES))] * part_count + [near_shape((8, LANES), F32)],
        in_specs=whole(5),
        out_specs=whole(part_count + 1),
        compiler_params=params(24),
        cost_estimate=cost(1, 1),
        name="returning",
    )(node_grad, rim, low, high, ids)
    *begun, token = begin_weights(
        keep, swap(send, "geom", 1), geom_count, part_count, token
    )

    grad_edge, edge_token = run_edges(
        fan_in, cot, summed_grad, pre_grad, w_edge_in, token
    )
    back = {0: returning[0]}
    for step in send_order(part_count):
        back[step] = shift(returning[step], -step)
    early = [back[step] for step in send_order(part_count)]
    ends, end = pair_weights(
        *begun, geom_count, part_count, (early[:FIRST], early[:SECOND])
    )
    grad_in, late = pl.pallas_call(
        placed(finish_kernel, part_count, capacity),
        out_shape=[shape((cell_count, width)), near_shape((8, LANES), F32)],
        in_specs=whole(1 + part_count),
        out_specs=whole(2),
        scratch_shapes=[
            VMEM((part_count * LANES, width), BF16),
            VMEM((part_count * LANES, cell_count), BF16),
        ],
        compiler_params=params(24),
        name="finish",
    )(new_index, *[back[step] for step in range(part_count)])
    weight_grads = reduce_weights(ends, end, geom_count, part_count, edge_token, late)
    return (node_new[None], edge_new[None], grad_in[None], grad_edge[None], weight_grads)


def solution(mesh):
    return jax.shard_map(
        local,
        mesh=mesh,
        in_specs=(
            P("geom", "dom", None),
            P("geom", "dom", None),
            P("geom", "dom"),
            P("geom", "dom"),
            P(),
            P(),
            P(),
            P(),
            P("geom", "dom", None),
            P("geom", "dom", None),
        ),
        out_specs=(
            P("geom", "dom", None),
            P("geom", "dom", None),
            P("geom", "dom", None),
            P("geom", "dom", None),
            P("dom", None),
        ),
        check_vma=False,
    )
```

```python
import functools
import math

import jax
import jax.numpy as jnp
from jax import lax
from jax.experimental import pallas as pl
from jax.experimental.pallas import tpu as pltpu
from jax.sharding import PartitionSpec as P

HB = 64
LANES = 128
EDGE_BLOCK = 512
MIB = 1024 * 1024
MAIN_LIMIT = 25
FIRST, SECOND = 3, 7
PREP_LIMIT = 20
PART, CORE, DOM_BIT, OWNER, GEOM_BITS = range(5)
F32 = jnp.float32
BF16 = jnp.bfloat16
VMEM = pltpu.VMEM


class Places:
    def __getitem__(self, at):
        part = lax.axis_index("dom")
        geom = lax.axis_index("geom")
        if at == PART:
            return part
        if at == CORE:
            return geom & 1
        if at == DOM_BIT:
            return part & 1
        if at == OWNER:
            return part >> 1
        return (geom >> (at - GEOM_BITS + 1)) & 1


def placed(kernel, *fixed):
    return lambda *refs: kernel(*fixed, Places(), *refs)


def dot_nn(left, right):
    return lax.dot_general(left, right, (((1,), (0,)), ((), ())), preferred_element_type=F32)


def dot_nt(left, right):
    return lax.dot_general(left, right, (((1,), (1,)), ((), ())), preferred_element_type=F32)


def dot_tn(left, right):
    return lax.dot_general(left, right, (((0,), (0,)), ((), ())), preferred_element_type=F32)


def iota(shape, axis):
    return lax.broadcasted_iota(jnp.int32, shape, axis)


def hot(condition):
    return jnp.where(condition, 1.0, 0.0).astype(BF16)


def sigmoid(values):
    return 0.5 * jnp.tanh(0.5 * values) + 0.5


def normalize(values):
    center = values - jnp.mean(values, axis=-1, keepdims=True)
    inverse = lax.rsqrt(jnp.mean(center * center, axis=-1, keepdims=True) + 1e-05)
    return center * inverse, inverse


def normalize_back(normed, inverse, upstream):
    return inverse * (
        upstream
        - jnp.mean(upstream, axis=-1, keepdims=True)
        - normed * jnp.mean(upstream * normed, axis=-1, keepdims=True)
    )


def slots_of(index, me, part_count, cell_count):
    owner = jnp.zeros_like(index)
    for part in range(1, part_count):
        owner = owner + jnp.where(index >= part * cell_count, 1, 0)
    row = index - owner * cell_count
    ahead = owner - me
    ahead = jnp.where(ahead < 0, ahead + part_count, ahead)
    high = -(-part_count // 16) * 16
    member = hot(iota((high, cell_count), 0) == ahead)
    before = hot(iota((cell_count, cell_count), 0) < iota((cell_count, cell_count), 1))
    rank = jnp.sum(member.astype(F32) * dot_nn(member, before), axis=0, keepdims=True)
    return ahead * LANES + rank.astype(jnp.int32), row


def pack_kernel(part_count, capacity, scal, h_hbm, index_hbm, *refs):
    outs = refs[:-3]
    h_ref, index_ref, sems = refs[-3:]
    cell_count, width = h_ref.shape
    loads = [
        pltpu.make_async_copy(index_hbm, index_ref, sems.at[0]),
        pltpu.make_async_copy(h_hbm, h_ref, sems.at[1]),
    ]
    for load in loads:
        load.start()
    loads[0].wait()
    chunks = width // LANES
    slot, row = slots_of(index_ref[...], scal[PART], part_count, cell_count)
    kind = iota((16, cell_count), 0)
    coded = jnp.where(
        kind == 0, row >> 8, jnp.where(kind == 1, row & 255, jnp.where(kind == 2, 1, 0))
    )
    coded = coded.astype(F32).astype(BF16)
    loads[1].wait()
    cells = h_ref[...]
    for step in range(part_count):
        pick = hot(iota((LANES, cell_count), 0) + step * LANES == slot)
        rows = dot_nn(pick, cells).astype(BF16)
        for chunk in range(chunks):
            outs[step][chunk * capacity : (chunk + 1) * capacity, :] = rows[
                :capacity, chunk * LANES : (chunk + 1) * LANES
            ]
        outs[step][chunks * capacity :, :] = dot_nt(coded, pick).astype(BF16)
    outs[part_count][...] = jnp.zeros(outs[part_count].shape, F32)


def place(ids, cell_count):
    ids = ids.astype(F32)
    spot = ids[0:1] * 256.0 + ids[1:2] + (ids[2:3] - 1.0) * 65536.0
    return hot(iota((cell_count, LANES), 0) == spot.astype(jnp.int32))


def unpack_kernel(part_count, capacity, scal, *refs):
    blocks = refs[:part_count]
    _, nodes_ref, low_ref, high_ref, ids_ref, rows_ref, hot_ref = refs[part_count:]
    cell_count, width = nodes_ref.shape
    chunks = width // LANES
    for step in range(part_count):
        base = step * LANES
        ids = blocks[step][chunks * capacity :, :]
        ids_ref[step * 16 : (step + 1) * 16, :] = ids
        hot_ref[:, base : base + LANES] = place(ids, cell_count)
        for chunk in range(chunks):
            rows_ref[base : base + capacity, chunk * LANES : (chunk + 1) * LANES] = blocks[step][
                chunk * capacity : (chunk + 1) * capacity, :
            ]
        if capacity < LANES:
            rows_ref[base + capacity : base + LANES, :] = jnp.zeros(
                (LANES - capacity, width), BF16
            )
    nodes = dot_nn(hot_ref[...], rows_ref[...]).astype(BF16)
    nodes_ref[...] = nodes
    odd = scal[DOM_BIT] == 1
    head = nodes[:HB]
    tail = nodes[cell_count - HB :]
    low_ref[...] = jnp.where(odd, head, tail)
    high_ref[...] = jnp.where(odd, tail, head)


def spread_rows(wide, base, rows, fan_in):
    count, width = rows.shape
    chunks = width // LANES
    for chunk in range(chunks):
        for at in range(fan_in):
            wide[base + chunk, pl.ds(at, count, stride=fan_in), :] = rows[
                :, chunk * LANES : (chunk + 1) * LANES
            ]
    return jnp.concatenate([wide[base + chunk] for chunk in range(chunks)], axis=1)


def collect_rows(wide, base, values, fan_in):
    count = values.shape[0] // fan_in
    sums = []
    for chunk in range(values.shape[1] // LANES):
        wide[base + chunk] = values[:, chunk * LANES : (chunk + 1) * LANES]
        total = wide[base + chunk, pl.ds(0, count, stride=fan_in), :]
        for at in range(1, fan_in):
            total = total + wide[base + chunk, pl.ds(at, count, stride=fan_in), :]
        sums.append(total)
    return jnp.concatenate(sums, axis=1)


def prep_kernel(
    fan_in,
    cell_count,
    scal,
    source_hbm,
    edges_hbm,
    cot_nodes_hbm,
    cot_edges_hbm,
    w_edge_in_hbm,
    w_edge_out_hbm,
    w_node_in_hbm,
    w_node_out_hbm,
    _,
    edges_ref,
    cot_nodes_ref,
    cot_edges_ref,
    w_edge_in_ref,
    w_edge_out_ref,
    w_node_in_ref,
    w_node_out_ref,
    gather_ref,
    scatter_ref,
    pre_ref,
    token_ref,
    source_ref,
    sems,
):
    edge_count, width = edges_ref.shape
    padded = cell_count + 2 * HB
    cells = EDGE_BLOCK // fan_in
    loads = [
        pltpu.make_async_copy(far, near, sems.at[at])
        for at, (far, near) in enumerate(
            (
                (source_hbm, source_ref),
                (edges_hbm, edges_ref),
                (w_edge_in_hbm, w_edge_in_ref),
                (w_edge_out_hbm, w_edge_out_ref),
                (w_node_in_hbm, w_node_in_ref),
                (w_node_out_hbm, w_node_out_ref),
                (cot_nodes_hbm, cot_nodes_ref),
                (cot_edges_hbm, cot_edges_ref),
            )
        )
    ]
    for load in loads:
        load.start()
    token_ref[...] = jnp.zeros(token_ref.shape, F32)
    loads[0].wait()
    offset = scal[PART] * cell_count - HB

    def hots(step, carry):
        rows = pl.ds(pl.multiple_of(step * EDGE_BLOCK, EDGE_BLOCK), EDGE_BLOCK)
        local = source_ref[:, rows] - offset
        scatter_ref[:, rows] = hot(iota((padded, EDGE_BLOCK), 0) == local)
        local = jnp.transpose(jnp.broadcast_to(local.astype(F32), (LANES, EDGE_BLOCK)))
        local = local.astype(jnp.int32)
        lane = iota((EDGE_BLOCK, LANES), 1)
        for at in range(0, padded, LANES):
            gather_ref[rows, at : at + LANES] = hot(local == lane + at)
        gather_ref[rows, padded:] = hot(
            iota((EDGE_BLOCK, cells), 0) // fan_in == iota((EDGE_BLOCK, cells), 1)
        )
        return carry

    lax.fori_loop(0, edge_count // EDGE_BLOCK, hots, 0)
    loads[1].wait()
    loads[2].wait()

    def first(step, carry):
        rows = pl.ds(pl.multiple_of(step * EDGE_BLOCK, EDGE_BLOCK), EDGE_BLOCK)
        pre_ref[rows, :] = dot_nn(edges_ref[rows, :], w_edge_in_ref[:width, :])
        return carry

    lax.fori_loop(0, edge_count // EDGE_BLOCK, first, 0)
    for load in loads[3:]:
        load.wait()


def main_kernel(
    fan_in,
    scale,
    scal,
    nodes_ref,
    low_ref,
    high_ref,
    edges_ref,
    cot_nodes_ref,
    cot_edges_ref,
    w_edge_in_ref,
    w_edge_out_ref,
    w_node_in_ref,
    w_node_out_ref,
    gather_ref,
    scatter_ref,
    pre_ref,
    edge_new_hbm,
    node_new_hbm,
    pre_grad_hbm,
    summed_grad_hbm,
    sent_ref,
    received_ref,
    base_ref,
    keep_ref,
    send_ref,
    pre_grad_ref,
    summed_grad_ref,
    node_new_ref,
    cells_ref,
    table_ref,
    recv_ref,
    hidden_ref,
    slope_ref,
    normed_ref,
    summed_ref,
    post_grad_ref,
    wide_ref,
    out_sems,
):
    cell_count, width = nodes_ref.shape
    edge_count = edges_ref.shape[0]
    steps = edge_count // EDGE_BLOCK
    padded = cell_count + 2 * HB
    cells = EDGE_BLOCK // fan_in
    half = width // 2
    inner = slice(HB, HB + cell_count)

    odd = scal[DOM_BIT] == 1
    low = low_ref[...]
    high = high_ref[...]
    cells_ref[:HB, :] = jnp.where(odd, low, high)
    cells_ref[inner, :] = nodes_ref[...]
    cells_ref[HB + cell_count :, :] = jnp.where(odd, high, low)
    table_ref[:padded, :] = dot_nn(cells_ref[...], w_edge_in_ref[width : 2 * width, :]).astype(BF16)
    recv_ref[...] = dot_nn(nodes_ref[...], w_edge_in_ref[2 * width :, :]).astype(BF16)

    inverses = []
    for step in range(steps):
        spot = slice(step * cells, (step + 1) * cells)
        rows = slice(step * EDGE_BLOCK, (step + 1) * EDGE_BLOCK)
        table_ref[padded : padded + cells, :] = recv_ref[spot, :]
        edges = edges_ref[rows, :]
        pre = pre_ref[rows, :] + dot_nn(gather_ref[rows, :], table_ref[...])
        gate = sigmoid(pre)
        hidden = (pre * gate).astype(BF16)
        hidden_ref[rows, :] = hidden
        slope_ref[rows, :] = (gate * (1.0 + pre * (1.0 - gate))).astype(BF16)
        normed, inverse = normalize(dot_nn(hidden, w_edge_out_ref[...]))
        normed_ref[rows, :] = normed.astype(BF16)
        inverses.append(inverse)
        edge_new = (edges.astype(F32) + normed).astype(BF16)
        post_grad_ref[rows, :] = edge_new
        summed_ref[spot, :] = collect_rows(wide_ref, 0, edge_new.astype(F32), fan_in).astype(BF16)

    edge_store = pltpu.make_async_copy(post_grad_ref, edge_new_hbm, out_sems.at[0])
    edge_store.start()
    nodes = nodes_ref[...]
    summed = summed_ref[...]
    node_pre = dot_nn(nodes, w_node_in_ref[:width, :]) + dot_nn(summed, w_node_in_ref[width:, :])
    node_gate = sigmoid(node_pre)
    node_hidden = (node_pre * node_gate).astype(BF16)
    node_normed, node_inverse = normalize(dot_nn(node_hidden, w_node_out_ref[...]))
    node_new_ref[...] = (nodes.astype(F32) + node_normed).astype(BF16)
    node_store = pltpu.make_async_copy(node_new_ref, node_new_hbm, out_sems.at[1])
    node_store.start()
    upstream = cot_nodes_ref[...].astype(F32)
    node_post_grad = normalize_back(node_normed, node_inverse, upstream).astype(BF16)
    node_slope = node_gate * (1.0 + node_pre * (1.0 - node_gate))
    node_pre_grad = (dot_nt(node_post_grad, w_node_out_ref[...]) * node_slope).astype(BF16)
    summed_grad = dot_nt(node_pre_grad, w_node_in_ref[width:, :])
    summed_grad_ref[...] = summed_grad
    summed_store = pltpu.make_async_copy(summed_grad_ref, summed_grad_hbm, out_sems.at[2])
    summed_store.start()
    base_ref[...] = upstream + dot_nt(node_pre_grad, w_node_in_ref[:width, :])
    edge_store.wait()
    for step in range(steps):
        spot = slice(step * cells, (step + 1) * cells)
        rows = slice(step * EDGE_BLOCK, (step + 1) * EDGE_BLOCK)
        base = (step % 2) * (width // LANES)
        upstream = cot_edges_ref[rows, :].astype(F32) + spread_rows(
            wide_ref, base, summed_grad_ref[spot, :], fan_in
        )
        post_grad = normalize_back(
            normed_ref[rows, :].astype(F32), inverses[step], upstream
        )
        post_grad = post_grad.astype(BF16)
        post_grad_ref[rows, :] = post_grad
        pre_grad = dot_nt(post_grad, w_edge_out_ref[...]) * slope_ref[rows, :].astype(F32)
        pre_grad = pre_grad.astype(BF16)
        pre_grad_ref[rows, :] = pre_grad
        received_ref[spot, :] = collect_rows(
            wide_ref, base, pre_grad.astype(F32), fan_in
        ).astype(BF16)

    pre_store = pltpu.make_async_copy(pre_grad_ref, pre_grad_hbm, out_sems.at[3])
    pre_store.start()
    first = scal[CORE] == 0

    def put(place_at, value):
        value = (value * scale).astype(BF16)
        rows = slice(place_at * width, (place_at + 1) * width)
        left = value[:, :half]
        right = value[:, half:]
        keep_ref[rows, :] = jnp.where(first, left, right)
        send_ref[rows, :] = jnp.where(first, right, left)

    sent = dot_nn(scatter_ref[...], pre_grad_ref[...]).astype(BF16)
    sent_ref[...] = sent
    put(0, dot_tn(edges_ref[...], pre_grad_ref[...]))
    put(1, dot_tn(cells_ref[...], sent))
    put(2, dot_tn(nodes, received_ref[...]))
    put(3, dot_tn(hidden_ref[...], post_grad_ref[...]))
    put(4, dot_tn(nodes, node_pre_grad))
    put(5, dot_tn(summed, node_pre_grad))
    put(6, dot_tn(node_hidden, node_post_grad))
    node_store.wait()
    summed_store.wait()
    pre_store.wait()


def cell_kernel(
    scal,
    sent_ref,
    received_ref,
    base_ref,
    w_edge_in_ref,
    low_ref,
    high_ref,
    node_grad_ref,
    rim_ref,
):
    cell_count, width = received_ref.shape
    sender = dot_nt(sent_ref[...], w_edge_in_ref[width : 2 * width, :])
    odd = scal[DOM_BIT] == 1
    to_prev = sender[:HB].astype(BF16)
    to_next = sender[HB + cell_count :].astype(BF16)
    low_ref[...] = jnp.where(odd, to_prev, to_next)
    high_ref[...] = jnp.where(odd, to_next, to_prev)
    node_grad = (
        base_ref[...]
        + dot_nt(received_ref[...], w_edge_in_ref[2 * width :, :])
        + sender[HB : HB + cell_count]
    )
    node_grad_ref[...] = node_grad.astype(BF16)
    rim_ref[:HB, :] = node_grad[:HB]
    rim_ref[HB:, :] = node_grad[cell_count - HB :]


def edge_kernel(
    fan_in,
    cot_hbm,
    summed_grad_hbm,
    pre_grad_hbm,
    w_edge_in_hbm,
    _,
    grad_edge_hbm,
    token_ref,
    cot_ref,
    summed_grad_ref,
    pre_grad_ref,
    w_edge_ref,
    grad_edge_ref,
    wide_ref,
    in_sems,
    out_sems,
):
    edge_count, width = cot_ref.shape
    steps = edge_count // EDGE_BLOCK
    cells = EDGE_BLOCK // fan_in
    loads = [
        pltpu.make_async_copy(w_edge_in_hbm.at[:width, :], w_edge_ref, in_sems.at[0]),
        pltpu.make_async_copy(summed_grad_hbm, summed_grad_ref, in_sems.at[1]),
    ]
    for step in range(steps):
        rows = slice(step * EDGE_BLOCK, (step + 1) * EDGE_BLOCK)
        for at, (far, near) in enumerate(((cot_hbm, cot_ref), (pre_grad_hbm, pre_grad_ref))):
            loads.append(
                pltpu.make_async_copy(
                    far.at[rows, :], near.at[rows, :], in_sems.at[2 + 2 * step + at]
                )
            )
    for load in loads:
        load.start()
    token_ref[...] = jnp.zeros(token_ref.shape, F32)
    loads[0].wait()
    loads[1].wait()
    stores = []
    for step in range(steps):
        rows = slice(step * EDGE_BLOCK, (step + 1) * EDGE_BLOCK)
        loads[2 + 2 * step].wait()
        loads[3 + 2 * step].wait()
        upstream = cot_ref[rows, :].astype(F32) + spread_rows(
            wide_ref, 0, summed_grad_ref[step * cells : (step + 1) * cells, :], fan_in
        )
        grad_edge_ref[rows, :] = (
            upstream + dot_nt(pre_grad_ref[rows, :], w_edge_ref[...])
        ).astype(BF16)
        stores.append(
            pltpu.make_async_copy(
                grad_edge_ref.at[rows, :], grad_edge_hbm.at[rows, :], out_sems.at[step]
            )
        )
        stores[-1].start()
    for store in stores:
        store.wait()


def return_kernel(
    part_count,
    capacity,
    scal,
    node_grad_ref,
    rim_ref,
    low_ref,
    high_ref,
    ids_ref,
    *outs,
):
    cell_count, width = node_grad_ref.shape
    chunks = width // LANES
    outs[part_count][...] = jnp.zeros(outs[part_count].shape, F32)
    odd = scal[DOM_BIT] == 1
    low = low_ref[...].astype(F32)
    high = high_ref[...].astype(F32)
    first = rim_ref[:HB, :] + jnp.where(odd, low, high)
    last = rim_ref[HB:, :] + jnp.where(odd, high, low)
    grad = jnp.concatenate(
        [first.astype(BF16), node_grad_ref[HB : cell_count - HB, :], last.astype(BF16)], axis=0
    )
    for step in range(part_count):
        pick = place(ids_ref[step * 16 : (step + 1) * 16, :], cell_count)
        rows = dot_tn(pick, grad).astype(BF16)
        for chunk in range(chunks):
            outs[step][chunk * capacity : (chunk + 1) * capacity, :] = rows[
                :capacity, chunk * LANES : (chunk + 1) * LANES
            ]


def finish_kernel(part_count, capacity, scal, index_ref, *refs):
    blocks = refs[:part_count]
    out_ref, token_ref, rows_ref, pick_ref = refs[part_count:]
    cell_count, width = out_ref.shape
    chunks = width // LANES
    token_ref[...] = jnp.zeros(token_ref.shape, F32)
    slot, _ = slots_of(index_ref[...], scal[PART], part_count, cell_count)
    for step in range(part_count):
        base = step * LANES
        pick_ref[base : base + LANES, :] = hot(iota((LANES, cell_count), 0) + base == slot)
        for chunk in range(chunks):
            rows_ref[base : base + capacity, chunk * LANES : (chunk + 1) * LANES] = blocks[step][
                chunk * capacity : (chunk + 1) * capacity, :
            ]
        if capacity < LANES:
            rows_ref[base + capacity : base + LANES, :] = jnp.zeros(
                (LANES - capacity, width), BF16
            )
    out_ref[...] = dot_tn(pick_ref[...], rows_ref[...]).astype(BF16)


def shape(dims, kind=BF16):
    return jax.ShapeDtypeStruct(dims, kind)


def whole(count):
    return [pl.BlockSpec(memory_space=VMEM)] * count


def params(limit):
    return pltpu.CompilerParams(vmem_limit_bytes=limit * MIB)


def cost(flops, bytes_accessed):
    return pl.CostEstimate(flops=flops, bytes_accessed=bytes_accessed, transcendentals=0)


def full(dims):
    return pl.BlockSpec(dims, lambda step: (0,) * len(dims))


def rows_spec(rows, columns):
    return pl.BlockSpec((rows, columns), lambda step: (step, 0))


def swap(value, axis, bit):
    count = lax.axis_size(axis)
    return lax.ppermute(value, axis, [(at, at ^ bit) for at in range(count)])


def take(value, kind, bit):
    if kind == "columns":
        half = value.shape[2] // 2
        parts = value[:, :, :half], value[:, :, half:]
    else:
        pairs = value.reshape((value.shape[0] // 2, 2) + value.shape[1:])
        parts = pairs[:, 0], pairs[:, 1]
    return jnp.where(bit == 0, parts[0], parts[1])


def core_kernel(kinds, bits, scal, keep_ref, got_ref, _, *refs):
    total_ref, left_ref, right_ref, token_ref = refs
    token_ref[...] = jnp.zeros(token_ref.shape, F32)
    total = (keep_ref[...].astype(F32) + got_ref[...].astype(F32)).astype(BF16)
    total = total.reshape(total_ref.shape)
    total_ref[...] = total
    half = total.shape[1] // 2
    left_ref[...] = take(total[:, :half], kinds[0], 1 - scal[bits[0]])
    right_ref[...] = take(total[:, half:], kinds[1], 1 - scal[bits[1]])


def stage_kernel(part, kinds, bits, scal, value_ref, got_ref, *refs):
    total_ref, send_ref = refs[-2:]
    value = value_ref[...]
    if part is not None:
        half = value.shape[1] // 2
        value = value[:, part * half : (part + 1) * half]
    mine = take(value, kinds[0], scal[bits[0]]).astype(F32)
    total = (mine + got_ref[...].astype(F32)).astype(BF16)
    total_ref[...] = total
    send_ref[...] = take(total, kinds[1], 1 - scal[bits[1]])


def split_kernel(kinds, bits, scal, *refs):
    left_ref, left_got_ref, right_ref, right_got_ref = refs[:4]
    outs = refs[-(left_got_ref.shape[0]) :]
    left = take(left_ref[...], kinds[0], scal[bits[0]]).astype(F32)
    left = (left + left_got_ref[...].astype(F32)).astype(BF16)
    right = take(right_ref[...], kinds[1], scal[bits[1]]).astype(F32)
    right = (right + right_got_ref[...].astype(F32)).astype(BF16)
    half = left.shape[1]
    owner = scal[OWNER]
    for other, out in enumerate(outs):
        for at in range(len(outs)):

            @pl.when((owner ^ other) == at)
            def _(out=out, at=at):
                out[:half, :] = left[at]
                out[half:, :] = right[at]


def sum_kernel(*refs):
    total = refs[0][...].astype(F32)
    for ref in refs[1:-2]:
        total = total + ref[...].astype(F32)
    refs[-1][...] = total.astype(BF16)


def join_kernel(at, scal, mine_ref, theirs_ref, out_ref):
    mine = mine_ref[...]
    theirs = theirs_ref[...]
    columns = mine.shape[1]
    first = scal[at] == 0
    out_ref[:, :columns] = jnp.where(first, mine, theirs).astype(out_ref.dtype)
    out_ref[:, columns:] = jnp.where(first, theirs, mine).astype(out_ref.dtype)


def local_call(kernel, outs, name, *operands):
    return pl.pallas_call(
        kernel,
        out_shape=[near_shape(*out) for out in outs],
        in_specs=whole(len(operands)),
        out_specs=whole(len(outs)),
        compiler_params=params(24),
        name=name,
    )(*operands)


def halved(dims, kind):
    if kind == "columns":
        return (dims[0], dims[1], dims[2] // 2)
    return (dims[0] // 2,) + dims[1:]


def chains(geom_count):
    columns = []
    bit = 2
    while bit < geom_count:
        columns.append(("columns", "geom", bit, GEOM_BITS + len(columns)))
        bit *= 2
    owner = ("owners", "dom", 1, DOM_BIT)
    return columns + [owner], [owner] + columns


def begin_weights(keep, got, geom_count, part_count, *tokens):
    left, right = chains(geom_count)
    rows, width = keep.shape
    dims = (part_count, rows // part_count, width)
    piece = (part_count, rows // part_count // 2, width)
    return local_call(
        placed(core_kernel, (left[0][0], right[0][0]), (left[0][3], right[0][3])),
        [
            (dims,),
            (halved(piece, left[0][0]),),
            (halved(piece, right[0][0]),),
            ((8, LANES), F32),
        ],
        "core",
        keep,
        got,
        *tokens,
    )


def pair_weights(total, send_left, send_right, geom_count, part_count, early):
    rows = total.shape[1]
    ends = []
    for part, chain, send in zip((0, 1), chains(geom_count), (send_left, send_right)):
        value = total
        now = (part_count, rows // 2, total.shape[2])
        for at in range(len(chain) - 1):
            kind, axis, bit, place_at = chain[at]
            follow = chain[at + 1]
            now = halved(now, kind)
            value, send = local_call(
                placed(
                    stage_kernel,
                    part if at == 0 else None,
                    (kind, follow[0]),
                    (place_at, follow[3]),
                ),
                [(now,), (halved(now, follow[0]),)],
                "stage",
                value,
                swap(send, axis, bit),
                *early[part],
            )
        if len(chain) == 1:
            half = rows // 2
            value = value[:, part * half : (part + 1) * half]
        ends.append((value, swap(send, chain[-1][1], chain[-1][2])))
        end = halved(now, chain[-1][0])
    return ends, end


def reduce_weights(ends, end, geom_count, part_count, early, late):
    left, right = chains(geom_count)
    out = (2 * end[1], end[2])
    owners = part_count // 2
    pieces = local_call(
        placed(split_kernel, (left[-1][0], right[-1][0]), (left[-1][3], right[-1][3])),
        [(out,)] * owners,
        "split",
        *ends[0],
        *ends[1],
        early,
    )
    got = [swap(pieces[other], "dom", 2 * other) for other in range(owners - 1, 0, -1)]
    total = pl.pallas_call(
        sum_kernel,
        out_shape=near_shape(out),
        in_specs=whole(owners + 1),
        out_specs=pl.BlockSpec(memory_space=VMEM),
        compiler_params=params(24),
        name="sum",
    )(pieces[0], *got, late)
    for place_at, bit in [(link[3], link[2]) for link in left[-2::-1]] + [(CORE, 1)]:
        out = (out[0], 2 * out[1])
        last = bit == 1
        total = pl.pallas_call(
            placed(join_kernel, place_at),
            out_shape=shape(out, F32) if last else near_shape(out),
            in_specs=whole(2),
            out_specs=pl.BlockSpec(memory_space=VMEM),
            compiler_params=params(24),
            name="join",
        )(total, swap(total, "geom", bit))
    return total


def shift(value, steps):
    count = lax.axis_size("dom")
    return lax.ppermute(value, "dom", [(at, (at + steps) % count) for at in range(count)])


def neighbour(value, first):
    count = lax.axis_size("dom")
    pairs = [(at, at + 1) for at in range(first, count - 1, 2)]
    return lax.ppermute(value, "dom", pairs + [(right, left) for left, right in pairs])


def send_order(part_count):
    return sorted(range(1, part_count), key=lambda at: (-min(at, part_count - at), at))


def pinned(value):
    return pltpu.with_memory_space_constraint(value, pltpu.HBM)


def near_shape(dims, kind=BF16):
    return pltpu.VMEM(dims, kind)


def run_prep(
    fan_in,
    cell_count,
    source,
    edges,
    cot_nodes,
    cot_edges,
    w_edge_in,
    w_edge_out,
    w_node_in,
    w_node_out,
    token,
):
    edge_count = edges.shape[0]
    padded = cell_count + 2 * HB
    cells = EDGE_BLOCK // fan_in
    near = pl.BlockSpec(memory_space=VMEM)
    return pl.pallas_call(
        placed(prep_kernel, fan_in, cell_count),
        out_shape=[
            near_shape(like.shape)
            for like in (edges, cot_nodes, cot_edges, w_edge_in, w_edge_out, w_node_in, w_node_out)
        ]
        + [
            near_shape((edge_count, padded + cells)),
            near_shape((padded, edge_count)),
            near_shape(edges.shape, F32),
            near_shape((8, LANES), F32),
        ],
        in_specs=[pl.BlockSpec(memory_space=pltpu.HBM)] * 8 + [near],
        out_specs=[near] * 11,
        scratch_shapes=[VMEM(source.shape, jnp.int32), pltpu.SemaphoreType.DMA((8,))],
        compiler_params=params(PREP_LIMIT),
        cost_estimate=cost(4 * edge_count * edges.shape[1] ** 2, 20 * MIB),
        name="prep",
    )(
        *[
            pinned(value)
            for value in (
                source,
                edges,
                cot_nodes,
                cot_edges,
                w_edge_in,
                w_edge_out,
                w_node_in,
                w_node_out,
            )
        ],
        token,
    )


def run_main(fan_in, scale, nodes, low, high, prepared):
    edge_count, width = prepared[0].shape
    cell_count = nodes.shape[0]
    cells = EDGE_BLOCK // fan_in
    padded = cell_count + 2 * HB
    far = pl.BlockSpec(memory_space=pltpu.HBM)
    near = pl.BlockSpec(memory_space=VMEM)
    by_edge = (edge_count, width)
    by_cell = (cell_count, width)
    weights = (7 * width, width // 2)
    return pl.pallas_call(
        placed(main_kernel, fan_in, scale),
        out_shape=[
            shape(by_edge),
            shape(by_cell),
            pltpu.HBM(by_edge, BF16),
            pltpu.HBM(by_cell, F32),
            near_shape((padded, width)),
            near_shape(by_cell),
            near_shape(by_cell, F32),
            near_shape(weights),
            near_shape(weights),
        ],
        in_specs=[near] * 13,
        out_specs=[far] * 4 + [near] * 5,
        scratch_shapes=[
            VMEM(by_edge, BF16),
            VMEM(by_cell, F32),
            VMEM(by_cell, BF16),
            VMEM((padded, width), BF16),
            VMEM((padded + cells, width), BF16),
            VMEM(by_cell, BF16),
            VMEM(by_edge, BF16),
            VMEM(by_edge, BF16),
            VMEM(by_edge, BF16),
            VMEM(by_cell, BF16),
            VMEM(by_edge, BF16),
            VMEM((2 * width // LANES, EDGE_BLOCK, LANES), F32),
            pltpu.SemaphoreType.DMA((4,)),
        ],
        compiler_params=params(MAIN_LIMIT),
        cost_estimate=cost(28 * edge_count * width * width, 16 * MIB),
        name="main",
    )(nodes, low, high, *prepared)


def run_edges(fan_in, cot, summed_grad, pre_grad, w_edge_in, *tokens):
    edge_count, width = cot.shape
    steps = edge_count // EDGE_BLOCK
    far = pl.BlockSpec(memory_space=pltpu.HBM)
    return pl.pallas_call(
        functools.partial(edge_kernel, fan_in),
        out_shape=[shape((edge_count, width)), near_shape((8, LANES), F32)],
        in_specs=[far] * 4 + whole(len(tokens)),
        out_specs=[far, pl.BlockSpec(memory_space=VMEM)],
        scratch_shapes=[
            VMEM((edge_count, width), BF16),
            VMEM(summed_grad.shape, F32),
            VMEM((edge_count, width), BF16),
            VMEM((width, width), BF16),
            VMEM((edge_count, width), BF16),
            VMEM((width // LANES, EDGE_BLOCK, LANES), F32),
            pltpu.SemaphoreType.DMA((2 + 2 * steps,)),
            pltpu.SemaphoreType.DMA((steps,)),
        ],
        compiler_params=params(24),
        cost_estimate=cost(1, 1),
        name="edges",
    )(*[pinned(value) for value in (cot, summed_grad, pre_grad, w_edge_in)], *tokens)


def local(
    h_in,
    edge_in,
    new_index,
    source,
    w_edge_in,
    w_edge_out,
    w_node_in,
    w_node_out,
    cot_nodes,
    cot_edges,
):
    _, cell_count, width = h_in.shape
    edge_count = source.shape[1]
    fan_in = edge_count // cell_count
    part_count = lax.axis_size("dom")
    geom_count = lax.axis_size("geom")
    capacity = cell_count // part_count + cell_count // part_count // 2
    chunks = width // LANES
    block_rows = chunks * capacity
    scale = 1.0 / math.sqrt(geom_count * part_count * cell_count * fan_in)
    edges = edge_in[0]
    cot = cot_edges[0]

    sends = pl.pallas_call(
        placed(pack_kernel, part_count, capacity),
        out_shape=[shape((block_rows + 16, LANES))] * part_count + [near_shape((8, LANES), F32)],
        in_specs=[pl.BlockSpec(memory_space=pltpu.HBM)] * 2,
        out_specs=whole(part_count + 1),
        scratch_shapes=[
            VMEM((cell_count, width), BF16),
            VMEM((1, cell_count), jnp.int32),
            pltpu.SemaphoreType.DMA((2,)),
        ],
        compiler_params=params(24),
        name="pack",
    )(pinned(h_in[0]), pinned(new_index))
    prepared = run_prep(
        fan_in,
        cell_count,
        source,
        edges,
        cot_nodes[0],
        cot,
        w_edge_in,
        w_edge_out,
        w_node_in,
        w_node_out,
        sends[part_count],
    )
    got = {0: sends[0]}
    for step in send_order(part_count):
        got[step] = shift(sends[step], step)
    nodes, low, high, ids = pl.pallas_call(
        placed(unpack_kernel, part_count, capacity),
        out_shape=[
            shape((cell_count, width)),
            shape((HB, width)),
            shape((HB, width)),
            shape((part_count * 16, LANES)),
        ],
        in_specs=whole(part_count + 1),
        out_specs=whole(4),
        scratch_shapes=[
            VMEM((part_count * LANES, width), BF16),
            VMEM((cell_count, part_count * LANES), BF16),
        ],
        compiler_params=params(24),
        name="unpack",
    )(*[got[step] for step in range(part_count)], prepared[-1])
    low = neighbour(low, 0)
    high = neighbour(high, 1)

    (
        edge_new,
        node_new,
        pre_grad,
        summed_grad,
        sent,
        received,
        base,
        keep,
        send,
    ) = run_main(fan_in, scale, nodes, low, high, prepared[:-1])
    low, high, node_grad, rim = pl.pallas_call(
        placed(cell_kernel),
        out_shape=[
            near_shape((HB, width)),
            near_shape((HB, width)),
            near_shape((cell_count, width)),
            near_shape((2 * HB, width), F32),
        ],
        in_specs=whole(4),
        out_specs=whole(4),
        compiler_params=params(24),
        cost_estimate=cost(3 * cell_count * width * width, 3 * MIB),
        name="cells",
    )(sent, received, base, prepared[3])
    low = neighbour(low, 0)
    high = neighbour(high, 1)
    *returning, token = pl.pallas_call(
        placed(return_kernel, part_count, capacity),
        out_shape=[near_shape((block_rows, LANES))] * part_count + [near_shape((8, LANES), F32)],
        in_specs=whole(5),
        out_specs=whole(part_count + 1),
        compiler_params=params(24),
        cost_estimate=cost(1, 1),
        name="returning",
    )(node_grad, rim, low, high, ids)
    *begun, token = begin_weights(
        keep, swap(send, "geom", 1), geom_count, part_count, token
    )

    grad_edge, edge_token = run_edges(
        fan_in, cot, summed_grad, pre_grad, w_edge_in, token
    )
    back = {0: returning[0]}
    for step in send_order(part_count):
        back[step] = shift(returning[step], -step)
    early = [back[step] for step in send_order(part_count)]
    ends, end = pair_weights(
        *begun, geom_count, part_count, (early[:FIRST], early[:SECOND])
    )
    grad_in, late = pl.pallas_call(
        placed(finish_kernel, part_count, capacity),
        out_shape=[shape((cell_count, width)), near_shape((8, LANES), F32)],
        in_specs=whole(1 + part_count),
        out_specs=whole(2),
        scratch_shapes=[
            VMEM((part_count * LANES, width), BF16),
            VMEM((part_count * LANES, cell_count), BF16),
        ],
        compiler_params=params(24),
        name="finish",
    )(new_index, *[back[step] for step in range(part_count)])
    weight_grads = reduce_weights(ends, end, geom_count, part_count, edge_token, late)
    return (node_new[None], edge_new[None], grad_in[None], grad_edge[None], weight_grads)


def solution(mesh):
    return jax.shard_map(
        local,
        mesh=mesh,
        in_specs=(
            P("geom", "dom", None),
            P("geom", "dom", None),
            P("geom", "dom"),
            P("geom", "dom"),
            P(),
            P(),
            P(),
            P(),
            P("geom", "dom", None),
            P("geom", "dom", None),
        ),
        out_specs=(
            P("geom", "dom", None),
            P("geom", "dom", None),
            P("geom", "dom", None),
            P("geom", "dom", None),
            P("dom", None),
        ),
        check_vma=False,
    )
```
